32 devices in a mesh: wide: 16 (over z, y, core), narrow: 2 (over x).
Axes of the slice: x: 2, y: 2, z: 4, core: 2. Of those that a mesh axis runs over, the one named last changes fastest.
Arguments:
- inputs: bfloat16 [64, 256, 1152], P(('wide', 'narrow')), may hold values from -6 to 6
- cotangent: bfloat16 [64, 256, 1152], P(('wide', 'narrow')), may hold values from -6 to 6
- class_ids: int32 [64], P(('wide', 'narrow')), may hold values from 0 to 999
- step_ids: int32 [64], P(('wide', 'narrow')), may hold values from 0 to 999
- image_counts: int32 [32], P(('wide', 'narrow')), may hold values from 0 to 2, as said below
- w_qkv: bfloat16 [1152, 3456], P('wide', 'narrow'), may hold values from -0.1875 to 0.1875
- w_out: bfloat16 [1152, 1152], P('wide', 'narrow'), may hold values from -0.75 to 0.75
- w_gate: bfloat16 [1152, 3072], P('wide', 'narrow'), may hold values from -0.1875 to 0.1875
- w_up: bfloat16 [1152, 3072], P('wide', 'narrow'), may hold values from -0.1875 to 0.1875
- w_down: bfloat16 [3072, 1152], P('wide', 'narrow'), may hold values from -0.109375 to 0.109375
- ada_weight: bfloat16 [1152, 6912], P('wide', 'narrow'), may hold values from -0.1875 to 0.1875
- ada_bias: bfloat16 [6912], P(('wide', 'narrow')), may hold values from -3 to 3
- class_table: bfloat16 [1000, 1152], P('narrow', 'wide'), may hold values from -6 to 6
- norm_gains: float32 [2, 72], replicated, may hold values from 0.6 to 1.8
Outputs:
- block_output: bfloat16 [64, 256, 1152], P(('wide', 'narrow'))
- input_grad: bfloat16 [64, 256, 1152], P(('wide', 'narrow'))
- grad_qkv: float32 [1152, 3456], P('wide', 'narrow')
- grad_out: float32 [1152, 1152], P('wide', 'narrow')
- grad_gate: float32 [1152, 3072], P('wide', 'narrow')
- grad_up: float32 [1152, 3072], P('wide', 'narrow')
- grad_down: float32 [3072, 1152], P('wide', 'narrow')
- grad_ada_weight: float32 [1152, 6912], P('wide', 'narrow')
- grad_ada_bias: float32 [6912], P(('wide', 'narrow'))
- grad_table: float32 [1000, 1152], P('narrow', 'wide')
- grad_gains: float32 [2, 72], replicated
The draws below stay inside these ranges and needn't reach their ends.
Inputs may be any that keep to these rules, and one draw needn't show every extreme that they name: image_counts[d] real images fill the first slots of device d, numbered wide index times the size of narrow plus narrow index; its other slots hold padding images. Some device has all 2 slots real and some has none.
All inputs are finite; a program needn't handle non-finite values.
Results may differ from the reference program's by a relative error of at most 0.018.
Values may be sent and summed in bfloat16 or wider, within the bound.
No kernel may reach another device: no remote copies, remote signals or barrier semaphores. Data moves between devices by JAX's collectives and lax.ppermute only.
A program may use at most 256 MiB of HBM per device.

```python
import math
import jax
import jax.numpy as jnp
from jax import lax

D = 1152
H = 16
HD = 72
FF = 3072
CLASSES = 1000
GRID = 16
MB = 2
IMG_MB = 1
S = 256
IMAGES = 64
DEVICES = 32


def draw_image_counts(key, part):
    key = jax.random.fold_in(key, 7)
    subkeys = jax.random.split(key, 3)
    capacity = MB * IMG_MB
    samples = jax.random.randint(subkeys[0], (3, DEVICES), 0, capacity + 1)
    low_two = jnp.minimum(samples[0], samples[1])
    high_two = jnp.maximum(samples[0], samples[1])
    low_three = jnp.minimum(low_two, samples[2])
    high_three = jnp.maximum(high_two, samples[2])
    device_index = jnp.arange(DEVICES, dtype=jnp.int32)
    quarter = device_index * 4 // DEVICES
    counts = jnp.where(quarter == 0, low_three, jnp.where(quarter == 1, low_two, jnp.where(quarter == 2, high_two, high_three)))
    span = max(DEVICES // 4, 1)
    full_at = DEVICES - 1 - jax.random.randint(subkeys[1], (), 0, span)
    empty_at = jax.random.randint(subkeys[2], (), 0, span)
    counts = jnp.where(device_index == full_at, capacity, counts)
    counts = jnp.where(device_index == empty_at, 0, counts)
    return counts.astype(jnp.int32)


def with_ends(values, rng, smallest, high):
    spot = [jax.random.randint(jax.random.fold_in(rng, axis), (), 0, length) for axis, length in enumerate(values.shape)]
    longest = values.shape.index(max(values.shape))
    next_to = spot[:longest] + [(spot[longest] + 1) % values.shape[longest]] + spot[longest + 1:]
    return values.at[tuple(spot)].set(smallest).at[tuple(next_to)].set(high)


def shard_levels(stream_key, dims, shards, least, largest):
    def one(axis_at, shards_of):
        heights = jax.random.uniform(jax.random.fold_in(jax.random.fold_in(stream_key, 6), axis_at), (shards_of,), jnp.float32, least / len(shards), largest / len(shards))
        return jnp.repeat(jnp.exp(heights), dims[axis_at] // shards_of).reshape((-1,) + (1,) * (len(dims) - axis_at - 1))

    level = one(*shards[0])
    for cut in shards[1:]:
        level = level * one(*cut)
    return level


def gaussian(stream_key, dims, scale, bound, cuts=(), kind=jnp.bfloat16):
    loudness = shard_levels(stream_key, dims, cuts, -0.22, 0.18) if cuts else 1.0
    values = jax.random.normal(stream_key, dims, jnp.float32) * scale * loudness
    return jnp.minimum(jnp.maximum(values, -bound), bound).astype(kind)


def setup_inputs(seed: int = 0) -> dict:
    key_of = jax.random.split(jax.random.key(seed), 15)
    inputs = gaussian(key_of[0], (IMAGES, S, D), 1.0, 6.0, ((0, 32),))
    cotangent = gaussian(key_of[1], (IMAGES, S, D), 1.0, 6.0, ((0, 32),))
    class_ids = with_ends(jax.random.randint(key_of[2], (IMAGES,), 0, CLASSES), jax.random.fold_in(key_of[2], 1), 0, CLASSES - 1).astype(jnp.int32)
    step_ids = with_ends(jax.random.randint(key_of[3], (IMAGES,), 0, 1000), jax.random.fold_in(key_of[3], 1), 0, 999).astype(jnp.int32)
    image_counts = draw_image_counts(jax.random.fold_in(key_of[14], 71), 0)
    w_qkv = gaussian(key_of[5], (D, 3 * D), D ** -0.5, 0.1875, ((0, 16), (1, 2)))
    w_out = gaussian(key_of[6], (D, D), (D // 16) ** -0.5, 0.75, ((0, 16), (1, 2)))
    w_gate = gaussian(key_of[7], (D, FF), D ** -0.5, 0.1875, ((0, 16), (1, 2)))
    w_up = gaussian(key_of[8], (D, FF), D ** -0.5, 0.1875, ((0, 16), (1, 2)))
    w_down = gaussian(key_of[9], (FF, D), FF ** -0.5, 0.109375, ((0, 16), (1, 2)))
    ada_weight = gaussian(key_of[10], (D, 6 * D), D ** -0.5, 0.1875, ((0, 16), (1, 2)))
    ada_bias = gaussian(key_of[11], (6 * D,), 0.5, 3.0, ((0, 32),))
    class_table = gaussian(key_of[12], (CLASSES, D), 1.0, 6.0, ((0, 2), (1, 16)))
    norm_gains = jnp.clip(jax.random.uniform(key_of[13], (2, HD), jnp.float32, 0.6, 1.8), 0.6, 1.8)
    return dict(inputs=inputs, cotangent=cotangent, class_ids=class_ids, step_ids=step_ids, image_counts=image_counts, w_qkv=w_qkv, w_out=w_out, w_gate=w_gate, w_up=w_up, w_down=w_down, ada_weight=ada_weight, ada_bias=ada_bias, class_table=class_table, norm_gains=norm_gains)


@jax.custom_vjp
def low(v):
    return lax.optimization_barrier(v.astype(jnp.bfloat16)).astype(jnp.float32)

@jax.custom_vjp
def low_back(v):
    return v

def low_keep(v):
    return (low(v), None)

def low_pass(kept, grad):
    return (grad,)

def back_keep(v):
    return (v, None)

def back_low(kept, grad):
    return (low(grad),)
low.defvjp(low_keep, low_pass)
low_back.defvjp(back_keep, back_low)
EPSILON = 1e-06
HIGHEST = lax.Precision.HIGHEST

def sinusoid(steps, width):
    half_width = width // 2
    frequency = jnp.exp(-math.log(10000.0) * jnp.arange(half_width, dtype=jnp.float32) / half_width)
    angles = steps.astype(jnp.float32)[:, None] * frequency[None, :]
    return jnp.concatenate([jnp.cos(angles), jnp.sin(angles)], axis=-1)

def rope_tables(length, grid_side, head):
    quarter = head // 4
    frequency = 10000.0 ** (-jnp.arange(quarter, dtype=jnp.float32) / quarter)
    patch_index = jnp.arange(length, dtype=jnp.int32)
    row_place = (patch_index // grid_side).astype(jnp.float32)
    col_place = (patch_index % grid_side).astype(jnp.float32)
    row_angle = row_place[:, None] * frequency[None, :]
    col_angle = col_place[:, None] * frequency[None, :]
    angles = jnp.concatenate([row_angle, row_angle, col_angle, col_angle], axis=-1)
    return (jnp.cos(angles)[:, None, :], jnp.sin(angles)[:, None, :])

def rotate_half(vector):
    quarter = vector.shape[-1] // 4
    part_one = vector[..., :quarter]
    part_two = vector[..., quarter:2 * quarter]
    part_three = vector[..., 2 * quarter:3 * quarter]
    part_four = vector[..., 3 * quarter:]
    return jnp.concatenate([-part_two, part_one, -part_four, part_three], axis=-1)

def rotary(vector, cosine_table, sine_table):
    return vector * cosine_table + rotate_half(vector) * sine_table

def layer_norm(values):
    centre = values - lax.optimization_barrier(jnp.mean(values, axis=-1, keepdims=True))
    return centre * lax.rsqrt(lax.optimization_barrier(jnp.mean(centre * centre, axis=-1, keepdims=True)) + EPSILON)

def rms_norm(values):
    return values * lax.rsqrt(lax.optimization_barrier(jnp.mean(values * values, axis=-1, keepdims=True)) + EPSILON)

def block_forward(parameters, tokens, class_ids, step_ids, cosine_table, sine_table):
    w_qkv, w_out, w_gate, w_up, w_down, ada_weight, ada_bias, class_table, norm_gains = parameters
    images, length, width = tokens.shape
    condition = jnp.take(class_table, class_ids, axis=0) + sinusoid(step_ids, width)
    cond_act = low(jax.nn.silu(condition))
    modulation = low_back(jnp.dot(cond_act, ada_weight, precision=HIGHEST) + ada_bias)
    pieces = jnp.split(modulation[:, None, :], 6, axis=-1)
    normed = layer_norm(tokens)
    attn_in = low(normed * (1.0 + pieces[1]) + pieces[0])
    packed = low_back(jnp.einsum('bsd,de->bse', attn_in, w_qkv, precision=HIGHEST))
    packed = packed.reshape(images, length, 3, H, HD)
    queries = low(rotary(rms_norm(packed[:, :, 0]) * norm_gains[0], cosine_table, sine_table))
    key_rows = low(rotary(rms_norm(packed[:, :, 1]) * norm_gains[1], cosine_table, sine_table))
    value_rows = low(packed[:, :, 2])
    scores = low_back(jnp.einsum('bshe,bthe->bhst', queries, key_rows, precision=HIGHEST))
    scores = scores * HD ** (-0.5)
    row_max = lax.optimization_barrier(jnp.max(scores, axis=-1, keepdims=True))
    exponent = jnp.exp(scores - row_max)
    attention = low(exponent / lax.optimization_barrier(jnp.sum(exponent, axis=-1, keepdims=True)))
    mixed = jnp.einsum('bhst,bthe->bshe', attention, value_rows, precision=HIGHEST)
    mixed = low(low_back(mixed.reshape(images, length, width)))
    attn_out = low_back(jnp.einsum('bsd,de->bse', mixed, w_out, precision=HIGHEST))
    hidden_one = tokens + pieces[2] * attn_out
    normed_two = layer_norm(hidden_one)
    mlp_in = low(normed_two * (1.0 + pieces[4]) + pieces[3])
    gate_val = low_back(jnp.einsum('bsd,df->bsf', mlp_in, w_gate, precision=HIGHEST))
    up_val = low_back(jnp.einsum('bsd,df->bsf', mlp_in, w_up, precision=HIGHEST))
    hidden_mid = low(jax.nn.silu(gate_val) * up_val)
    mlp_out = low_back(jnp.einsum('bsf,fd->bsd', hidden_mid, w_down, precision=HIGHEST))
    return hidden_one + pieces[5] * mlp_out

def reference(inputs, cotangent, class_ids, step_ids, image_counts, w_qkv, w_out, w_gate, w_up, w_down, ada_weight, ada_bias, class_table, norm_gains):
    slot_count = MB * IMG_MB
    image_index = jnp.arange(IMAGES, dtype=jnp.int32)
    owner_device = (image_index // slot_count).astype(jnp.int32)
    real_mask = (image_index % slot_count < jnp.take(image_counts, owner_device)).astype(jnp.float32)
    real_count = jnp.sum(real_mask)
    parameters = (w_qkv.astype(jnp.float32), w_out.astype(jnp.float32), w_gate.astype(jnp.float32), w_up.astype(jnp.float32), w_down.astype(jnp.float32), ada_weight.astype(jnp.float32), ada_bias.astype(jnp.float32), class_table.astype(jnp.float32), norm_gains.astype(jnp.float32))
    group_size = math.gcd(IMAGES, 16)
    block_count = IMAGES // group_size
    length = inputs.shape[1]
    cosine_table, sine_table = rope_tables(length, GRID, HD)

    def forward(params_in, tokens):
        stacked = tokens.reshape(block_count, group_size, length, D)

        def one_block(packed_in):
            return block_forward(params_in, packed_in[0], packed_in[1], packed_in[2], cosine_table, sine_table)
        result = lax.map(jax.checkpoint(one_block), (stacked, class_ids.reshape(block_count, group_size), step_ids.reshape(block_count, group_size)))
        return result.reshape(IMAGES, length, D)
    output, pullback = jax.vjp(forward, parameters, inputs.astype(jnp.float32))
    grad_params, grad_inputs = pullback(cotangent.astype(jnp.float32) * real_mask[:, None, None])
    return (output.astype(jnp.bfloat16), grad_inputs.astype(jnp.bfloat16), grad_params[0] / real_count, grad_params[1] / real_count, grad_params[2] / real_count, grad_params[3] / real_count, grad_params[4] / real_count, grad_params[5] / real_count, grad_params[6] / real_count, grad_params[7] / real_count, grad_params[8] / real_count)
```

```python
import math

import jax
import jax.numpy as jnp
from jax import lax
from jax.experimental import pallas as pl
from jax.experimental.pallas import tpu as pltpu
from jax.sharding import PartitionSpec as P

H = 16
HD = 72
CLASSES = 1000
GRID = 16

EPSILON = 1e-06
HIGHEST = lax.Precision.HIGHEST
ALL = ("wide", "narrow")
BF = jnp.bfloat16
F32 = jnp.float32


def rope_tables(length, grid_side, head):
    quarter = head // 4
    frequency = 10000.0 ** (-jnp.arange(quarter, dtype=jnp.float32) / quarter)
    patch_index = jnp.arange(length, dtype=jnp.int32)
    row_place = (patch_index // grid_side).astype(jnp.float32)
    col_place = (patch_index % grid_side).astype(jnp.float32)
    row_angle = row_place[:, None] * frequency[None, :]
    col_angle = col_place[:, None] * frequency[None, :]
    angles = jnp.concatenate([row_angle, row_angle, col_angle, col_angle], axis=-1)
    return (jnp.cos(angles)[:, None, :], jnp.sin(angles)[:, None, :])


def rotate_half(vector):
    quarter = vector.shape[-1] // 4
    part_one = vector[..., :quarter]
    part_two = vector[..., quarter : 2 * quarter]
    part_three = vector[..., 2 * quarter : 3 * quarter]
    part_four = vector[..., 3 * quarter :]
    return jnp.concatenate([-part_two, part_one, -part_four, part_three], axis=-1)


def rotary(vector, cosine_table, sine_table):
    return vector * cosine_table + rotate_half(vector) * sine_table


def rotary_back(gradient, cosine_table, sine_table):
    return gradient * cosine_table - rotate_half(gradient * sine_table)


def layer_norm(values):
    centre = values - jnp.mean(values, axis=-1, keepdims=True)
    inverse = lax.rsqrt(jnp.mean(centre * centre, axis=-1, keepdims=True) + EPSILON)
    return (centre * inverse, inverse)


def layer_norm_back(gradient, normed, inverse):
    return inverse * (
        gradient
        - jnp.mean(gradient, axis=-1, keepdims=True)
        - normed * jnp.mean(gradient * normed, axis=-1, keepdims=True)
    )


def rms_norm(values):
    inverse = lax.rsqrt(jnp.mean(values * values, axis=-1, keepdims=True) + EPSILON)
    return (values * inverse, inverse)


def rms_back(gradient, normed, inverse):
    return inverse * (gradient - normed * jnp.mean(gradient * normed, axis=-1, keepdims=True))


class Places:
    def __init__(self):
        self.wide, self.narrow = lax.axis_size("wide"), lax.axis_size("narrow")
        self.z = self.wide // 4
        w = lax.axis_index("wide")
        self.w, self.x = w, lax.axis_index("narrow")
        self.at_z, self.at_y, self.at_c = w // 4, (w // 2) % 2, w % 2
        self.z_bits = [1 << i for i in range(self.z.bit_length() - 1)]
        self.x_bits = [1 << i for i in range(self.narrow.bit_length() - 1)]
        x_masks = [(0, bit) for bit in self.x_bits]
        self.orders = ([(1, 0)] + x_masks, x_masks + [(1, 0)])

    def swap(self, value, flip):
        pairs = []
        for w in range(self.wide):
            for x in range(self.narrow):
                dz, dy, dc, dx = flip(w % 2)
                to = (w // 4 ^ dz) * 4 + (w // 2 % 2 ^ dy) * 2 + (w % 2 ^ dc)
                pairs.append((w * self.narrow + x, to * self.narrow + (x ^ dx)))
        return lax.ppermute(value, ALL, pairs)

    def step_flip(self, i):
        return lambda core: (0, self.orders[core][i][0], 0, self.orders[core][i][1])

    def masks(self, core):
        out = [(0, 0)]
        for dy, dx in self.orders[core]:
            out = out + [(y ^ dy, x ^ dx) for y, x in out]
        return out

    def all_bits(self):
        out = [(0, (bit, 0, 0, 0), self.at_z // bit % 2) for bit in self.z_bits]
        out.append((1, (0, 1, 0, 0), self.at_y))
        out += [(3, (0, 0, 0, bit), self.x // bit % 2) for bit in self.x_bits]
        out.append((2, (0, 0, 1, 0), self.at_c))
        return out

    def gather_small(self, value):
        value = value[None, None, None, None]
        for axis, flip, bit in self.all_bits():
            other = self.swap(value, lambda core: flip)
            low = jnp.where(bit == 0, value, other)
            high = jnp.where(bit == 0, other, value)
            value = jnp.concatenate([low, high], axis)
        return value.reshape(self.wide * self.narrow, *value.shape[4:])

    def add_all(self, value):
        for _, flip, _ in self.all_bits():
            value = value + self.swap(value, lambda core: flip)
        return value

    def add_narrow(self, value):
        for bit in self.x_bits:
            value = value + self.swap(value, lambda core: (0, 0, 0, bit))
        return value

    def scatter_wide(self, value):
        value = value.reshape(self.z, 2, 2, *value.shape[1:])
        other = self.swap(take(value, 2, 1 - self.at_c), lambda core: (0, 0, 1, 0))
        value = take(value, 2, self.at_c) + other
        other = self.swap(take(value, 1, 1 - self.at_y), lambda core: (0, 1, 0, 0))
        value = take(value, 1, self.at_y) + other
        for bit in reversed(self.z_bits):
            value = value.reshape(2, bit, *value.shape[1:])
            here = self.at_z // bit % 2
            other = self.swap(take(value, 0, 1 - here), lambda core: (bit, 0, 0, 0))
            value = take(value, 0, here) + other
        return value[0]


def pick(parts, index):
    if len(parts) == 1:
        return parts[0]
    if len(parts) == 2:
        return jnp.where(index == 0, parts[0], parts[1])
    return lax.dynamic_index_in_dim(jnp.stack(parts), index, 0, keepdims=False)


def take(value, axis, index):
    return lax.dynamic_index_in_dim(value, index, axis, keepdims=False)


def after(value, *before):
    return lax.optimization_barrier((value,) + before)[0]


def assemble(places, parts):
    half, z, rows, columns = parts[0].shape
    masks = [places.masks(0), places.masks(1)]

    def kernel(at, s0, s1, t0, t1, out, held, sem, out_sem):
        core, y, x, here_z = at[0], at[1], at[2], at[3]
        copies = []
        for i, src in enumerate((s0, s1, t0, t1)):
            owner = core ^ (i // 2)
            for j in range(half):
                k = j + half * (i % 2)
                dy = jnp.where(owner == 0, masks[0][k][0], masks[1][k][0])
                dx = jnp.where(owner == 0, masks[0][k][1], masks[1][k][1])
                for d in range(z):
                    to = held.at[x ^ dx, here_z ^ d, y ^ dy, owner]
                    copies.append(pltpu.make_async_copy(src.at[j, d], to, sem.at[len(copies)]))
        for copy in copies:
            copy.start()
        for copy in copies:
            copy.wait()
        whole = pltpu.make_async_copy(held, out, out_sem)
        whole.start()
        whole.wait()

    shape = (places.narrow, z, 2, 2, rows, columns)
    at = jnp.stack([places.at_c, places.at_y, places.x, places.at_z]).astype(jnp.int32)
    size = 2 * math.prod(shape)
    return pl.pallas_call(
        kernel,
        out_shape=jax.ShapeDtypeStruct(shape, BF),
        in_specs=[pl.BlockSpec(memory_space=pltpu.SMEM)] + [pl.BlockSpec(memory_space=pl.ANY)] * 4,
        out_specs=pl.BlockSpec(memory_space=pl.ANY),
        scratch_shapes=[
            pltpu.VMEM(shape, BF),
            pltpu.SemaphoreType.DMA((4 * half * z,)),
            pltpu.SemaphoreType.DMA,
        ],
        compiler_params=pltpu.CompilerParams(vmem_limit_bytes=24 * 2**20),
        cost_estimate=pl.CostEstimate(flops=0, bytes_accessed=2 * size, transcendentals=0),
        name="assemble",
    )(at, *parts)


def gather_weights(places, shards):
    outs, last = [], {}

    def swap(kind, value, flip):
        if kind in last:
            value = after(value, last[kind])
        last[kind] = places.swap(value, flip)
        return last[kind]

    steps = len(places.orders[0])
    for shard in shards:
        held = shard[None]
        for bit in places.z_bits:
            held = jnp.concatenate([held, swap("z", held, lambda core: (bit, 0, 0, 0))], 0)
        held = held[None]
        for i in range(steps):
            other = swap(i, held, places.step_flip(i))
            if i < steps - 1:
                held = jnp.concatenate([held, other], 0)
        parts = [held, other]
        parts += [places.swap(part, lambda core: (0, 0, 1, 0)) for part in parts]
        whole = assemble(places, parts)
        outs.append(list(whole.reshape(places.narrow, places.wide * shard.shape[0], shard.shape[1])))
    return outs


def scatter(places, blocks):
    z = places.z
    blocks = [b.reshape(z, 2, 2, -1, b.shape[-1]) for b in blocks]
    masks = [places.masks(0), places.masks(1)]

    def stack(owner, first, count):
        out = []
        for j in range(first, first + count):
            dy = jnp.where(owner == 0, masks[0][j][0], masks[1][j][0])
            dx = jnp.where(owner == 0, masks[0][j][1], masks[1][j][1])
            rows = [
                take(take(b, 2, owner), 1, places.at_y ^ dy) for b in blocks
            ]
            out.append(pick(rows, places.x ^ dx))
        return jnp.stack(out)

    total = len(masks[0])
    arrived = places.swap(stack(1 - places.at_c, 0, total), lambda core: (0, 0, 1, 0))
    half = total // 2
    send = (stack(places.at_c, half, half).astype(F32) + arrived[half:].astype(F32)).astype(BF)
    other = places.swap(send, places.step_flip(len(places.orders[0]) - 1))
    held = stack(places.at_c, 0, half).astype(F32) + arrived[:half].astype(F32) + other.astype(F32)
    for i in reversed(range(len(places.orders[0]) - 1)):
        half //= 2
        other = places.swap(held[half:].astype(BF), places.step_flip(i))
        held = held[:half] + other.astype(F32)
    held = held[0]
    held = jnp.stack([take(held, 0, places.at_z ^ d) for d in range(z)])
    for bit in reversed(places.z_bits):
        other = places.swap(held[bit:].astype(BF), lambda core: (bit, 0, 0, 0))
        held = held[:bit] + other.astype(F32)
    return held[0]


def dot(a, b, dims, out=F32):
    return lax.dot_general(a, b, (dims, ((), ())), preferred_element_type=F32).astype(out)


def times(a, blocks):
    return jnp.concatenate([dot(a, b, ((1,), (0,))) for b in blocks], axis=1)


def times_t(a, blocks):
    width = blocks[0].shape[1]
    total = None
    for n, b in enumerate(blocks):
        term = dot(a[:, n * width : (n + 1) * width], b, ((1,), (1,)))
        total = term if total is None else total + term
    return total


def grad_blocks(a, d, narrow):
    width = d.shape[1] // narrow
    return [dot(a, d[:, n * width : (n + 1) * width], ((0,), (0,)), BF) for n in range(narrow)]


def on_device(
    inputs,
    cotangent,
    class_ids,
    step_ids,
    image_counts,
    w_qkv,
    w_out,
    w_gate,
    w_up,
    w_down,
    ada_weight,
    ada_bias,
    class_table,
    norm_gains,
):
    places = Places()
    wide, narrow, at_w, at_n = places.wide, places.narrow, places.w, places.x
    images, length, width = inputs.shape
    cosine_table, sine_table = rope_tables(length, GRID, HD)
    local_count = image_counts[0]
    score_scale = HD ** (-0.5)

    small = [class_ids, step_ids, image_counts, ada_bias]
    small = places.gather_small(jnp.concatenate([v.astype(F32) for v in small])[None])[:, 0]
    ids = small[:, : 2 * images].reshape(-1, 2, images).transpose(0, 2, 1).reshape(-1, 2)
    ids = ids.astype(jnp.int32)
    real_count = jnp.sum(small[:, 2 * images])
    bias = small[:, 2 * images + 1 :].reshape(-1)
    rows_here, cols_here = class_table.shape
    class_hot = ids[:, :1] - at_n * rows_here == jnp.arange(rows_here, dtype=jnp.int32)[None, :]
    picked = dot(class_hot.astype(BF), class_table, ((1,), (0,)))
    column = at_w * cols_here + jnp.arange(cols_here, dtype=jnp.int32)
    half_width = width // 2
    frequency = jnp.exp(-math.log(10000.0) * (column % half_width).astype(F32) / half_width)
    angles = ids[:, 1:].astype(F32) * frequency[None, :]
    wave = jnp.where(column[None, :] < half_width, jnp.cos(angles), jnp.sin(angles))
    condition = places.add_narrow(picked) + wave
    cond_act = jax.nn.silu(condition).astype(BF)
    mod_part = dot(cond_act, ada_weight, ((1,), (0,)))
    mod_part = places.scatter_wide(mod_part.reshape(wide, narrow, images, -1))
    modulation = lax.all_to_all(mod_part, "narrow", 0, 0, tiled=True)
    modulation = modulation.transpose(1, 0, 2).reshape(images, -1) + bias
    pieces = jnp.split(modulation[:, None, :], 6, axis=-1)

    qkv_b, out_b, gate_b, up_b, down_b = gather_weights(
        places, [w_qkv, w_out, w_gate, w_up, w_down]
    )
    tokens = images * length

    def flat(v):
        return v.reshape(tokens, -1)

    def deep(v):
        return v.reshape(images, length, -1)

    source = inputs.astype(F32)
    normed, inverse = layer_norm(source)
    attn_in = flat((normed * (1.0 + pieces[1]) + pieces[0]).astype(BF))
    packed = times(attn_in, qkv_b).reshape(images, length, 3, H, HD)
    query_normed, query_inverse = rms_norm(packed[:, :, 0])
    key_normed, key_inverse = rms_norm(packed[:, :, 1])
    queries = rotary(query_normed * norm_gains[0], cosine_table, sine_table).astype(BF)
    key_rows = rotary(key_normed * norm_gains[1], cosine_table, sine_table).astype(BF)
    value_rows = packed[:, :, 2].astype(BF)
    scores = (
        jnp.einsum("bshe,bthe->bhst", queries, key_rows, preferred_element_type=F32) * score_scale
    )
    row_max = jnp.max(scores, axis=-1, keepdims=True)
    exponent = jnp.exp(scores - row_max)
    softmax_out = exponent / jnp.sum(exponent, axis=-1, keepdims=True)
    attention = softmax_out.astype(BF)
    mixed = jnp.einsum("bhst,bthe->bshe", attention, value_rows, preferred_element_type=F32)
    mixed = mixed.reshape(tokens, width).astype(BF)
    attn_out = deep(times(mixed, out_b))
    hidden_one = source + pieces[2] * attn_out
    normed_two, inverse_two = layer_norm(hidden_one)
    mlp_in = flat((normed_two * (1.0 + pieces[4]) + pieces[3]).astype(BF))
    gate_val = times(mlp_in, gate_b)
    up_val = times(mlp_in, up_b)
    gate_sigmoid = jax.nn.sigmoid(gate_val)
    hidden_mid = (gate_val * gate_sigmoid * up_val).astype(BF)
    mlp_out = deep(times(hidden_mid, down_b))
    block_output = (hidden_one + pieces[5] * mlp_out).astype(BF)

    slot_real = (jnp.arange(images, dtype=jnp.int32) < local_count).astype(F32)
    grad_y = cotangent.astype(F32) * slot_real[:, None, None]
    d_gate_b = jnp.sum(grad_y * mlp_out, axis=1)
    d_mlp = flat((pieces[5] * grad_y).astype(BF))

    r_down = scatter(places, grad_blocks(hidden_mid, d_mlp, narrow))
    d_mid = times_t(d_mlp, down_b)
    d_gate = (d_mid * up_val * gate_sigmoid * (1.0 + gate_val * (1.0 - gate_sigmoid))).astype(BF)
    d_up = (d_mid * gate_val * gate_sigmoid).astype(BF)
    r_up = scatter(places, grad_blocks(mlp_in, d_up, narrow))
    r_gate = scatter(places, grad_blocks(mlp_in, d_gate, narrow))
    d_mlp_in = deep(times_t(d_gate, gate_b) + times_t(d_up, up_b))
    d_scale_b = jnp.sum(d_mlp_in * normed_two, axis=1)
    d_shift_b = jnp.sum(d_mlp_in, axis=1)
    d_hidden = grad_y + layer_norm_back(d_mlp_in * (1.0 + pieces[4]), normed_two, inverse_two)
    d_gate_a = jnp.sum(d_hidden * attn_out, axis=1)
    d_attn = flat((pieces[2] * d_hidden).astype(BF))
    r_out = scatter(places, grad_blocks(mixed, d_attn, narrow))
    d_mixed = times_t(d_attn, out_b).astype(BF).reshape(images, length, H, HD)
    d_values = jnp.einsum("bhst,bshe->bthe", attention, d_mixed, preferred_element_type=F32)
    d_soft = jnp.einsum("bshe,bthe->bhst", d_mixed, value_rows, preferred_element_type=F32)
    row_inner = jnp.sum(softmax_out * d_soft, axis=-1, keepdims=True)
    d_scores = (softmax_out * (d_soft - row_inner) * score_scale).astype(BF)
    d_queries = jnp.einsum("bhst,bthe->bshe", d_scores, key_rows, preferred_element_type=F32)
    d_keys = jnp.einsum("bhst,bshe->bthe", d_scores, queries, preferred_element_type=F32)
    query_scaled = rotary_back(d_queries, cosine_table, sine_table)
    key_scaled = rotary_back(d_keys, cosine_table, sine_table)
    grad_gains = jnp.stack(
        [
            jnp.sum(query_scaled * query_normed, axis=(0, 1, 2)),
            jnp.sum(key_scaled * key_normed, axis=(0, 1, 2)),
        ],
        axis=0,
    )
    d_query_raw = rms_back(query_scaled * norm_gains[0], query_normed, query_inverse)
    d_key_raw = rms_back(key_scaled * norm_gains[1], key_normed, key_inverse)
    d_packed = jnp.stack([d_query_raw, d_key_raw, d_values], axis=2)
    d_packed = d_packed.reshape(tokens, 3 * width).astype(BF)
    r_qkv = scatter(places, grad_blocks(attn_in, d_packed, narrow))
    d_attn_in = deep(times_t(d_packed, qkv_b))
    d_scale_a = jnp.sum(d_attn_in * normed, axis=1)
    d_shift_a = jnp.sum(d_attn_in, axis=1)
    d_tokens = d_hidden + layer_norm_back(d_attn_in * (1.0 + pieces[1]), normed, inverse)
    d_modulation = jnp.concatenate(
        [d_shift_a, d_scale_a, d_gate_a, d_shift_b, d_scale_b, d_gate_b], axis=-1
    ).astype(BF)

    d_mod = places.gather_small(d_modulation).reshape(-1, d_modulation.shape[1])
    ada_cols = ada_weight.shape[1]
    d_mod_here = lax.dynamic_slice_in_dim(d_mod, at_n * ada_cols, ada_cols, 1)
    g_ada = dot(cond_act, d_mod_here, ((0,), (0,)))
    bias_cols = ada_bias.shape[0]
    bias_at = (at_w * narrow + at_n) * bias_cols
    g_bias = jnp.sum(lax.dynamic_slice_in_dim(d_mod, bias_at, bias_cols, 1).astype(F32), axis=0)
    d_cond_act = places.add_narrow(dot(d_mod_here, ada_weight, ((1,), (1,))))
    cond_sigmoid = jax.nn.sigmoid(condition)
    d_condition = d_cond_act * cond_sigmoid * (1.0 + condition * (1.0 - cond_sigmoid))
    g_table = jnp.dot(class_hot.astype(F32).T, d_condition, precision=HIGHEST)
    gain_sum = places.add_all(grad_gains)
    return (
        block_output,
        d_tokens.astype(BF),
        r_qkv / real_count,
        r_out / real_count,
        r_gate / real_count,
        r_up / real_count,
        r_down / real_count,
        g_ada / real_count,
        g_bias / real_count,
        g_table / real_count,
        gain_sum / real_count,
    )


def solution(mesh):
    split = P("wide", "narrow")
    images = P(ALL, None, None)
    return jax.shard_map(
        on_device,
        mesh=mesh,
        in_specs=(
            images,
            images,
            P(ALL),
            P(ALL),
            P(ALL),
            split,
            split,
            split,
            split,
            split,
            split,
            P(ALL),
            P("narrow", "wide"),
            P(),
        ),
        out_specs=(
            images,
            images,
            split,
            split,
            split,
            split,
            split,
            split,
            P(ALL),
            P("narrow", "wide"),
            P(),
        ),
        check_vma=False,
    )
```

```python
import math

import jax
import jax.numpy as jnp
from jax import lax
from jax.experimental import pallas as pl
from jax.experimental.pallas import tpu as pltpu
from jax.sharding import PartitionSpec as P

H = 16
HD = 72
CLASSES = 1000
GRID = 16

EPSILON = 1e-06
HIGHEST = lax.Precision.HIGHEST
ALL = ("wide", "narrow")
BF = jnp.bfloat16
F32 = jnp.float32
SHORT = pl.CostEstimate(flops=10**6, bytes_accessed=10**6, transcendentals=0)


def layer_norm(values):
    centre = values - jnp.mean(values, axis=-1, keepdims=True)
    inverse = lax.rsqrt(jnp.mean(centre * centre, axis=-1, keepdims=True) + EPSILON)
    return (centre * inverse, inverse)


def head_tables(length):
    quarter = HD // 4
    frequency = 10000.0 ** (-jnp.arange(quarter, dtype=F32) / quarter)
    patch = jnp.arange(length, dtype=jnp.int32)
    row_angle = (patch // GRID).astype(F32)[:, None] * frequency[None, :]
    col_angle = (patch % GRID).astype(F32)[:, None] * frequency[None, :]
    angles = jnp.concatenate([row_angle, row_angle, col_angle, col_angle], axis=-1)
    cosine, sine = jnp.cos(angles), jnp.sin(angles)
    first = (jnp.arange(HD) // quarter) % 2 == 0
    above = jnp.where(first[None, :], -sine, 0.0)
    below = jnp.where(first[None, :], 0.0, sine)
    return [jnp.tile(t, (1, H)) for t in (cosine, above, below)]


def head_sums():
    lane = lax.broadcasted_iota(jnp.int32, (H * HD, 128), 0) // HD
    return (lane == lax.broadcasted_iota(jnp.int32, (H * HD, 128), 1)).astype(BF)


def exact_dot(a, b, dims):
    total = None
    for _ in range(3):
        term = a.astype(BF)
        a = a - term.astype(F32)
        part = lax.dot_general(term, b, (dims, ((), ())), preferred_element_type=F32)
        total = part if total is None else total + part
    return total


def head_mean(values, sums):
    mean = exact_dot(values, sums, ((1,), (0,))) * (1.0 / HD)
    return exact_dot(mean, sums, ((1,), (1,)))


def shifted(values, cosine, above, below, sign):
    quarter, width = HD // 4, values.shape[1]
    up = pltpu.roll(values, width - quarter, 1)
    down = pltpu.roll(values, quarter, 1)
    return values * cosine + sign * (up * above + down * below)


def window(head):
    first, last = head * HD // 128 * 128, ((head + 1) * HD + 127) // 128 * 128
    return first, last


def only(values, head):
    first, last = window(head)
    part = values[:, first:last]
    lane = first + lax.broadcasted_iota(jnp.int32, (1, last - first), 1)
    mine = ((lane >= head * HD) & (lane < (head + 1) * HD)).astype(values.dtype)
    return part * mine


class Tiles:
    def __init__(self, store):
        self.store, self.held = store, {}

    def add(self, head, value):
        first, last = window(head)
        for tile in range(first // 128, last // 128):
            part = value[:, tile * 128 - first : tile * 128 - first + 128]
            self.held[tile] = self.held[tile] + part if tile in self.held else part
        done = (head + 1) * HD // 128
        for tile in sorted(self.held):
            if tile < done or head == H - 1:
                self.store(tile * 128, self.held.pop(tile))


def mm(a, b, dims):
    return lax.dot_general(a, b, (dims, ((), ())), preferred_element_type=F32)


def softmax_of(queries, keys, head):
    first, last = window(head)
    scores = mm(queries[:, first:last], only(keys, head), ((1,), (1,))) * (HD ** (-0.5))
    exponent = jnp.exp(scores - jnp.max(scores, axis=1, keepdims=True))
    return exponent / jnp.sum(exponent, axis=1, keepdims=True)


def attention_forward(packed, gains, tables, sums, images):
    tokens = packed[0].shape[0]
    length, width, blocks = tokens // images, H * HD, len(packed)

    def kernel(*refs):
        parts, refs = refs[:blocks], refs[blocks:]
        gain, cosine, above, below, sums_ref, q_ref, k_ref, v_ref, mixed_ref = refs
        whole = jnp.concatenate([p[...] for p in parts], axis=1)
        sums_here = sums_ref[...]
        for i, ref in enumerate((q_ref, k_ref)):
            raw = whole[:, i * width : (i + 1) * width]
            normed = raw * lax.rsqrt(head_mean(raw * raw, sums_here) + EPSILON)
            turned = shifted(normed * gain[i : i + 1, :], cosine[...], above[...], below[...], 1.0)
            ref[...] = turned.astype(BF)
        v_ref[...] = whole[:, 2 * width :].astype(BF)

        def store(first, value):
            mixed_ref[:, first : first + 128] = value.astype(BF)

        mixed = Tiles(store)
        for head in range(H):
            attention = softmax_of(q_ref, k_ref, head).astype(BF)
            mixed.add(head, mm(attention, only(v_ref, head), ((1,), (0,))))

    def rows(n):
        return pl.BlockSpec((length, n), lambda i: (i, 0))

    def all_of(a):
        return pl.BlockSpec(a.shape, lambda i: (0, 0))

    out = jax.ShapeDtypeStruct((tokens, width), BF)
    return pl.pallas_call(
        kernel,
        grid=(images,),
        out_shape=[out] * 4,
        in_specs=[rows(p.shape[1]) for p in packed] + [all_of(a) for a in (gains, *tables, sums)],
        out_specs=[rows(width)] * 4,
        compiler_params=pltpu.CompilerParams(vmem_limit_bytes=48 * 2**20),
        cost_estimate=SHORT,
        name="attention_forward",
    )(*packed, gains, *tables, sums)


def attention_backward(packed, queries, keys, values, d_mixed, gains, tables, sums, images):
    tokens = queries.shape[0]
    length, width, blocks = tokens // images, H * HD, len(packed)
    block = packed[0].shape[1]

    def kernel(*refs):
        parts, refs = refs[:blocks], refs[blocks:]
        q_ref, k_ref, v_ref, d_ref, gain, cosine, above, below, sums_ref = refs[:9]
        outs, (gain_ref, d_q, d_k, d_v) = refs[9 : 9 + blocks], refs[9 + blocks :]

        def store_to(ref):
            def store(first, value):
                ref[:, first : first + 128] = value

            return store

        all_q, all_k, all_v = [Tiles(store_to(ref)) for ref in (d_q, d_k, d_v)]
        for head in range(H):
            first, last = window(head)
            soft = softmax_of(q_ref, k_ref, head)
            d_here = only(d_ref, head)
            all_v.add(head, mm(soft.astype(BF), d_here, ((0,), (0,))))
            d_soft = mm(d_here, v_ref[:, first:last], ((1,), (1,)))
            inner = jnp.sum(soft * d_soft, axis=1, keepdims=True)
            d_scores = (soft * (d_soft - inner) * (HD ** (-0.5))).astype(BF)
            all_q.add(head, mm(d_scores, only(k_ref, head), ((1,), (0,))))
            all_k.add(head, mm(d_scores, only(q_ref, head), ((0,), (0,))))
        whole = jnp.concatenate([p[...] for p in parts], axis=1)
        sums_here = sums_ref[...]
        done = []
        for i, ref in enumerate((d_q, d_k)):
            raw = whole[:, i * width : (i + 1) * width]
            inverse = lax.rsqrt(head_mean(raw * raw, sums_here) + EPSILON)
            normed = raw * inverse
            scaled = shifted(ref[...], cosine[...], above[...], below[...], -1.0)
            gain_ref[0, i : i + 1, :] = jnp.sum(scaled * normed, axis=0, keepdims=True)
            incoming = scaled * gain[i : i + 1, :]
            mean = head_mean(incoming * normed, sums_here)
            done.append((inverse * (incoming - normed * mean)).astype(BF))
        done.append(d_v[...].astype(BF))
        done = jnp.concatenate(done, axis=1)
        for j, out in enumerate(outs):
            out[...] = done[:, j * block : (j + 1) * block]

    def rows(n):
        return pl.BlockSpec((length, n), lambda i: (i, 0))

    def all_of(a):
        return pl.BlockSpec(a.shape, lambda i: (0, 0))

    outs = pl.pallas_call(
        kernel,
        grid=(images,),
        out_shape=[jax.ShapeDtypeStruct((tokens, block), BF)] * blocks
        + [jax.ShapeDtypeStruct((images, 2, width), F32)],
        in_specs=[rows(block)] * blocks
        + [rows(width)] * 4
        + [all_of(a) for a in (gains, *tables, sums)],
        out_specs=[rows(block)] * blocks + [pl.BlockSpec((1, 2, width), lambda i: (i, 0, 0))],
        scratch_shapes=[pltpu.VMEM((length, width), F32)] * 3,
        compiler_params=pltpu.CompilerParams(vmem_limit_bytes=56 * 2**20),
        cost_estimate=SHORT,
        name="attention_backward",
    )(*packed, queries, keys, values, d_mixed, gains, *tables, sums)
    return outs[:blocks], outs[blocks]

def whole_block(a):
    return pl.BlockSpec(a.shape, lambda *i: (0,) * a.ndim)


def chunk_of(columns, most):
    count = -(-columns // most)
    return columns if count == 1 else -(-columns // (128 * count)) * 128


def project(a, blocks):
    tokens, depth = a.shape
    columns = blocks[0].shape[1]
    count, chunk = len(blocks), chunk_of(columns, 640)

    def kernel(a_ref, *refs):
        for w_ref, out_ref in zip(refs[:count], refs[count:]):
            out_ref[...] = mm(a_ref[...], w_ref[...], ((1,), (0,)))

    return pl.pallas_call(
        kernel,
        grid=(-(-columns // chunk),),
        out_shape=[jax.ShapeDtypeStruct((tokens, columns), F32)] * count,
        in_specs=[whole_block(a)] + [pl.BlockSpec((depth, chunk), lambda i: (0, i))] * count,
        out_specs=[pl.BlockSpec((tokens, chunk), lambda i: (0, i))] * count,
        compiler_params=pltpu.CompilerParams(vmem_limit_bytes=40 * 2**20),
        cost_estimate=SHORT,
        name="project",
    )(a, *blocks)


def gated(a, w_gate, w_up):
    tokens, depth = a.shape
    columns = w_gate.shape[1]
    chunk = 512

    def kernel(a_ref, g_ref, u_ref, gate_ref, up_ref, mid_ref):
        gate = mm(a_ref[...], g_ref[...], ((1,), (0,)))
        up = mm(a_ref[...], u_ref[...], ((1,), (0,)))
        gate_ref[...] = gate
        up_ref[...] = up
        mid_ref[...] = (gate * jax.nn.sigmoid(gate) * up).astype(BF)

    weight = pl.BlockSpec((depth, chunk), lambda i: (0, i))
    out = pl.BlockSpec((tokens, chunk), lambda i: (0, i))
    return pl.pallas_call(
        kernel,
        grid=(columns // chunk,),
        out_shape=[jax.ShapeDtypeStruct((tokens, columns), t) for t in (F32, F32, BF)],
        in_specs=[whole_block(a), weight, weight],
        out_specs=[out] * 3,
        compiler_params=pltpu.CompilerParams(vmem_limit_bytes=40 * 2**20),
        cost_estimate=SHORT,
        name="gated",
    )(a, w_gate, w_up)


def gated_back(d_parts, down, gate_val, up_val, w_gate, w_up):
    tokens, columns = gate_val.shape
    depth, count, chunk = w_gate.shape[0], len(down), 512

    def kernel(*refs):
        d_refs, w_refs, refs = refs[:count], refs[count : 2 * count], refs[2 * count :]
        gate_ref, up_ref, g_ref, u_ref, d_gate_ref, d_up_ref, in_ref = refs
        d_mid = None
        for d_ref, w_ref in zip(d_refs, w_refs):
            term = mm(d_ref[...], w_ref[...], ((1,), (1,)))
            d_mid = term if d_mid is None else d_mid + term
        gate, up = gate_ref[...], up_ref[...]
        sigmoid = jax.nn.sigmoid(gate)
        silu = gate * sigmoid
        d_gate = (d_mid * up * (sigmoid + silu * (1.0 - sigmoid))).astype(BF)
        d_up = (d_mid * silu).astype(BF)
        d_gate_ref[...] = d_gate
        d_up_ref[...] = d_up
        term = mm(d_gate, g_ref[...], ((1,), (1,))) + mm(d_up, u_ref[...], ((1,), (1,)))

        @pl.when(pl.program_id(0) == 0)
        def _():
            in_ref[...] = term

        @pl.when(pl.program_id(0) > 0)
        def _():
            in_ref[...] += term

    width = down[0].shape[1]
    token = pl.BlockSpec((tokens, chunk), lambda i: (0, i))
    weight = pl.BlockSpec((depth, chunk), lambda i: (0, i))
    return pl.pallas_call(
        kernel,
        grid=(columns // chunk,),
        out_shape=[jax.ShapeDtypeStruct((tokens, columns), BF)] * 2
        + [jax.ShapeDtypeStruct((tokens, depth), F32)],
        in_specs=[whole_block(d) for d in d_parts]
        + [pl.BlockSpec((chunk, width), lambda i: (i, 0))] * count
        + [token, token, weight, weight],
        out_specs=[token, token, pl.BlockSpec((tokens, depth), lambda i: (0, 0))],
        compiler_params=pltpu.CompilerParams(vmem_limit_bytes=48 * 2**20),
        cost_estimate=SHORT,
        name="gated_back",
    )(*d_parts, *down, gate_val, up_val, w_gate, w_up)


def normal(values):
    centre = values - jnp.mean(values, axis=1, keepdims=True)
    inverse = lax.rsqrt(jnp.mean(centre * centre, axis=1, keepdims=True) + EPSILON)
    return centre * inverse, inverse


def normal_back(gradient, normed, inverse):
    mean = jnp.mean(gradient, axis=1, keepdims=True)
    return inverse * (
        gradient - mean - normed * jnp.mean(gradient * normed, axis=1, keepdims=True)
    )


def per_image(kernel, images, by_image, whole, outs, vmem, name, scalar=None):
    def spec(rows, rest):
        return pl.BlockSpec((rows, *rest), lambda i: (i,) + (0,) * len(rest))

    in_specs = [spec(a.shape[0] // images, a.shape[1:]) for a in by_image]
    in_specs += [whole_block(a) for a in whole]
    args = [*by_image, *whole]
    if scalar is not None:
        in_specs.append(pl.BlockSpec(memory_space=pltpu.SMEM))
        args.append(scalar)
    return pl.pallas_call(
        kernel,
        grid=(images,),
        out_shape=[jax.ShapeDtypeStruct((images * rows, *rest), t) for rows, rest, t in outs],
        in_specs=in_specs,
        out_specs=[spec(rows, rest) for rows, rest, _ in outs],
        compiler_params=pltpu.CompilerParams(vmem_limit_bytes=vmem * 2**20),
        cost_estimate=SHORT,
        name=name,
    )(*args)


def attention_tail(mixed, out_b, inputs, pieces, images):
    tokens, width = mixed.shape

    def kernel(mixed_ref, in_ref, piece, *refs):
        w_refs, (attn_ref, hidden_ref, mlp_ref) = refs[:-3], refs[-3:]
        attn = [mm(mixed_ref[...], w[...], ((1,), (0,))) for w in w_refs]
        attn = jnp.concatenate(attn, axis=1)
        attn_ref[...] = attn
        hidden = in_ref[...].astype(F32) + piece[0, 2:3, :] * attn
        hidden_ref[...] = hidden
        normed, _ = normal(hidden)
        mlp_ref[...] = (normed * (1.0 + piece[0, 4:5, :]) + piece[0, 3:4, :]).astype(BF)

    rows = tokens // images
    outs = [(rows, (width,), F32), (rows, (width,), F32), (rows, (width,), BF)]
    return per_image(kernel, images, [mixed, inputs, pieces], out_b, outs, 32, "attention_tail")


def block_tail(hidden_mid, down_b, hidden_one, cotangent, pieces, count, images):
    tokens, width = hidden_one.shape

    def kernel(mid_ref, hidden_ref, cot_ref, piece, *refs):
        w_refs, (count_ref, out_ref, gate_ref) = refs[:-3], refs[-3:]
        mlp = [mm(mid_ref[...], w[...], ((1,), (0,))) for w in w_refs]
        mlp = jnp.concatenate(mlp, axis=1)
        out_ref[...] = (hidden_ref[...] + piece[0, 5:6, :] * mlp).astype(BF)
        real = (pl.program_id(0) < count_ref[0]).astype(F32)
        grad = cot_ref[...].astype(F32) * real
        gate_ref[0] = jnp.sum(grad * mlp, axis=0, keepdims=True)

    rows = tokens // images
    outs = [(rows, (width,), BF), (1, (1, width), F32)]
    by_image = [hidden_mid, hidden_one, cotangent, pieces]
    return per_image(kernel, images, by_image, down_b, outs, 40, "block_tail", count)


def middle_back(d_mlp_in, hidden_one, attn_out, cotangent, pieces, out_b, count, images):
    tokens, width = d_mlp_in.shape
    blocks, columns = len(out_b), out_b[0].shape[1]

    def kernel(in_ref, hidden_ref, attn_ref, cot_ref, piece, *refs):
        w_refs, count_ref, refs = refs[:blocks], refs[blocks], refs[blocks + 1 :]
        d_hidden_ref, d_mixed_ref, sums_ref = refs[:3]
        d_in = in_ref[...]
        normed, inverse = normal(hidden_ref[...])
        sums_ref[0, 0:1] = jnp.sum(d_in, axis=0, keepdims=True)
        sums_ref[0, 1:2] = jnp.sum(d_in * normed, axis=0, keepdims=True)
        real = (pl.program_id(0) < count_ref[0]).astype(F32)
        grad = cot_ref[...].astype(F32) * real
        d_hidden = grad + normal_back(d_in * (1.0 + piece[0, 4:5, :]), normed, inverse)
        d_hidden_ref[...] = d_hidden
        sums_ref[0, 2:3] = jnp.sum(d_hidden * attn_ref[...], axis=0, keepdims=True)
        d_attn = (piece[0, 2:3, :] * d_hidden).astype(BF)
        d_mixed = None
        for j, (w, out) in enumerate(zip(w_refs, refs[3:])):
            part = d_attn[:, j * columns : (j + 1) * columns]
            out[...] = part
            term = mm(part, w[...], ((1,), (1,)))
            d_mixed = term if d_mixed is None else d_mixed + term
        d_mixed_ref[...] = d_mixed.astype(BF)

    rows = tokens // images
    outs = [(rows, (width,), F32), (rows, (width,), BF), (1, (3, width), F32)]
    outs += [(rows, (columns,), BF)] * blocks
    by_image = [d_mlp_in, hidden_one, attn_out, cotangent, pieces]
    return per_image(kernel, images, by_image, out_b, outs, 40, "middle_back", count)


def block_head_back(d_packed, d_hidden, inputs, pieces, qkv_b, images):
    tokens, width = d_hidden.shape
    blocks = len(qkv_b)

    def kernel(*refs):
        d_refs, (d_hidden_ref, in_ref, piece) = refs[:blocks], refs[blocks : blocks + 3]
        w_refs, (out_ref, sums_ref) = refs[blocks + 3 : -2], refs[-2:]
        d_in = None
        for d, w in zip(d_refs, w_refs):
            term = mm(d[...], w[...], ((1,), (1,)))
            d_in = term if d_in is None else d_in + term
        normed, inverse = normal(in_ref[...].astype(F32))
        sums_ref[0, 0:1] = jnp.sum(d_in, axis=0, keepdims=True)
        sums_ref[0, 1:2] = jnp.sum(d_in * normed, axis=0, keepdims=True)
        back = normal_back(d_in * (1.0 + piece[0, 1:2, :]), normed, inverse)
        out_ref[...] = (d_hidden_ref[...] + back).astype(BF)

    outs = [(tokens // images, (width,), BF), (1, (2, width), F32)]
    by_image = [*d_packed, d_hidden, inputs, pieces]
    return per_image(kernel, images, by_image, qkv_b, outs, 48, "block_head_back")


def grad_stacks(places, a, parts):
    tokens, features = a.shape
    columns = parts[0].shape[1]
    z, count = places.z, len(parts)
    rows = features // (4 * z)
    chunk = chunk_of(columns, 900)
    masks = [places.masks(0), places.masks(1)]
    total = len(masks[0])

    def kernel(at, a_ref, *refs):
        d_refs, (own_ref, send_ref, turned, product) = refs[:count], refs[count:]

        @pl.when(pl.program_id(0) == 0)
        def _():
            turned[...] = a_ref[...].T

        for i, d_ref in enumerate(d_refs):
            whole = mm(turned[...], d_ref[...], ((1,), (0,)))
            for k in range(4 * z):
                product[i, k] = whole[k * rows : (k + 1) * rows].astype(BF)
        core, y, x = at[0], at[1], at[2]
        for out, owner in ((own_ref, core), (send_ref, 1 - core)):
            for j in range(total):
                dy = jnp.where(owner == 0, masks[0][j][0], masks[1][j][0])
                dx = jnp.where(owner == 0, masks[0][j][1], masks[1][j][1])
                for k in range(z):
                    out[j, k] = product[x ^ dx, (k * 2 + (y ^ dy)) * 2 + owner]

    at = jnp.stack([places.at_c, places.at_y, places.x]).astype(jnp.int32)
    shape = (total, z, rows, columns)
    out = pl.BlockSpec((total, z, rows, chunk), lambda i: (0, 0, 0, i))
    return pl.pallas_call(
        kernel,
        grid=(-(-columns // chunk),),
        out_shape=[jax.ShapeDtypeStruct(shape, BF)] * 2,
        in_specs=[pl.BlockSpec(memory_space=pltpu.SMEM), whole_block(a)]
        + [pl.BlockSpec((tokens, chunk), lambda i: (0, i))] * count,
        out_specs=[out, out],
        scratch_shapes=[
            pltpu.VMEM((features, tokens), BF),
            pltpu.VMEM((count, 4 * z, rows, chunk), BF),
        ],
        compiler_params=pltpu.CompilerParams(vmem_limit_bytes=56 * 2**20),
        cost_estimate=SHORT,
        name="grad_stacks",
    )(at, a, *parts)


class Places:
    def __init__(self):
        self.wide, self.narrow = lax.axis_size("wide"), lax.axis_size("narrow")
        self.z = self.wide // 4
        w = lax.axis_index("wide")
        self.w, self.x = w, lax.axis_index("narrow")
        self.at_z, self.at_y, self.at_c = w // 4, (w // 2) % 2, w % 2
        self.z_bits = [1 << i for i in range(self.z.bit_length() - 1)]
        self.x_bits = [1 << i for i in range(self.narrow.bit_length() - 1)]
        x_masks = [(0, bit) for bit in self.x_bits]
        self.orders = ([(1, 0)] + x_masks, x_masks + [(1, 0)])

    def swap(self, value, flip):
        pairs = []
        for w in range(self.wide):
            for x in range(self.narrow):
                dz, dy, dc, dx = flip(w % 2)
                to = (w // 4 ^ dz) * 4 + (w // 2 % 2 ^ dy) * 2 + (w % 2 ^ dc)
                pairs.append((w * self.narrow + x, to * self.narrow + (x ^ dx)))
        return lax.ppermute(value, ALL, pairs)

    def step_flip(self, i):
        return lambda core: (0, self.orders[core][i][0], 0, self.orders[core][i][1])

    def masks(self, core):
        out = [(0, 0)]
        for dy, dx in self.orders[core]:
            out = out + [(y ^ dy, x ^ dx) for y, x in out]
        return out

    def all_bits(self):
        out = [(0, (bit, 0, 0, 0), self.at_z // bit % 2) for bit in self.z_bits]
        out.append((1, (0, 1, 0, 0), self.at_y))
        out += [(3, (0, 0, 0, bit), self.x // bit % 2) for bit in self.x_bits]
        out.append((2, (0, 0, 1, 0), self.at_c))
        return out

    def gather_small(self, value):
        value = value[None, None, None, None]
        for axis, flip, bit in self.all_bits():
            other = self.swap(value, lambda core: flip)
            low = jnp.where(bit == 0, value, other)
            high = jnp.where(bit == 0, other, value)
            value = jnp.concatenate([low, high], axis)
        return value.reshape(self.wide * self.narrow, *value.shape[4:])

    def add_all(self, value):
        for _, flip, _ in self.all_bits():
            value = value + self.swap(value, lambda core: flip)
        return value

    def add_narrow(self, value):
        for bit in self.x_bits:
            value = value + self.swap(value, lambda core: (0, 0, 0, bit))
        return value

    def scatter_chip_row(self, value):
        value = value.reshape(self.z, 2, 2, *value.shape[1:])
        other = self.swap(take(value, 2, 1 - self.at_c), lambda core: (0, 0, 1, 0))
        value = take(value, 2, self.at_c) + other
        other = self.swap(take(value, 1, 1 - self.at_y), lambda core: (0, 1, 0, 0))
        return take(value, 1, self.at_y) + other

    def scatter_z(self, value):
        for bit in reversed(self.z_bits):
            value = value.reshape(2, bit, *value.shape[1:])
            here = self.at_z // bit % 2
            other = self.swap(take(value, 0, 1 - here), lambda core: (bit, 0, 0, 0))
            value = take(value, 0, here) + other
        return value[0]

    def trade_narrow(self, value):
        if self.narrow != 2:
            return lax.all_to_all(value, "narrow", 0, 0, tiled=True)
        other = self.swap(take(value, 0, 1 - self.x), lambda core: (0, 0, 0, 1))
        own = take(value, 0, self.x)
        return jnp.stack([pick([own, other], self.x), pick([other, own], self.x)])


def pick(parts, index):
    if len(parts) == 1:
        return parts[0]
    if len(parts) == 2:
        return jnp.where(index == 0, parts[0], parts[1])
    return lax.dynamic_index_in_dim(jnp.stack(parts), index, 0, keepdims=False)


def take(value, axis, index):
    return lax.dynamic_index_in_dim(value, index, axis, keepdims=False)


def after(value, *before):
    return lax.optimization_barrier((value,) + before)[0]


def assemble(places, parts):
    half, z, rows, columns = parts[0].shape
    joined = columns % 128 == 0
    masks = [places.masks(0), places.masks(1)]

    def kernel(at, s0, s1, t0, t1, out, held, sem, out_sem):
        core, y, x, here_z = at[0], at[1], at[2], at[3]
        copies = []
        for i, src in enumerate((s0, s1, t0, t1)):
            owner = core ^ (i // 2)
            for j in range(half):
                k = j + half * (i % 2)
                dy = jnp.where(owner == 0, masks[0][k][0], masks[1][k][0])
                dx = jnp.where(owner == 0, masks[0][k][1], masks[1][k][1])
                for d in range(z):
                    if joined:
                        lanes = pl.ds(pl.multiple_of((x ^ dx) * columns, 128), columns)
                        to = held.at[here_z ^ d, y ^ dy, owner, :, lanes]
                    else:
                        to = held.at[x ^ dx, here_z ^ d, y ^ dy, owner]
                    copies.append(pltpu.make_async_copy(src.at[j, d], to, sem.at[len(copies)]))
        for copy in copies:
            copy.start()
        for copy in copies:
            copy.wait()
        whole = pltpu.make_async_copy(held, out, out_sem)
        whole.start()
        whole.wait()

    shape = (places.narrow, z, 2, 2, rows, columns)
    if joined:
        shape = (z, 2, 2, rows, places.narrow * columns)
    at = jnp.stack([places.at_c, places.at_y, places.x, places.at_z]).astype(jnp.int32)
    return pl.pallas_call(
        kernel,
        out_shape=jax.ShapeDtypeStruct(shape, BF),
        in_specs=[pl.BlockSpec(memory_space=pltpu.SMEM)] + [pl.BlockSpec(memory_space=pl.ANY)] * 4,
        out_specs=pl.BlockSpec(memory_space=pl.ANY),
        scratch_shapes=[
            pltpu.VMEM(shape, BF),
            pltpu.SemaphoreType.DMA((4 * half * z,)),
            pltpu.SemaphoreType.DMA,
        ],
        compiler_params=pltpu.CompilerParams(vmem_limit_bytes=24 * 2**20),
        cost_estimate=SHORT,
        name="assemble",
    )(at, *parts)


class Slots:
    def __init__(self):
        self.before, self.now = (), []

    def tie(self, value):
        return after(value, *self.before) if self.before else value

    def note(self, *values):
        self.now += values

    def next(self, *values):
        self.note(*values)
        self.before, self.now = tuple(self.now), []


class Gather:
    def __init__(self, places, shard):
        self.places, self.rows = places, places.wide * shard.shape[0]
        self.held, self.other = shard[None], None

    def step_z(self, bit, *before):
        other = self.places.swap(after(self.held, *before), lambda core: (bit, 0, 0, 0))
        self.held = jnp.concatenate([self.held, other], 0)
        if bit == self.places.z_bits[-1]:
            self.held = self.held[None]
        return other

    def all_z(self, *before):
        other = None
        for i, bit in enumerate(self.places.z_bits):
            other = self.step_z(bit, *(before if i == 0 else ()))
        return other

    def step(self, i, *before):
        if self.other is not None:
            self.held = jnp.concatenate([self.held, self.other], 0)
        self.other = self.places.swap(after(self.held, *before), self.places.step_flip(i))
        return self.other

    def first(self, *before):
        for i in range(len(self.places.orders[0]) - 1):
            other = self.step(i, *(before if i == 0 else ()))
        return other

    def last(self, *before):
        return self.step(len(self.places.orders[0]) - 1, *before)

    def cores(self, *before):
        parts = after((self.held, self.other), *before)
        parts = list(parts)
        self.parts = parts + [self.places.swap(p, lambda core: (0, 0, 1, 0)) for p in parts]
        return self.parts[2:]

    def whole(self, *before):
        whole = assemble(self.places, after(tuple(self.parts), *before))
        return list(whole.reshape(-1, self.rows, whole.shape[-1]))


class Scatter:
    def __init__(self, places, a, parts):
        self.places = places
        self.stack, self.to_core = grad_stacks(places, a, parts)
        self.half = self.stack.shape[0]

    def cores(self, *before):
        self.arrived = self.places.swap(after(self.to_core, *before), lambda core: (0, 0, 1, 0))
        return self.arrived

    def first(self, *before):
        places, arrived = self.places, self.arrived
        self.half = half = self.half // 2
        send = self.stack[half:].astype(F32) + arrived[half:].astype(F32)
        flip = places.step_flip(len(places.orders[0]) - 1)
        self.other = places.swap(after(send.astype(BF), *before), flip)
        self.own = self.stack[:half].astype(F32) + arrived[:half].astype(F32)
        return self.other

    def last(self, *before):
        places = self.places
        for i in reversed(range(len(places.orders[0]) - 1)):
            held = self.own + self.other.astype(F32)
            self.half = half = self.half // 2
            send = after(held[half:].astype(BF), *before)
            self.own, self.other = held[:half], places.swap(send, places.step_flip(i))
        return self.other

    def step_z(self, bit, *before):
        places = self.places
        held = self.own + self.other.astype(F32)
        if bit == places.z_bits[-1]:
            held = held[0]
            held = jnp.stack([take(held, 0, places.at_z ^ d) for d in range(places.z)])
        send = after(held[bit:].astype(BF), *before)
        self.own, self.other = held[:bit], places.swap(send, lambda core: (bit, 0, 0, 0))
        return self.other

    def all_z(self, *before):
        for i, bit in enumerate(reversed(self.places.z_bits)):
            other = self.step_z(bit, *(before if i == 0 else ()))
        return other

    def result(self):
        return (self.own + self.other.astype(F32))[0]


def dot(a, b, dims, out=F32):
    return lax.dot_general(a, b, (dims, ((), ())), preferred_element_type=F32).astype(out)


def split(a, count):
    width = a.shape[1] // count
    return [a[:, n * width : (n + 1) * width] for n in range(count)]


def on_device(
    inputs,
    cotangent,
    class_ids,
    step_ids,
    image_counts,
    w_qkv,
    w_out,
    w_gate,
    w_up,
    w_down,
    ada_weight,
    ada_bias,
    class_table,
    norm_gains,
):
    places = Places()
    wide, narrow, at_w, at_n = places.wide, places.narrow, places.w, places.x
    images, length, width = inputs.shape
    tables, sums = head_tables(length), head_sums()
    gains = jnp.tile(norm_gains, (1, H))
    local_count = image_counts[0]

    tokens = images * length

    def flat(v):
        return v.reshape(tokens, -1)

    def deep(v):
        return v.reshape(images, length, -1)

    t = Slots()
    z_low, z_high = places.z_bits[0], places.z_bits[1:]
    qkv, out, gate, up, down = [
        Gather(places, shard) for shard in (w_qkv, w_out, w_gate, w_up, w_down)
    ]

    def high_z(weight):
        for i, bit in enumerate(z_high):
            other = weight.step_z(bit, *(t.before if i == 0 else ()))
        return other

    def high_sum(grad):
        for i, bit in enumerate(reversed(z_high)):
            other = grad.step_z(bit, *(t.before if i == 0 else ()))
        return other

    small = [class_ids, step_ids, image_counts, ada_bias]
    small = jnp.concatenate([v.astype(F32) for v in small])[None]
    small = places.gather_small(small)[:, 0]
    t.next(qkv.step_z(z_low), small)

    ids = small[:, : 2 * images].reshape(-1, 2, images).transpose(0, 2, 1).reshape(-1, 2)
    ids = t.tie(ids).astype(jnp.int32)
    real_count = jnp.sum(small[:, 2 * images])
    bias = small[:, 2 * images + 1 :].reshape(-1)
    rows_here, cols_here = class_table.shape
    class_hot = ids[:, :1] - at_n * rows_here == jnp.arange(rows_here, dtype=jnp.int32)[None, :]
    picked = dot(class_hot.astype(BF), class_table, ((1,), (0,)))
    column = at_w * cols_here + jnp.arange(cols_here, dtype=jnp.int32)
    half_width = width // 2
    frequency = jnp.exp(-math.log(10000.0) * (column % half_width).astype(F32) / half_width)
    angles = ids[:, 1:].astype(F32) * frequency[None, :]
    wave = jnp.where(column[None, :] < half_width, jnp.cos(angles), jnp.sin(angles))
    condition = places.add_narrow(picked) + wave
    cond_act = jax.nn.silu(condition).astype(BF)
    mod_part = dot(cond_act, ada_weight, ((1,), (0,)))
    mod_part = places.scatter_chip_row(mod_part.reshape(wide, narrow, images, -1))
    t.next(high_z(qkv), mod_part)

    mod_part = places.trade_narrow(places.scatter_z(t.tie(mod_part)))
    modulation = mod_part.transpose(1, 0, 2).reshape(images, -1) + bias
    t.next(qkv.first(*t.before), out.all_z(*t.before), modulation)

    pieces = t.tie(modulation).reshape(images, 6, width)
    normed, _ = layer_norm(inputs.astype(F32))
    attn_in = flat((normed * (1.0 + pieces[:, 1:2]) + pieces[:, 0:1]).astype(BF))
    t.next(qkv.last(*t.before), gate.all_z(*t.before), attn_in, *tables, sums)

    t.note(*qkv.cores(*t.before))
    t.next(out.first(*t.before), gate.first(*t.before), up.step_z(z_low, *t.before))

    qkv_b = qkv.whole(*t.before)
    packed = project(attn_in, qkv_b)
    t.next(out.last(*t.before), gate.last(*t.before), high_z(up), *packed)

    t.note(*out.cores(*t.before), *gate.cores(*t.before))
    packed = t.tie(packed)
    queries, key_rows, value_rows, mixed = attention_forward(packed, gains, tables, sums, images)
    t.next(up.first(*t.before), down.step_z(z_low, *t.before), mixed)

    out_b = out.whole(*t.before)
    attn_out, hidden_one, mlp_in = attention_tail(mixed, out_b, flat(inputs), pieces, images)
    t.next(up.last(*t.before), high_z(down), mlp_in)

    t.note(*up.cores(*t.before))
    (gate_b,) = gate.whole(*t.before)
    t.next(down.first(*t.before), gate_b)

    (up_b,) = up.whole(*t.before)
    gate_val, up_val, hidden_mid = gated(mlp_in, gate_b, up_b)
    slot_real = (jnp.arange(images, dtype=jnp.int32) < local_count).astype(F32)
    grad_y = cotangent.astype(F32) * slot_real[:, None, None]
    d_mlp = flat((pieces[:, 5:6] * grad_y).astype(BF))
    t.next(down.last(*t.before), hidden_mid)

    t.note(*down.cores(*t.before))
    g_down = Scatter(places, t.tie(hidden_mid), split(d_mlp, narrow))
    t.next(g_down.cores())

    g_down_1 = g_down.first(*t.before)
    down_b = down.whole(*t.before)
    d_gate, d_up, d_mlp_in = gated_back(
        split(d_mlp, narrow), down_b, gate_val, up_val, gate_b, up_b
    )
    t.next(g_down_1, d_mlp_in)

    g_down_2 = g_down.last(*t.before)
    g_gate = Scatter(places, mlp_in, split(t.tie(d_gate), narrow))
    t.next(g_down_2, g_gate.cores())

    g_gate_1 = g_gate.first(*t.before)
    t.note(g_gate_1, high_sum(g_down))
    g_up = Scatter(places, mlp_in, split(t.tie(d_up), narrow))
    t.note(g_up.cores())
    d_hidden, d_mixed, sums_b, *d_attn = middle_back(
        t.tie(d_mlp_in), hidden_one, attn_out, flat(cotangent), pieces, out_b, image_counts, images
    )
    g_out = Scatter(places, mixed, d_attn)
    t.note(g_out.cores())
    t.next(d_mixed)

    t.note(g_up.first(*t.before), g_gate.last(*t.before), g_down.step_z(z_low, *t.before))
    d_packed, gain_terms = attention_backward(
        packed, queries, key_rows, value_rows, t.tie(d_mixed), gains, tables, sums, images
    )
    t.next(*d_packed)

    t.note(g_up.last(*t.before), g_out.first(*t.before), high_sum(g_gate))
    g_qkv = Scatter(places, attn_in, t.tie(d_packed))
    grad_gains = gain_terms.sum(0).reshape(2, H, HD).sum(1)
    t.next(g_qkv.cores())

    t.note(g_qkv.first(*t.before), g_out.last(*t.before), high_sum(g_up))
    t.note(g_gate.step_z(z_low, *t.before))
    d_tokens, sums_a = block_head_back(
        t.tie(d_packed), d_hidden, flat(inputs), pieces, qkv_b, images
    )
    block_output, sums_gate = block_tail(
        t.tie(hidden_mid), down_b, hidden_one, flat(cotangent), pieces, image_counts, images
    )
    d_modulation = jnp.concatenate([sums_a, sums_b[:, 2:], sums_b[:, :2], sums_gate], axis=1)
    d_modulation = d_modulation.astype(BF).reshape(images, -1)
    t.next(d_modulation, d_tokens, block_output)

    t.note(high_sum(g_out), g_up.step_z(z_low, *t.before))
    gain_sum = places.add_all(t.tie(grad_gains))
    t.next(g_qkv.last(*t.before))

    t.note(high_sum(g_qkv), g_out.step_z(z_low, *t.before))
    d_mod = places.gather_small(t.tie(d_modulation)).reshape(-1, d_modulation.shape[1])
    g_qkv.step_z(z_low)
    r_qkv, r_out, r_gate, r_up, r_down = [
        g.result() for g in (g_qkv, g_out, g_gate, g_up, g_down)
    ]

    ada_cols = ada_weight.shape[1]
    d_mod_here = lax.dynamic_slice_in_dim(d_mod, at_n * ada_cols, ada_cols, 1)
    g_ada = dot(cond_act, d_mod_here, ((0,), (0,)))
    bias_cols = ada_bias.shape[0]
    bias_at = (at_w * narrow + at_n) * bias_cols
    g_bias = jnp.sum(lax.dynamic_slice_in_dim(d_mod, bias_at, bias_cols, 1).astype(F32), axis=0)
    d_cond_act = places.add_narrow(dot(d_mod_here, ada_weight, ((1,), (1,))))
    cond_sigmoid = jax.nn.sigmoid(condition)
    d_condition = d_cond_act * cond_sigmoid * (1.0 + condition * (1.0 - cond_sigmoid))
    g_table = jnp.dot(class_hot.astype(F32).T, d_condition, precision=HIGHEST)
    return (
        deep(block_output),
        deep(d_tokens),
        r_qkv / real_count,
        r_out / real_count,
        r_gate / real_count,
        r_up / real_count,
        r_down / real_count,
        g_ada / real_count,
        g_bias / real_count,
        g_table / real_count,
        gain_sum / real_count,
    )


def solution(mesh):
    split = P("wide", "narrow")
    images = P(ALL, None, None)
    return jax.shard_map(
        on_device,
        mesh=mesh,
        in_specs=(
            images,
            images,
            P(ALL),
            P(ALL),
            P(ALL),
            split,
            split,
            split,
            split,
            split,
            split,
            P(ALL),
            P("narrow", "wide"),
            P(),
        ),
        out_specs=(
            images,
            images,
            split,
            split,
            split,
            split,
            split,
            split,
            P(ALL),
            P("narrow", "wide"),
            P(),
        ),
        check_vma=False,
    )
```

```python
import math

import jax
import jax.numpy as jnp
from jax import lax
from jax.experimental import pallas as pl
from jax.experimental.pallas import tpu as pltpu
from jax.sharding import PartitionSpec as P

H = 16
HD = 72
CLASSES = 1000
GRID = 16

EPSILON = 1e-06
HIGHEST = lax.Precision.HIGHEST
ALL = ("wide", "narrow")
BF = jnp.bfloat16
F32 = jnp.float32
LONG = pl.CostEstimate(flops=10**12, bytes_accessed=1, transcendentals=0)


def layer_norm(values):
    centre = values - jnp.mean(values, axis=-1, keepdims=True)
    inverse = lax.rsqrt(jnp.mean(centre * centre, axis=-1, keepdims=True) + EPSILON)
    return (centre * inverse, inverse)


def head_tables(length):
    quarter = HD // 4
    lane = jnp.arange(H * HD, dtype=jnp.int32) % HD
    frequency = 10000.0 ** (-(lane % quarter).astype(F32) / quarter)
    patch = jnp.arange(length, dtype=jnp.int32)[:, None]
    place = jnp.where(lane[None, :] < 2 * quarter, patch // GRID, patch % GRID)
    angles = place.astype(F32) * frequency[None, :]
    cosine, sine = jnp.cos(angles), jnp.sin(angles)
    first = (lane // quarter % 2 == 0)[None, :]
    return [cosine, jnp.where(first, -sine, 0.0), jnp.where(first, 0.0, sine)]


def head_sums():
    lane = lax.broadcasted_iota(jnp.int32, (H * HD, 128), 0) // HD
    return (lane == lax.broadcasted_iota(jnp.int32, (H * HD, 128), 1)).astype(BF)


def exact_dot(a, b, dims):
    total = None
    for _ in range(3):
        term = a.astype(BF)
        a = a - term.astype(F32)
        part = lax.dot_general(term, b, (dims, ((), ())), preferred_element_type=F32)
        total = part if total is None else total + part
    return total


def head_mean(values, sums):
    mean = exact_dot(values, sums, ((1,), (0,))) * (1.0 / HD)
    return exact_dot(mean, sums, ((1,), (1,)))


def shifted(values, cosine, above, below, sign):
    quarter, width = HD // 4, values.shape[1]
    up = pltpu.roll(values, width - quarter, 1)
    down = pltpu.roll(values, quarter, 1)
    return values * cosine + sign * (up * above + down * below)


def window(head):
    first, last = head * HD // 128 * 128, ((head + 1) * HD + 127) // 128 * 128
    return first, last


def only(values, head):
    first, last = window(head)
    part = values[:, first:last]
    lane = first + lax.broadcasted_iota(jnp.int32, (1, last - first), 1)
    mine = ((lane >= head * HD) & (lane < (head + 1) * HD)).astype(values.dtype)
    return part * mine


class Tiles:
    def __init__(self, store):
        self.store, self.held = store, {}

    def add(self, head, value):
        first, last = window(head)
        for tile in range(first // 128, last // 128):
            part = value[:, tile * 128 - first : tile * 128 - first + 128]
            self.held[tile] = self.held[tile] + part if tile in self.held else part
        done = (head + 1) * HD // 128
        for tile in sorted(self.held):
            if tile < done or head == H - 1:
                self.store(tile * 128, self.held.pop(tile))


def mm(a, b, dims):
    return lax.dot_general(a, b, (dims, ((), ())), preferred_element_type=F32)


def softmax_of(queries, keys, head):
    first, last = window(head)
    scores = mm(queries[:, first:last], only(keys, head), ((1,), (1,))) * (HD ** (-0.5))
    exponent = jnp.exp(scores - jnp.max(scores, axis=1, keepdims=True))
    return exponent / jnp.sum(exponent, axis=1, keepdims=True)


def attention_forward(packed, gains, tables, sums, images):
    tokens = packed[0].shape[0]
    length, width, blocks = tokens // images, H * HD, len(packed)

    def kernel(*refs):
        parts, refs = refs[:blocks], refs[blocks:]
        gain, cosine, above, below, sums_ref, q_ref, k_ref, v_ref, mixed_ref = refs
        whole = jnp.concatenate([p[...] for p in parts], axis=1)
        sums_here = sums_ref[...]
        for i, ref in enumerate((q_ref, k_ref)):
            raw = whole[:, i * width : (i + 1) * width]
            normed = raw * lax.rsqrt(head_mean(raw * raw, sums_here) + EPSILON)
            turned = shifted(normed * gain[i : i + 1, :], cosine[...], above[...], below[...], 1.0)
            ref[...] = turned.astype(BF)
        v_ref[...] = whole[:, 2 * width :].astype(BF)

        def store(first, value):
            mixed_ref[:, first : first + 128] = value.astype(BF)

        mixed = Tiles(store)
        for head in range(H):
            attention = softmax_of(q_ref, k_ref, head).astype(BF)
            mixed.add(head, mm(attention, only(v_ref, head), ((1,), (0,))))

    def rows(n):
        return pl.BlockSpec((length, n), lambda i: (i, 0))

    def all_of(a):
        return pl.BlockSpec(a.shape, lambda i: (0, 0))

    out = jax.ShapeDtypeStruct((tokens, width), BF)
    return pl.pallas_call(
        kernel,
        grid=(images,),
        out_shape=[out] * 4,
        in_specs=[rows(p.shape[1]) for p in packed] + [all_of(a) for a in (gains, *tables, sums)],
        out_specs=[rows(width)] * 4,
        compiler_params=pltpu.CompilerParams(vmem_limit_bytes=48 * 2**20),
        cost_estimate=LONG,
        name="attention_forward",
    )(*packed, gains, *tables, sums)


def attention_backward(packed, queries, keys, values, d_mixed, gains, tables, sums, images):
    tokens = queries.shape[0]
    length, width, blocks = tokens // images, H * HD, len(packed)
    block = packed[0].shape[1]

    def kernel(*refs):
        parts, refs = refs[:blocks], refs[blocks:]
        q_ref, k_ref, v_ref, d_ref, gain, cosine, above, below, sums_ref = refs[:9]
        outs, (gain_ref, d_q, d_k, d_v) = refs[9 : 9 + blocks], refs[9 + blocks :]

        def store_to(ref):
            def store(first, value):
                ref[:, first : first + 128] = value

            return store

        all_q, all_k, all_v = [Tiles(store_to(ref)) for ref in (d_q, d_k, d_v)]
        for head in range(H):
            first, last = window(head)
            q_here, k_here, d_here = [only(ref, head) for ref in (q_ref, k_ref, d_ref)]
            scores = mm(k_here, q_ref[:, first:last], ((1,), (1,))) * (HD ** (-0.5))
            exponent = jnp.exp(scores - jnp.max(scores, axis=0, keepdims=True))
            soft = exponent / jnp.sum(exponent, axis=0, keepdims=True)
            all_v.add(head, mm(soft.astype(BF), d_here, ((1,), (0,))))
            d_soft = mm(v_ref[:, first:last], d_here, ((1,), (1,)))
            inner = jnp.sum(soft * d_soft, axis=0, keepdims=True)
            d_scores = (soft * (d_soft - inner) * (HD ** (-0.5))).astype(BF)
            all_k.add(head, mm(d_scores, q_here, ((1,), (0,))))
            all_q.add(head, mm(d_scores, k_here, ((0,), (0,))))
        whole = jnp.concatenate([p[...] for p in parts], axis=1)
        sums_here = sums_ref[...]
        done = []
        for i, ref in enumerate((d_q, d_k)):
            raw = whole[:, i * width : (i + 1) * width]
            inverse = lax.rsqrt(head_mean(raw * raw, sums_here) + EPSILON)
            normed = raw * inverse
            scaled = shifted(ref[...], cosine[...], above[...], below[...], -1.0)
            gain_ref[0, i : i + 1, :] = jnp.sum(scaled * normed, axis=0, keepdims=True)
            incoming = scaled * gain[i : i + 1, :]
            mean = head_mean(incoming * normed, sums_here)
            done.append((inverse * (incoming - normed * mean)).astype(BF))
        done.append(d_v[...].astype(BF))
        done = jnp.concatenate(done, axis=1)
        for j, out in enumerate(outs):
            out[...] = done[:, j * block : (j + 1) * block]

    def rows(n):
        return pl.BlockSpec((length, n), lambda i: (i, 0))

    def all_of(a):
        return pl.BlockSpec(a.shape, lambda i: (0, 0))

    outs = pl.pallas_call(
        kernel,
        grid=(images,),
        out_shape=[jax.ShapeDtypeStruct((tokens, block), BF)] * blocks
        + [jax.ShapeDtypeStruct((images, 2, width), F32)],
        in_specs=[rows(block)] * blocks
        + [rows(width)] * 4
        + [all_of(a) for a in (gains, *tables, sums)],
        out_specs=[rows(block)] * blocks + [pl.BlockSpec((1, 2, width), lambda i: (i, 0, 0))],
        scratch_shapes=[pltpu.VMEM((length, width), F32)] * 3,
        compiler_params=pltpu.CompilerParams(vmem_limit_bytes=56 * 2**20),
        cost_estimate=LONG,
        name="attention_backward",
    )(*packed, queries, keys, values, d_mixed, gains, *tables, sums)
    return outs[:blocks], outs[blocks]

def whole_block(a):
    return pl.BlockSpec(a.shape, lambda *i: (0,) * a.ndim)


def chunk_of(columns, most):
    count = -(-columns // most)
    return columns if count == 1 else -(-columns // (128 * count)) * 128


def project(a, blocks):
    tokens, depth = a.shape
    count, _, columns = blocks.shape
    chunk = chunk_of(columns, 640)

    def kernel(a_ref, *refs):
        for w_ref, out_ref in zip(refs[:count], refs[count:]):
            out_ref[...] = mm(a_ref[...], w_ref[...], ((1,), (0,)))

    return pl.pallas_call(
        kernel,
        grid=(-(-columns // chunk),),
        out_shape=[jax.ShapeDtypeStruct((tokens, columns), F32)] * count,
        in_specs=[whole_block(a)]
        + [pl.BlockSpec((None, depth, chunk), lambda i, j=j: (j, 0, i)) for j in range(count)],
        out_specs=[pl.BlockSpec((tokens, chunk), lambda i: (0, i))] * count,
        compiler_params=pltpu.CompilerParams(vmem_limit_bytes=40 * 2**20),
        cost_estimate=LONG,
        name="project",
    )(a, *[blocks] * count)


def gated(a, w_gate, w_up):
    tokens, depth = a.shape
    columns = w_gate.shape[1]
    chunk = 512

    def kernel(a_ref, g_ref, u_ref, gate_ref, up_ref, mid_ref):
        gate = mm(a_ref[...], g_ref[...], ((1,), (0,)))
        up = mm(a_ref[...], u_ref[...], ((1,), (0,)))
        gate_ref[...] = gate
        up_ref[...] = up
        mid_ref[...] = (gate * jax.nn.sigmoid(gate) * up).astype(BF)

    weight = pl.BlockSpec((depth, chunk), lambda i: (0, i))
    out = pl.BlockSpec((tokens, chunk), lambda i: (0, i))
    return pl.pallas_call(
        kernel,
        grid=(columns // chunk,),
        out_shape=[jax.ShapeDtypeStruct((tokens, columns), t) for t in (F32, F32, BF)],
        in_specs=[whole_block(a), weight, weight],
        out_specs=[out] * 3,
        compiler_params=pltpu.CompilerParams(vmem_limit_bytes=40 * 2**20),
        cost_estimate=LONG,
        name="gated",
    )(a, w_gate, w_up)


def gated_back(d_parts, down, gate_val, up_val, w_gate, w_up):
    tokens, columns = gate_val.shape
    depth, count, chunk = w_gate.shape[0], down.shape[0], 512

    def kernel(*refs):
        d_refs, w_refs, refs = refs[:count], refs[count : 2 * count], refs[2 * count :]
        gate_ref, up_ref, g_ref, u_ref, d_gate_ref, d_up_ref, in_ref = refs
        d_mid = None
        for d_ref, w_ref in zip(d_refs, w_refs):
            term = mm(d_ref[...], w_ref[...], ((1,), (1,)))
            d_mid = term if d_mid is None else d_mid + term
        gate, up = gate_ref[...], up_ref[...]
        sigmoid = jax.nn.sigmoid(gate)
        silu = gate * sigmoid
        d_gate = (d_mid * up * (sigmoid + silu * (1.0 - sigmoid))).astype(BF)
        d_up = (d_mid * silu).astype(BF)
        d_gate_ref[...] = d_gate
        d_up_ref[...] = d_up
        term = mm(d_gate, g_ref[...], ((1,), (1,))) + mm(d_up, u_ref[...], ((1,), (1,)))

        @pl.when(pl.program_id(0) == 0)
        def _():
            in_ref[...] = term

        @pl.when(pl.program_id(0) > 0)
        def _():
            in_ref[...] += term

    width = down.shape[2]
    token = pl.BlockSpec((tokens, chunk), lambda i: (0, i))
    weight = pl.BlockSpec((depth, chunk), lambda i: (0, i))
    return pl.pallas_call(
        kernel,
        grid=(columns // chunk,),
        out_shape=[jax.ShapeDtypeStruct((tokens, columns), BF)] * 2
        + [jax.ShapeDtypeStruct((tokens, depth), F32)],
        in_specs=[whole_block(d) for d in d_parts]
        + [pl.BlockSpec((None, chunk, width), lambda i, j=j: (j, i, 0)) for j in range(count)]
        + [token, token, weight, weight],
        out_specs=[token, token, pl.BlockSpec((tokens, depth), lambda i: (0, 0))],
        compiler_params=pltpu.CompilerParams(vmem_limit_bytes=48 * 2**20),
        cost_estimate=LONG,
        name="gated_back",
    )(*d_parts, *[down] * count, gate_val, up_val, w_gate, w_up)


def normal(values):
    centre = values - jnp.mean(values, axis=1, keepdims=True)
    inverse = lax.rsqrt(jnp.mean(centre * centre, axis=1, keepdims=True) + EPSILON)
    return centre * inverse, inverse


def normal_back(gradient, normed, inverse):
    mean = jnp.mean(gradient, axis=1, keepdims=True)
    return inverse * (
        gradient - mean - normed * jnp.mean(gradient * normed, axis=1, keepdims=True)
    )


def per_image(kernel, images, by_image, whole, outs, vmem, name, scalar=None):
    def spec(rows, rest):
        return pl.BlockSpec((rows, *rest), lambda i: (i,) + (0,) * len(rest))

    in_specs = [spec(a.shape[0] // images, a.shape[1:]) for a in by_image]
    in_specs += [whole_block(a) for a in whole]
    args = [*by_image, *whole]
    if scalar is not None:
        in_specs.append(pl.BlockSpec(memory_space=pltpu.SMEM))
        args.append(scalar)
    return pl.pallas_call(
        kernel,
        grid=(images,),
        out_shape=[jax.ShapeDtypeStruct((images * rows, *rest), t) for rows, rest, t in outs],
        in_specs=in_specs,
        out_specs=[spec(rows, rest) for rows, rest, _ in outs],
        compiler_params=pltpu.CompilerParams(vmem_limit_bytes=vmem * 2**20),
        cost_estimate=LONG,
        name=name,
    )(*args)


def attention_tail(mixed, out_b, inputs, pieces, images):
    tokens, width = mixed.shape

    def kernel(mixed_ref, in_ref, piece, *refs):
        w_ref, attn_ref, hidden_ref, mlp_ref = refs
        attn = [mm(mixed_ref[...], w_ref[j], ((1,), (0,))) for j in range(out_b.shape[0])]
        attn = jnp.concatenate(attn, axis=1)
        attn_ref[...] = attn
        hidden = in_ref[...].astype(F32) + piece[0, 2:3, :] * attn
        hidden_ref[...] = hidden
        normed, _ = normal(hidden)
        mlp_ref[...] = (normed * (1.0 + piece[0, 4:5, :]) + piece[0, 3:4, :]).astype(BF)

    rows = tokens // images
    outs = [(rows, (width,), F32), (rows, (width,), F32), (rows, (width,), BF)]
    return per_image(kernel, images, [mixed, inputs, pieces], [out_b], outs, 32, "attention_tail")


def block_tail(hidden_mid, down_b, hidden_one, cotangent, pieces, count, images):
    tokens, width = hidden_one.shape

    def kernel(mid_ref, hidden_ref, cot_ref, piece, *refs):
        w_ref, count_ref, out_ref, gate_ref = refs
        mlp = [mm(mid_ref[...], w_ref[j], ((1,), (0,))) for j in range(down_b.shape[0])]
        mlp = jnp.concatenate(mlp, axis=1)
        out_ref[...] = (hidden_ref[...] + piece[0, 5:6, :] * mlp).astype(BF)
        real = (pl.program_id(0) < count_ref[0]).astype(F32)
        grad = cot_ref[...].astype(F32) * real
        gate_ref[0] = jnp.sum(grad * mlp, axis=0, keepdims=True)

    rows = tokens // images
    outs = [(rows, (width,), BF), (1, (1, width), F32)]
    by_image = [hidden_mid, hidden_one, cotangent, pieces]
    return per_image(kernel, images, by_image, [down_b], outs, 40, "block_tail", count)


def middle_back(d_mlp_in, hidden_one, attn_out, cotangent, pieces, out_b, count, images):
    tokens, width = d_mlp_in.shape
    blocks, _, columns = out_b.shape

    def kernel(in_ref, hidden_ref, attn_ref, cot_ref, piece, *refs):
        w_ref, count_ref, refs = refs[0], refs[1], refs[2:]
        d_hidden_ref, d_mixed_ref, sums_ref = refs[:3]
        d_in = in_ref[...]
        normed, inverse = normal(hidden_ref[...])
        sums_ref[0, 0:1] = jnp.sum(d_in, axis=0, keepdims=True)
        sums_ref[0, 1:2] = jnp.sum(d_in * normed, axis=0, keepdims=True)
        real = (pl.program_id(0) < count_ref[0]).astype(F32)
        grad = cot_ref[...].astype(F32) * real
        d_hidden = grad + normal_back(d_in * (1.0 + piece[0, 4:5, :]), normed, inverse)
        d_hidden_ref[...] = d_hidden
        sums_ref[0, 2:3] = jnp.sum(d_hidden * attn_ref[...], axis=0, keepdims=True)
        d_attn = (piece[0, 2:3, :] * d_hidden).astype(BF)
        d_mixed = None
        for j, out in enumerate(refs[3:]):
            part = d_attn[:, j * columns : (j + 1) * columns]
            out[...] = part
            term = mm(part, w_ref[j], ((1,), (1,)))
            d_mixed = term if d_mixed is None else d_mixed + term
        d_mixed_ref[...] = d_mixed.astype(BF)

    rows = tokens // images
    outs = [(rows, (width,), F32), (rows, (width,), BF), (1, (3, width), F32)]
    outs += [(rows, (columns,), BF)] * blocks
    by_image = [d_mlp_in, hidden_one, attn_out, cotangent, pieces]
    return per_image(kernel, images, by_image, [out_b], outs, 40, "middle_back", count)


def block_head_back(d_packed, d_hidden, inputs, pieces, qkv_b, images):
    tokens, width = d_hidden.shape
    blocks = qkv_b.shape[0]

    def kernel(*refs):
        d_refs, (d_hidden_ref, in_ref, piece) = refs[:blocks], refs[blocks : blocks + 3]
        w_ref, out_ref, sums_ref = refs[blocks + 3 :]
        d_in = None
        for j, d in enumerate(d_refs):
            term = mm(d[...], w_ref[j], ((1,), (1,)))
            d_in = term if d_in is None else d_in + term
        normed, inverse = normal(in_ref[...].astype(F32))
        sums_ref[0, 0:1] = jnp.sum(d_in, axis=0, keepdims=True)
        sums_ref[0, 1:2] = jnp.sum(d_in * normed, axis=0, keepdims=True)
        back = normal_back(d_in * (1.0 + piece[0, 1:2, :]), normed, inverse)
        out_ref[...] = (d_hidden_ref[...] + back).astype(BF)

    outs = [(tokens // images, (width,), BF), (1, (2, width), F32)]
    by_image = [*d_packed, d_hidden, inputs, pieces]
    return per_image(kernel, images, by_image, [qkv_b], outs, 48, "block_head_back")


def grad_stacks(places, a, parts):
    tokens, features = a.shape
    z, count = places.z, places.narrow
    joined = len(parts) < count
    columns = parts[0].shape[1] // (count if joined else 1)
    rows = features // (4 * z)
    chunk = chunk_of(columns, 900)
    masks = [places.masks(0), places.masks(1)]
    total = len(masks[0])

    def kernel(at, a_ref, *refs):
        d_refs, (own_ref, send_ref, turned, product) = refs[:count], refs[count:]

        @pl.when(pl.program_id(0) == 0)
        def _():
            turned[...] = a_ref[...].T

        for i, d_ref in enumerate(d_refs):
            whole = mm(turned[...], d_ref[...], ((1,), (0,)))
            for k in range(4 * z):
                product[i, k] = whole[k * rows : (k + 1) * rows].astype(BF)
        core, y, x = at[0], at[1], at[2]
        for out, owner in ((own_ref, core), (send_ref, 1 - core)):
            for j in range(total):
                dy = jnp.where(owner == 0, masks[0][j][0], masks[1][j][0])
                dx = jnp.where(owner == 0, masks[0][j][1], masks[1][j][1])
                for k in range(z):
                    out[j, k] = product[x ^ dx, (k * 2 + (y ^ dy)) * 2 + owner]

    at = jnp.stack([places.at_c, places.at_y, places.x]).astype(jnp.int32)
    shape = (total, z, rows, columns)
    out = pl.BlockSpec((total, z, rows, chunk), lambda i: (0, 0, 0, i))
    return pl.pallas_call(
        kernel,
        grid=(-(-columns // chunk),),
        out_shape=[jax.ShapeDtypeStruct(shape, BF)] * 2,
        in_specs=[pl.BlockSpec(memory_space=pltpu.SMEM), whole_block(a)]
        + [
            pl.BlockSpec((tokens, chunk), lambda i, j=j: (0, j * (columns // chunk) + i if joined else i))
            for j in range(count)
        ],
        out_specs=[out, out],
        scratch_shapes=[
            pltpu.VMEM((features, tokens), BF),
            pltpu.VMEM((count, 4 * z, rows, chunk), BF),
        ],
        compiler_params=pltpu.CompilerParams(vmem_limit_bytes=56 * 2**20),
        cost_estimate=LONG,
        name="grad_stacks",
    )(at, a, *(parts * count if joined else parts))


class Places:
    def __init__(self):
        self.wide, self.narrow = lax.axis_size("wide"), lax.axis_size("narrow")
        self.z = self.wide // 4
        w = lax.axis_index("wide")
        self.w, self.x = w, lax.axis_index("narrow")
        self.at_z, self.at_y, self.at_c = w // 4, (w // 2) % 2, w % 2
        self.z_bits = [1 << i for i in range(self.z.bit_length() - 1)]
        self.x_bits = [1 << i for i in range(self.narrow.bit_length() - 1)]
        x_masks = [(0, bit) for bit in self.x_bits]
        self.orders = ([(1, 0)] + x_masks, x_masks + [(1, 0)])

    def swap(self, value, flip):
        pairs = []
        for w in range(self.wide):
            for x in range(self.narrow):
                dz, dy, dc, dx = flip(w % 2)
                to = (w // 4 ^ dz) * 4 + (w // 2 % 2 ^ dy) * 2 + (w % 2 ^ dc)
                pairs.append((w * self.narrow + x, to * self.narrow + (x ^ dx)))
        return lax.ppermute(value, ALL, pairs)

    def step_flip(self, i):
        return lambda core: (0, self.orders[core][i][0], 0, self.orders[core][i][1])

    def masks(self, core):
        out = [(0, 0)]
        for dy, dx in self.orders[core]:
            out = out + [(y ^ dy, x ^ dx) for y, x in out]
        return out

    def all_bits(self):
        out = [(0, (bit, 0, 0, 0), self.at_z // bit % 2) for bit in self.z_bits]
        out.append((1, (0, 1, 0, 0), self.at_y))
        out += [(3, (0, 0, 0, bit), self.x // bit % 2) for bit in self.x_bits]
        out.append((2, (0, 0, 1, 0), self.at_c))
        return out

    def open_small(self, value):
        return value[None, None, None, None]

    def gather_bits(self, value, bits):
        for axis, flip, bit in bits:
            other = self.swap(value, lambda core: flip)
            low = jnp.where(bit == 0, value, other)
            high = jnp.where(bit == 0, other, value)
            value = jnp.concatenate([low, high], axis)
        return value

    def add_narrow(self, value):
        for bit in self.x_bits:
            value = value + self.swap(value, lambda core: (0, 0, 0, bit))
        return value

    def scatter_chip_row(self, value):
        value = value.reshape(self.z, 2, 2, *value.shape[1:])
        other = self.swap(take(value, 2, 1 - self.at_c), lambda core: (0, 0, 1, 0))
        value = take(value, 2, self.at_c) + other
        other = self.swap(take(value, 1, 1 - self.at_y), lambda core: (0, 1, 0, 0))
        return take(value, 1, self.at_y) + other

    def scatter_z(self, value):
        for bit in reversed(self.z_bits):
            value = value.reshape(2, bit, *value.shape[1:])
            here = self.at_z // bit % 2
            other = self.swap(take(value, 0, 1 - here), lambda core: (bit, 0, 0, 0))
            value = take(value, 0, here) + other
        return value[0]

    def trade_narrow(self, value):
        if self.narrow != 2:
            return lax.all_to_all(value, "narrow", 0, 0, tiled=True)
        other = self.swap(take(value, 0, 1 - self.x), lambda core: (0, 0, 0, 1))
        own = take(value, 0, self.x)
        return jnp.stack([pick([own, other], self.x), pick([other, own], self.x)])


def pick(parts, index):
    if len(parts) == 1:
        return parts[0]
    if len(parts) == 2:
        return jnp.where(index == 0, parts[0], parts[1])
    return lax.dynamic_index_in_dim(jnp.stack(parts), index, 0, keepdims=False)


def take(value, axis, index):
    return lax.dynamic_index_in_dim(value, index, axis, keepdims=False)


def after(value, *before):
    return lax.optimization_barrier((value,) + before)[0]


def assemble(places, parts):
    half, z, rows, columns = parts[0].shape
    joined = columns % 128 == 0
    masks = [places.masks(0), places.masks(1)]

    def kernel(at, s0, s1, t0, t1, out, held, sem, out_sem):
        core, y, x, here_z = at[0], at[1], at[2], at[3]
        copies = []
        for i, src in enumerate((s0, s1, t0, t1)):
            owner = core ^ (i // 2)
            for j in range(half):
                k = j + half * (i % 2)
                dy = jnp.where(owner == 0, masks[0][k][0], masks[1][k][0])
                dx = jnp.where(owner == 0, masks[0][k][1], masks[1][k][1])
                for d in range(z):
                    if joined:
                        lanes = pl.ds(pl.multiple_of((x ^ dx) * columns, 128), columns)
                        to = held.at[here_z ^ d, y ^ dy, owner, :, lanes]
                    else:
                        to = held.at[x ^ dx, here_z ^ d, y ^ dy, owner]
                    copies.append(pltpu.make_async_copy(src.at[j, d], to, sem.at[len(copies)]))
        for copy in copies:
            copy.start()
        for copy in copies:
            copy.wait()
        whole = pltpu.make_async_copy(held, out, out_sem)
        whole.start()
        whole.wait()

    shape = (places.narrow, z, 2, 2, rows, columns)
    if joined:
        shape = (z, 2, 2, rows, places.narrow * columns)
    at = jnp.stack([places.at_c, places.at_y, places.x, places.at_z]).astype(jnp.int32)
    return pl.pallas_call(
        kernel,
        out_shape=jax.ShapeDtypeStruct(shape, BF),
        in_specs=[pl.BlockSpec(memory_space=pltpu.SMEM)] + [pl.BlockSpec(memory_space=pl.ANY)] * 4,
        out_specs=pl.BlockSpec(memory_space=pl.ANY),
        scratch_shapes=[
            pltpu.VMEM(shape, BF),
            pltpu.SemaphoreType.DMA((4 * half * z,)),
            pltpu.SemaphoreType.DMA,
        ],
        compiler_params=pltpu.CompilerParams(vmem_limit_bytes=24 * 2**20),
        cost_estimate=LONG,
        name="assemble",
    )(at, *parts)


def join(parts):
    counts = [p.shape[0] for p in parts]

    def kernel(*refs):
        first = 0
        for ref, count in zip(refs[:-1], counts):
            refs[-1][first : first + count] = ref[...]
            first += count

    shape = jax.ShapeDtypeStruct((sum(counts), *parts[0].shape[1:]), BF)
    return pl.pallas_call(
        kernel,
        grid=(1,),
        out_shape=shape,
        in_specs=[whole_block(p) for p in parts],
        out_specs=whole_block(shape),
        compiler_params=pltpu.CompilerParams(vmem_limit_bytes=24 * 2**20),
        cost_estimate=LONG,
        name="join",
    )(*parts)


def add_stacks(terms, half):
    shape = (half, *terms[0].shape[1:])

    def kernel(*refs):
        total = refs[0][...].astype(F32)
        for ref in refs[1:-1]:
            total += ref[...].astype(F32)
        refs[-1][...] = total.astype(BF)

    deep = 2 if shape[1] % 2 == 0 else 1
    block = (1, deep, *shape[2:])
    return pl.pallas_call(
        kernel,
        grid=(half, shape[1] // deep),
        out_shape=jax.ShapeDtypeStruct(shape, BF),
        in_specs=[pl.BlockSpec(block, lambda i, j: (half + i, j, 0, 0))] * len(terms),
        out_specs=pl.BlockSpec(block, lambda i, j: (i, j, 0, 0)),
        compiler_params=pltpu.CompilerParams(vmem_limit_bytes=24 * 2**20),
        cost_estimate=LONG,
        name="add_stacks",
    )(*terms)


def add_slabs(places, terms, z_terms, first, count, divisor=None):
    rows, columns = terms[0].shape[2:]
    late = [(at, term) for at, term in z_terms if at <= first < at + term.shape[0]]

    def kernel(at_ref, *refs):
        out, refs = refs[-1], refs[:-1]
        total = None
        for i, ref in enumerate(refs[: len(terms) + len(late)]):
            value = (ref[0, 0] if i < len(terms) else ref[0]).astype(F32)
            total = value if total is None else total + value
        if divisor is not None:
            total = total / refs[-1][0]
        out[0] = total.astype(out.dtype)

    in_specs = [
        pl.BlockSpec((1, 1, rows, columns), lambda i, at: (0, at[0] ^ (first + i), 0, 0))
        for _ in terms
    ]
    in_specs += [
        pl.BlockSpec((1, rows, columns), lambda i, at, f=first - at_first: (f + i, 0, 0))
        for at_first, _ in late
    ]
    args = [*terms, *[term for _, term in late]]
    if divisor is not None:
        in_specs.append(pl.BlockSpec(memory_space=pltpu.SMEM))
        args.append(divisor.reshape(1))
    kind = BF if divisor is None else F32
    return pl.pallas_call(
        kernel,
        grid_spec=pltpu.PrefetchScalarGridSpec(
            num_scalar_prefetch=1,
            grid=(count,),
            in_specs=in_specs,
            out_specs=pl.BlockSpec((1, rows, columns), lambda i, at: (i, 0, 0)),
        ),
        out_shape=jax.ShapeDtypeStruct((count, rows, columns), kind),
        compiler_params=pltpu.CompilerParams(vmem_limit_bytes=24 * 2**20),
        cost_estimate=LONG,
        name="add_slabs",
    )(places.at_z.astype(jnp.int32).reshape(1), *args)


class Slots:
    def __init__(self, places):
        self.places = places
        self.before, self.now, self.ready = (), [], []

    def tie(self, value):
        return after(value, *self.before, *self.ready)

    def note(self, *values):
        self.now += values

    def next(self, *values):
        self.note(*values)
        self.before, self.now, self.ready = tuple(self.now), [], []

    def send(self, value, flip):
        value = after(value, *self.before)
        self.ready.append(value)
        return self.follow(value, flip)

    def follow(self, value, flip):
        other = self.places.swap(value, flip)
        self.note(other)
        return other


class Gather:
    def __init__(self, slots, shard):
        self.slots, self.places = slots, slots.places
        self.rows = self.places.wide * shard.shape[0]
        self.parts = [shard[None]]

    def all_z(self):
        for d in range(1, self.places.z):
            self.parts.append(self.slots.send(self.parts[0], lambda core: (d, 0, 0, 0)))

    def step(self, i, exchange):
        joined = join([p.reshape(-1, *p.shape[-2:]) for p in self.parts])
        self.parts = [joined]
        self.parts.append(exchange(joined, self.places.step_flip(i)))

    def first(self):
        for i in range(len(self.places.orders[0]) - 1):
            self.step(i, self.slots.follow if i else self.slots.send)

    def last(self):
        self.step(len(self.places.orders[0]) - 1, self.slots.send)

    def cores(self):
        parts = [p.reshape(-1, self.places.z, *p.shape[-2:]) for p in self.parts]
        self.parts = parts + [self.slots.send(p, lambda core: (0, 0, 1, 0)) for p in parts]

    def whole(self):
        whole = assemble(self.places, self.slots.tie(tuple(self.parts)))
        return whole.reshape(-1, self.rows, whole.shape[-1])


class Scatter:
    def __init__(self, slots, a, parts):
        self.slots, self.places = slots, slots.places
        stack, self.to_core = grad_stacks(self.places, a, parts)
        self.terms, self.z_terms, self.half = [stack], [], stack.shape[0]

    def cores(self, exchange):
        self.terms.append(exchange(self.to_core, lambda core: (0, 0, 1, 0)))

    def step(self, i, exchange):
        self.half //= 2
        send = add_stacks(self.terms, self.half)
        self.terms.append(exchange(send, self.places.step_flip(i)))

    def first(self):
        self.step(len(self.places.orders[0]) - 1, self.slots.send)

    def last(self):
        for i in reversed(range(len(self.places.orders[0]) - 1)):
            chained = i < len(self.places.orders[0]) - 2
            self.step(i, self.slots.follow if chained else self.slots.send)

    def step_z(self, *bits):
        for i, bit in enumerate(bits):
            exchange = self.slots.follow if i else self.slots.send
            send = add_slabs(self.places, self.terms, self.z_terms, bit, bit)
            self.z_terms.append((0, exchange(send, lambda core: (bit, 0, 0, 0))))

    def direct_z(self):
        for d in reversed(range(1, self.places.z)):
            send = add_slabs(self.places, self.terms, self.z_terms, d, 1)
            self.z_terms.append((0, self.slots.send(send, lambda core: (d, 0, 0, 0))))

    def result(self, divisor):
        return add_slabs(self.places, self.terms, self.z_terms, 0, 1, divisor)[0]


def dot(a, b, dims, out=F32):
    return lax.dot_general(a, b, (dims, ((), ())), preferred_element_type=F32).astype(out)


def split(a, count):
    width = a.shape[1] // count
    return [a[:, n * width : (n + 1) * width] for n in range(count)]


def on_device(
    inputs,
    cotangent,
    class_ids,
    step_ids,
    image_counts,
    w_qkv,
    w_out,
    w_gate,
    w_up,
    w_down,
    ada_weight,
    ada_bias,
    class_table,
    norm_gains,
):
    places = Places()
    wide, narrow, at_w, at_n = places.wide, places.narrow, places.w, places.x
    images, length, width = inputs.shape
    tables, sums = head_tables(length), head_sums()
    gains = jnp.tile(norm_gains, (1, H))
    local_count = image_counts[0]

    tokens = images * length

    def flat(v):
        return v.reshape(tokens, -1)

    def deep(v):
        return v.reshape(images, length, -1)

    t = Slots(places)
    z_low, z_high = places.z_bits[:1], places.z_bits[1:]
    z_down = z_high[::-1]
    qkv, out, gate, up, down = [
        Gather(t, shard) for shard in (w_qkv, w_out, w_gate, w_up, w_down)
    ]

    qkv.all_z()
    small = [class_ids, step_ids, image_counts, ada_bias]
    small = jnp.concatenate([v.astype(F32) for v in small])[None]
    bits = places.all_bits()
    small = places.gather_bits(places.open_small(small), bits)
    small = small.reshape(wide * narrow, -1)
    t.next(small)

    qkv.first()
    out.all_z()
    small = t.tie(small)
    ids = small[:, : 2 * images].reshape(-1, 2, images).transpose(0, 2, 1).reshape(-1, 2)
    ids = ids.astype(jnp.int32)
    real_count = jnp.sum(small[:, 2 * images])
    bias = small[:, 2 * images + 1 :].reshape(-1)
    rows_here, cols_here = class_table.shape
    class_hot = ids[:, :1] - at_n * rows_here == jnp.arange(rows_here, dtype=jnp.int32)[None, :]
    picked = dot(class_hot.astype(BF), class_table, ((1,), (0,)))
    column = at_w * cols_here + jnp.arange(cols_here, dtype=jnp.int32)
    half_width = width // 2
    frequency = jnp.exp(-math.log(10000.0) * (column % half_width).astype(F32) / half_width)
    angles = ids[:, 1:].astype(F32) * frequency[None, :]
    wave = jnp.where(column[None, :] < half_width, jnp.cos(angles), jnp.sin(angles))
    condition = places.add_narrow(picked) + wave
    cond_act = jax.nn.silu(condition).astype(BF)
    t.next(cond_act)

    qkv.last()
    gate.all_z()
    mod_part = dot(t.tie(cond_act), ada_weight, ((1,), (0,)))
    mod_part = places.scatter_chip_row(mod_part.reshape(wide, narrow, images, -1))
    t.next(mod_part, *tables, sums)

    qkv.cores()
    out.first()
    gate.first()
    mod_part = places.trade_narrow(places.scatter_z(t.tie(mod_part)))
    t.next(mod_part)

    out.last()
    gate.last()
    up.all_z()
    qkv_b = qkv.whole()
    modulation = t.tie(mod_part).transpose(1, 0, 2).reshape(images, -1) + bias
    pieces = modulation.reshape(images, 6, width)
    normed, _ = layer_norm(inputs.astype(F32))
    attn_in = flat((normed * (1.0 + pieces[:, 1:2]) + pieces[:, 0:1]).astype(BF))
    t.next(attn_in, qkv_b)

    out.cores()
    gate.cores()
    up.first()
    packed = project(t.tie(attn_in), qkv_b)
    t.next(*packed)

    up.last()
    down.all_z()
    packed = t.tie(packed)
    queries, key_rows, value_rows, mixed = attention_forward(packed, gains, tables, sums, images)
    slot_real = (jnp.arange(images, dtype=jnp.int32) < local_count).astype(F32)
    grad_y = cotangent.astype(F32) * slot_real[:, None, None]
    d_mlp = split(flat((pieces[:, 5:6] * grad_y).astype(BF)), narrow)
    t.next(mixed, *d_mlp)

    up.cores()
    down.first()
    out_b = out.whole()
    attn_out, hidden_one, mlp_in = attention_tail(mixed, out_b, flat(inputs), pieces, images)
    gate_b = gate.whole()[0]
    t.next(mlp_in, gate_b)

    down.last()
    up_b = up.whole()[0]
    gate_val, up_val, hidden_mid = gated(mlp_in, gate_b, up_b)
    t.next(hidden_mid)

    down.cores()
    g_down = Scatter(t, t.tie(hidden_mid), d_mlp)
    t.next(g_down.to_core)

    g_down.cores(t.send)
    down_b = down.whole()
    t.next(down_b)

    g_down.first()
    d_gate, d_up, d_mlp_in = gated_back(t.tie(d_mlp), down_b, gate_val, up_val, gate_b, up_b)
    t.next(d_mlp_in)

    g_down.last()
    g_gate = Scatter(t, mlp_in, [t.tie(d_gate)])
    g_gate.cores(t.follow)
    t.next()

    g_gate.first()
    g_down.step_z(*z_down)
    g_up = Scatter(t, mlp_in, [t.tie(d_up)])
    g_up.cores(t.follow)
    d_hidden, d_mixed, sums_b, *d_attn = middle_back(
        t.tie(d_mlp_in), hidden_one, attn_out, flat(cotangent), pieces, out_b, image_counts, images
    )
    g_out = Scatter(t, mixed, d_attn)
    t.next(g_out.to_core, d_mixed)

    g_gate.last()
    g_up.first()
    g_out.cores(t.send)
    g_down.step_z(*z_low)
    d_packed, gain_terms = attention_backward(
        packed, queries, key_rows, value_rows, t.tie(d_mixed), gains, tables, sums, images
    )
    t.next(*d_packed)

    g_up.last()
    g_out.first()
    g_gate.step_z(*z_down)
    g_qkv = Scatter(t, attn_in, t.tie(d_packed))
    g_qkv.cores(t.follow)
    t.next()

    g_qkv.first()
    g_out.last()
    g_up.step_z(*z_down)
    g_gate.step_z(*z_low)
    d_tokens, sums_a = block_head_back(
        t.tie(d_packed), d_hidden, flat(inputs), pieces, qkv_b, images
    )
    block_output, sums_gate = block_tail(
        t.tie(hidden_mid), down_b, hidden_one, flat(cotangent), pieces, image_counts, images
    )
    grad_gains = gain_terms.sum(0).reshape(2, H, HD).sum(1).reshape(1, -1)
    gains_high = grad_gains.astype(BF)
    gains_low = (grad_gains - gains_high.astype(F32)).astype(BF)
    rest = jnp.zeros((images - 2, 2 * HD), BF)
    grad_gains = jnp.concatenate([gains_high, gains_low, rest], axis=0)
    d_modulation = jnp.concatenate([sums_a, sums_b[:, 2:], sums_b[:, :2], sums_gate], axis=1)
    d_modulation = d_modulation.astype(BF).reshape(images, -1)
    rest = jnp.zeros((images, 65 * 128 - 6 * width - 2 * HD), BF)
    d_modulation = jnp.concatenate([d_modulation, grad_gains, rest], axis=1)
    t.next(d_modulation)

    g_qkv.last()
    g_up.step_z(*z_low)
    g_out.step_z(*z_down)
    d_all = lax.all_gather(t.tie(d_modulation), ALL, axis=0, tiled=True)
    t.next()

    g_qkv.direct_z()
    g_out.step_z(*z_low)
    gain_sum = d_all[:, 6 * width : 6 * width + 2 * HD].astype(F32)
    gain_sum = jnp.sum(gain_sum, axis=0).reshape(2, HD) / real_count
    d_mod = d_all[:, : 6 * width]
    ada_cols = ada_weight.shape[1]
    d_mod_here = lax.dynamic_slice_in_dim(d_mod, at_n * ada_cols, ada_cols, 1)
    g_ada = dot(cond_act, d_mod_here, ((0,), (0,))) / real_count
    bias_cols = ada_bias.shape[0]
    bias_at = (at_w * narrow + at_n) * bias_cols
    g_bias = jnp.sum(lax.dynamic_slice_in_dim(d_mod, bias_at, bias_cols, 1).astype(F32), axis=0)
    g_bias = g_bias / real_count
    d_cond_act = places.add_narrow(dot(d_mod_here, ada_weight, ((1,), (1,))))
    cond_sigmoid = jax.nn.sigmoid(condition)
    d_condition = d_cond_act * cond_sigmoid * (1.0 + condition * (1.0 - cond_sigmoid))
    g_table = jnp.dot(class_hot.astype(F32).T, d_condition, precision=HIGHEST) / real_count
    r_out, r_gate, r_up, r_down = [g.result(real_count) for g in (g_out, g_gate, g_up, g_down)]
    at, late = g_qkv.z_terms[-1]
    g_qkv.z_terms[-1] = (at, after(late, g_ada, g_table, r_out, r_gate, r_up, r_down))
    r_qkv = g_qkv.result(real_count)

    return (
        deep(block_output),
        deep(d_tokens),
        r_qkv,
        r_out,
        r_gate,
        r_up,
        r_down,
        g_ada,
        g_bias,
        g_table,
        gain_sum,
    )


def solution(mesh):
    split = P("wide", "narrow")
    images = P(ALL, None, None)
    return jax.shard_map(
        on_device,
        mesh=mesh,
        in_specs=(
            images,
            images,
            P(ALL),
            P(ALL),
            P(ALL),
            split,
            split,
            split,
            split,
            split,
            split,
            P(ALL),
            P("narrow", "wide"),
            P(),
        ),
        out_specs=(
            images,
            images,
            split,
            split,
            split,
            split,
            split,
            split,
            P(ALL),
            P("narrow", "wide"),
            P(),
        ),
        check_vma=False,
    )
```

```python
import math

import jax
import jax.numpy as jnp
from jax import lax
from jax.experimental import pallas as pl
from jax.experimental.pallas import tpu as pltpu
from jax.sharding import PartitionSpec as P

H = 16
HD = 72
CLASSES = 1000
GRID = 16

EPSILON = 1e-06
HIGHEST = lax.Precision.HIGHEST
ALL = ("wide", "narrow")
BF = jnp.bfloat16
F32 = jnp.float32
LONG = pl.CostEstimate(flops=10**12, bytes_accessed=1, transcendentals=0)
SHORT = pl.CostEstimate(flops=1, bytes_accessed=1, transcendentals=0)


def layer_norm(values):
    centre = values - jnp.mean(values, axis=-1, keepdims=True)
    inverse = lax.rsqrt(jnp.mean(centre * centre, axis=-1, keepdims=True) + EPSILON)
    return (centre * inverse, inverse)


def head_tables(length):
    quarter = HD // 4
    lane = jnp.arange(H * HD, dtype=jnp.int32) % HD
    frequency = 10000.0 ** (-(lane % quarter).astype(F32) / quarter)
    patch = jnp.arange(length, dtype=jnp.int32)[:, None]
    place = jnp.where(lane[None, :] < 2 * quarter, patch // GRID, patch % GRID)
    angles = place.astype(F32) * frequency[None, :]
    cosine, sine = jnp.cos(angles), jnp.sin(angles)
    first = (lane // quarter % 2 == 0)[None, :]
    return [cosine, jnp.where(first, -sine, 0.0), jnp.where(first, 0.0, sine)]


def head_sums():
    lane = lax.broadcasted_iota(jnp.int32, (H * HD, 128), 0) // HD
    return (lane == lax.broadcasted_iota(jnp.int32, (H * HD, 128), 1)).astype(BF)


def exact_dot(a, b, dims):
    total = None
    for _ in range(3):
        term = a.astype(BF)
        a = a - term.astype(F32)
        part = lax.dot_general(term, b, (dims, ((), ())), preferred_element_type=F32)
        total = part if total is None else total + part
    return total


def head_mean(values, sums):
    mean = exact_dot(values, sums, ((1,), (0,))) * (1.0 / HD)
    return exact_dot(mean, sums, ((1,), (1,)))


def shifted(values, cosine, above, below, sign):
    quarter, width = HD // 4, values.shape[1]
    up = pltpu.roll(values, width - quarter, 1)
    down = pltpu.roll(values, quarter, 1)
    return values * cosine + sign * (up * above + down * below)


def window(head):
    first, last = head * HD // 128 * 128, ((head + 1) * HD + 127) // 128 * 128
    return first, last


def only(values, head):
    first, last = window(head)
    part = values[:, first:last]
    lane = first + lax.broadcasted_iota(jnp.int32, (1, last - first), 1)
    mine = ((lane >= head * HD) & (lane < (head + 1) * HD)).astype(values.dtype)
    return part * mine


class Tiles:
    def __init__(self, store):
        self.store, self.held = store, {}

    def add(self, head, value):
        first, last = window(head)
        for tile in range(first // 128, last // 128):
            part = value[:, tile * 128 - first : tile * 128 - first + 128]
            self.held[tile] = self.held[tile] + part if tile in self.held else part
        done = (head + 1) * HD // 128
        for tile in sorted(self.held):
            if tile < done or head == H - 1:
                self.store(tile * 128, self.held.pop(tile))


def mm(a, b, dims):
    return lax.dot_general(a, b, (dims, ((), ())), preferred_element_type=F32)


def only_turned(values, head):
    first, last = window(head)
    part = values[first:last, :]
    row = first + lax.broadcasted_iota(jnp.int32, (last - first, 1), 0)
    mine = ((row >= head * HD) & (row < (head + 1) * HD)).astype(values.dtype)
    return part * mine


def softmax_of(queries, keys_turned, head):
    first, last = window(head)
    scores = mm(only(queries, head), keys_turned[first:last, :], ((1,), (0,))) * (HD ** (-0.5))
    exponent = jnp.exp(scores - jnp.max(scores, axis=1, keepdims=True))
    return exponent / jnp.sum(exponent, axis=1, keepdims=True)


def attention_forward(packed, gains, tables, sums, images):
    tokens = packed[0].shape[0]
    length, width, blocks = tokens // images, H * HD, len(packed)

    def kernel(*refs):
        parts, refs = refs[:blocks], refs[blocks:]
        gain, cosine, above, below, sums_ref, q_ref, k_ref, v_ref, mixed_ref, k_turned = refs
        whole = jnp.concatenate([p[...] for p in parts], axis=1)
        sums_here = sums_ref[...]
        for i, ref in enumerate((q_ref, k_ref)):
            raw = whole[:, i * width : (i + 1) * width]
            normed = raw * lax.rsqrt(head_mean(raw * raw, sums_here) + EPSILON)
            turned = shifted(normed * gain[i : i + 1, :], cosine[...], above[...], below[...], 1.0)
            ref[...] = turned.astype(BF)
        v_ref[...] = whole[:, 2 * width :].astype(BF)

        def store(first, value):
            mixed_ref[:, first : first + 128] = value.astype(BF)

        k_turned[...] = k_ref[...].T
        mixed = Tiles(store)
        for head in range(H):
            attention = softmax_of(q_ref, k_turned, head).astype(BF)
            mixed.add(head, mm(attention, only(v_ref, head), ((1,), (0,))))

    def rows(n):
        return pl.BlockSpec((length, n), lambda i: (i, 0))

    def all_of(a):
        return pl.BlockSpec(a.shape, lambda i: (0, 0))

    out = jax.ShapeDtypeStruct((tokens, width), BF)
    return pl.pallas_call(
        kernel,
        grid=(images,),
        out_shape=[out] * 4,
        in_specs=[rows(p.shape[1]) for p in packed] + [all_of(a) for a in (gains, *tables, sums)],
        out_specs=[rows(width)] * 4,
        scratch_shapes=[pltpu.VMEM((width, length), BF)],
        compiler_params=pltpu.CompilerParams(vmem_limit_bytes=60 * 2**20),
        cost_estimate=LONG,
        name="attention_forward",
    )(*packed, gains, *tables, sums)


def attention_backward(packed, queries, keys, values, d_mixed, gains, tables, sums, images):
    tokens = queries.shape[0]
    length, width, blocks = tokens // images, H * HD, len(packed)
    block = packed[0].shape[1]

    def kernel(*refs):
        parts, refs = refs[:blocks], refs[blocks:]
        q_ref, k_ref, v_ref, d_ref, gain, cosine, above, below, sums_ref = refs[:9]
        outs, refs = refs[9 : 9 + blocks], refs[9 + blocks :]
        gain_ref, d_q_turned, d_k, d_v, q_turned, k_turned, d_turned = refs

        def store_to(ref):
            def store(first, value):
                ref[:, first : first + 128] = value

            return store

        for ref, turned in ((q_ref, q_turned), (k_ref, k_turned), (d_ref, d_turned)):
            turned[...] = ref[...].T
        all_k, all_v = [Tiles(store_to(ref)) for ref in (d_k, d_v)]
        rows_q = {}
        for head in range(H):
            first, last = window(head)
            scores = mm(only(k_ref, head), q_turned[first:last, :], ((1,), (0,))) * (HD ** (-0.5))
            exponent = jnp.exp(scores - jnp.max(scores, axis=0, keepdims=True))
            soft = exponent / jnp.sum(exponent, axis=0, keepdims=True)
            all_v.add(head, mm(soft.astype(BF), only(d_ref, head), ((1,), (0,))))
            d_soft = mm(only(v_ref, head), d_turned[first:last, :], ((1,), (0,)))
            inner = jnp.sum(soft * d_soft, axis=0, keepdims=True)
            d_scores = (soft * (d_soft - inner) * (HD ** (-0.5))).astype(BF)
            all_k.add(head, mm(d_scores, only(q_ref, head), ((1,), (0,))))
            part = mm(only_turned(k_turned, head), d_scores, ((1,), (0,)))
            for tile in range(first // 128, last // 128):
                rows = part[tile * 128 - first : tile * 128 - first + 128]
                rows_q[tile] = rows_q[tile] + rows if tile in rows_q else rows
            for tile in sorted(rows_q):
                if tile < (head + 1) * HD // 128 or head == H - 1:
                    d_q_turned[tile * 128 : tile * 128 + 128, :] = rows_q.pop(tile)
        whole = jnp.concatenate([p[...] for p in parts], axis=1)
        sums_here = sums_ref[...]
        done = []
        for i, value in enumerate((d_q_turned[...].T, d_k[...])):
            raw = whole[:, i * width : (i + 1) * width]
            inverse = lax.rsqrt(head_mean(raw * raw, sums_here) + EPSILON)
            normed = raw * inverse
            scaled = shifted(value, cosine[...], above[...], below[...], -1.0)
            gain_ref[0, i : i + 1, :] = jnp.sum(scaled * normed, axis=0, keepdims=True)
            incoming = scaled * gain[i : i + 1, :]
            mean = head_mean(incoming * normed, sums_here)
            done.append((inverse * (incoming - normed * mean)).astype(BF))
        done.append(d_v[...].astype(BF))
        done = jnp.concatenate(done, axis=1)
        for j, out in enumerate(outs):
            out[...] = done[:, j * block : (j + 1) * block]

    def rows(n):
        return pl.BlockSpec((length, n), lambda i: (i, 0))

    def all_of(a):
        return pl.BlockSpec(a.shape, lambda i: (0, 0))

    outs = pl.pallas_call(
        kernel,
        grid=(images,),
        out_shape=[jax.ShapeDtypeStruct((tokens, block), BF)] * blocks
        + [jax.ShapeDtypeStruct((images, 2, width), F32)],
        in_specs=[rows(block)] * blocks
        + [rows(width)] * 4
        + [all_of(a) for a in (gains, *tables, sums)],
        out_specs=[rows(block)] * blocks + [pl.BlockSpec((1, 2, width), lambda i: (i, 0, 0))],
        scratch_shapes=[pltpu.VMEM((width, length), F32)]
        + [pltpu.VMEM((length, width), F32)] * 2
        + [pltpu.VMEM((width, length), BF)] * 3,
        compiler_params=pltpu.CompilerParams(vmem_limit_bytes=60 * 2**20),
        cost_estimate=LONG,
        name="attention_backward",
    )(*packed, queries, keys, values, d_mixed, gains, *tables, sums)
    return outs[:blocks], outs[blocks]

def whole_block(a):
    return pl.BlockSpec(a.shape, lambda *i: (0,) * a.ndim)


def chunk_of(columns, most):
    count = -(-columns // most)
    return columns if count == 1 else -(-columns // (128 * count)) * 128


def project(a, blocks):
    tokens, depth = a.shape
    count, _, columns = blocks.shape
    chunk = chunk_of(columns, 640)

    def kernel(a_ref, *refs):
        for w_ref, out_ref in zip(refs[:count], refs[count:]):
            out_ref[...] = mm(a_ref[...], w_ref[...], ((1,), (0,)))

    return pl.pallas_call(
        kernel,
        grid=(-(-columns // chunk),),
        out_shape=[jax.ShapeDtypeStruct((tokens, columns), F32)] * count,
        in_specs=[whole_block(a)]
        + [pl.BlockSpec((None, depth, chunk), lambda i, j=j: (j, 0, i)) for j in range(count)],
        out_specs=[pl.BlockSpec((tokens, chunk), lambda i: (0, i))] * count,
        compiler_params=pltpu.CompilerParams(vmem_limit_bytes=60 * 2**20),
        cost_estimate=LONG,
        name="project",
    )(a, *[blocks] * count)


def gated(a, w_gate, w_up):
    tokens, depth = a.shape
    columns = w_gate.shape[1]
    chunk = 512

    def kernel(a_ref, g_ref, u_ref, gate_ref, up_ref, mid_ref):
        gate = mm(a_ref[...], g_ref[...], ((1,), (0,)))
        up = mm(a_ref[...], u_ref[...], ((1,), (0,)))
        gate_ref[...] = gate
        up_ref[...] = up
        mid_ref[...] = (gate * jax.nn.sigmoid(gate) * up).astype(BF)

    weight = pl.BlockSpec((depth, chunk), lambda i: (0, i))
    out = pl.BlockSpec((tokens, chunk), lambda i: (0, i))
    return pl.pallas_call(
        kernel,
        grid=(columns // chunk,),
        out_shape=[jax.ShapeDtypeStruct((tokens, columns), t) for t in (F32, F32, BF)],
        in_specs=[whole_block(a), weight, weight],
        out_specs=[out] * 3,
        compiler_params=pltpu.CompilerParams(vmem_limit_bytes=60 * 2**20),
        cost_estimate=LONG,
        name="gated",
    )(a, w_gate, w_up)


def gated_back(d_parts, down, gate_val, up_val, w_gate, w_up):
    tokens, columns = gate_val.shape
    depth, count, chunk = w_gate.shape[0], down.shape[0], 512

    def kernel(*refs):
        d_refs, w_refs, refs = refs[:count], refs[count : 2 * count], refs[2 * count :]
        gate_ref, up_ref, g_ref, u_ref, d_gate_ref, d_up_ref, in_ref = refs
        d_mid = None
        for d_ref, w_ref in zip(d_refs, w_refs):
            term = mm(d_ref[...], w_ref[...], ((1,), (1,)))
            d_mid = term if d_mid is None else d_mid + term
        gate, up = gate_ref[...], up_ref[...]
        sigmoid = jax.nn.sigmoid(gate)
        silu = gate * sigmoid
        d_gate = (d_mid * up * (sigmoid + silu * (1.0 - sigmoid))).astype(BF)
        d_up = (d_mid * silu).astype(BF)
        d_gate_ref[...] = d_gate
        d_up_ref[...] = d_up
        term = mm(d_gate, g_ref[...], ((1,), (1,))) + mm(d_up, u_ref[...], ((1,), (1,)))

        @pl.when(pl.program_id(0) == 0)
        def _():
            in_ref[...] = term

        @pl.when(pl.program_id(0) > 0)
        def _():
            in_ref[...] += term

    width = down.shape[2]
    token = pl.BlockSpec((tokens, chunk), lambda i: (0, i))
    weight = pl.BlockSpec((depth, chunk), lambda i: (0, i))
    return pl.pallas_call(
        kernel,
        grid=(columns // chunk,),
        out_shape=[jax.ShapeDtypeStruct((tokens, columns), BF)] * 2
        + [jax.ShapeDtypeStruct((tokens, depth), F32)],
        in_specs=[whole_block(d) for d in d_parts]
        + [pl.BlockSpec((None, chunk, width), lambda i, j=j: (j, i, 0)) for j in range(count)]
        + [token, token, weight, weight],
        out_specs=[token, token, pl.BlockSpec((tokens, depth), lambda i: (0, 0))],
        compiler_params=pltpu.CompilerParams(vmem_limit_bytes=60 * 2**20),
        cost_estimate=LONG,
        name="gated_back",
    )(*d_parts, *[down] * count, gate_val, up_val, w_gate, w_up)


def normal(values):
    centre = values - jnp.mean(values, axis=1, keepdims=True)
    inverse = lax.rsqrt(jnp.mean(centre * centre, axis=1, keepdims=True) + EPSILON)
    return centre * inverse, inverse


def normal_back(gradient, normed, inverse):
    mean = jnp.mean(gradient, axis=1, keepdims=True)
    return inverse * (
        gradient - mean - normed * jnp.mean(gradient * normed, axis=1, keepdims=True)
    )


def per_image(kernel, images, by_image, whole, outs, vmem, name, scalar=None):
    def spec(rows, rest):
        return pl.BlockSpec((rows, *rest), lambda i: (i,) + (0,) * len(rest))

    in_specs = [spec(a.shape[0] // images, a.shape[1:]) for a in by_image]
    in_specs += [whole_block(a) for a in whole]
    args = [*by_image, *whole]
    if scalar is not None:
        in_specs.append(pl.BlockSpec(memory_space=pltpu.SMEM))
        args.append(scalar)
    return pl.pallas_call(
        kernel,
        grid=(images,),
        out_shape=[jax.ShapeDtypeStruct((images * rows, *rest), t) for rows, rest, t in outs],
        in_specs=in_specs,
        out_specs=[spec(rows, rest) for rows, rest, _ in outs],
        compiler_params=pltpu.CompilerParams(vmem_limit_bytes=60 * 2**20),
        cost_estimate=LONG,
        name=name,
    )(*args)


def attention_tail(mixed, out_b, inputs, pieces, images):
    tokens, width = mixed.shape

    def kernel(mixed_ref, in_ref, piece, *refs):
        w_ref, attn_ref, hidden_ref, mlp_ref = refs
        attn = [mm(mixed_ref[...], w_ref[j], ((1,), (0,))) for j in range(out_b.shape[0])]
        attn = jnp.concatenate(attn, axis=1)
        attn_ref[...] = attn
        hidden = in_ref[...].astype(F32) + piece[0, 2:3, :] * attn
        hidden_ref[...] = hidden
        normed, _ = normal(hidden)
        mlp_ref[...] = (normed * (1.0 + piece[0, 4:5, :]) + piece[0, 3:4, :]).astype(BF)

    rows = tokens // images
    outs = [(rows, (width,), F32), (rows, (width,), F32), (rows, (width,), BF)]
    return per_image(kernel, images, [mixed, inputs, pieces], [out_b], outs, 32, "attention_tail")


def block_tail(hidden_mid, down_b, hidden_one, cotangent, pieces, count, images):
    tokens, width = hidden_one.shape

    def kernel(mid_ref, hidden_ref, cot_ref, piece, *refs):
        w_ref, count_ref, out_ref, gate_ref = refs
        mlp = [mm(mid_ref[...], w_ref[j], ((1,), (0,))) for j in range(down_b.shape[0])]
        mlp = jnp.concatenate(mlp, axis=1)
        out_ref[...] = (hidden_ref[...] + piece[0, 5:6, :] * mlp).astype(BF)
        real = (pl.program_id(0) < count_ref[0]).astype(F32)
        grad = cot_ref[...].astype(F32) * real
        gate_ref[0] = jnp.sum(grad * mlp, axis=0, keepdims=True)

    rows = tokens // images
    outs = [(rows, (width,), BF), (1, (1, width), F32)]
    by_image = [hidden_mid, hidden_one, cotangent, pieces]
    return per_image(kernel, images, by_image, [down_b], outs, 40, "block_tail", count)


def middle_back(d_mlp_in, hidden_one, attn_out, cotangent, pieces, out_b, count, images):
    tokens, width = d_mlp_in.shape
    blocks, _, columns = out_b.shape

    def kernel(in_ref, hidden_ref, attn_ref, cot_ref, piece, *refs):
        w_ref, count_ref, refs = refs[0], refs[1], refs[2:]
        d_hidden_ref, d_mixed_ref, sums_ref = refs[:3]
        d_in = in_ref[...]
        normed, inverse = normal(hidden_ref[...])
        sums_ref[0, 0:1] = jnp.sum(d_in, axis=0, keepdims=True)
        sums_ref[0, 1:2] = jnp.sum(d_in * normed, axis=0, keepdims=True)
        real = (pl.program_id(0) < count_ref[0]).astype(F32)
        grad = cot_ref[...].astype(F32) * real
        d_hidden = grad + normal_back(d_in * (1.0 + piece[0, 4:5, :]), normed, inverse)
        d_hidden_ref[...] = d_hidden
        sums_ref[0, 2:3] = jnp.sum(d_hidden * attn_ref[...], axis=0, keepdims=True)
        d_attn = (piece[0, 2:3, :] * d_hidden).astype(BF)
        d_mixed = None
        for j, out in enumerate(refs[3:]):
            part = d_attn[:, j * columns : (j + 1) * columns]
            out[...] = part
            term = mm(part, w_ref[j], ((1,), (1,)))
            d_mixed = term if d_mixed is None else d_mixed + term
        d_mixed_ref[...] = d_mixed.astype(BF)

    rows = tokens // images
    outs = [(rows, (width,), F32), (rows, (width,), BF), (1, (3, width), F32)]
    outs += [(rows, (columns,), BF)] * blocks
    by_image = [d_mlp_in, hidden_one, attn_out, cotangent, pieces]
    return per_image(kernel, images, by_image, [out_b], outs, 40, "middle_back", count)


def block_head_back(d_packed, d_hidden, inputs, pieces, qkv_b, images):
    tokens, width = d_hidden.shape
    blocks = qkv_b.shape[0]

    def kernel(*refs):
        d_refs, (d_hidden_ref, in_ref, piece) = refs[:blocks], refs[blocks : blocks + 3]
        w_ref, out_ref, sums_ref = refs[blocks + 3 :]
        d_in = None
        for j, d in enumerate(d_refs):
            term = mm(d[...], w_ref[j], ((1,), (1,)))
            d_in = term if d_in is None else d_in + term
        normed, inverse = normal(in_ref[...].astype(F32))
        sums_ref[0, 0:1] = jnp.sum(d_in, axis=0, keepdims=True)
        sums_ref[0, 1:2] = jnp.sum(d_in * normed, axis=0, keepdims=True)
        back = normal_back(d_in * (1.0 + piece[0, 1:2, :]), normed, inverse)
        out_ref[...] = (d_hidden_ref[...] + back).astype(BF)

    outs = [(tokens // images, (width,), BF), (1, (2, width), F32)]
    by_image = [*d_packed, d_hidden, inputs, pieces]
    return per_image(kernel, images, by_image, [qkv_b], outs, 48, "block_head_back")


def grad_stacks(places, a, parts):
    tokens, features = a.shape
    z, count = places.z, places.narrow
    joined = len(parts) < count
    columns = parts[0].shape[1] // (count if joined else 1)
    rows = features // (4 * z)
    chunk = chunk_of(columns, 900)
    masks = [places.masks(0), places.masks(1)]
    total = len(masks[0])

    def kernel(at, a_ref, *refs):
        d_refs, (own_ref, send_ref, turned, product) = refs[:count], refs[count:]

        @pl.when(pl.program_id(0) == 0)
        def _():
            turned[...] = a_ref[...].T

        for i, d_ref in enumerate(d_refs):
            whole = mm(turned[...], d_ref[...], ((1,), (0,)))
            for k in range(4 * z):
                product[i, k] = whole[k * rows : (k + 1) * rows].astype(BF)
        core, y, x = at[0], at[1], at[2]
        for out, owner in ((own_ref, core), (send_ref, 1 - core)):
            for j in range(total):
                dy = jnp.where(owner == 0, masks[0][j][0], masks[1][j][0])
                dx = jnp.where(owner == 0, masks[0][j][1], masks[1][j][1])
                for k in range(z):
                    out[j, k] = product[x ^ dx, (k * 2 + (y ^ dy)) * 2 + owner]

    at = jnp.stack([places.at_c, places.at_y, places.x]).astype(jnp.int32)
    shape = (total, z, rows, columns)
    out = pl.BlockSpec((total, z, rows, chunk), lambda i: (0, 0, 0, i))
    return pl.pallas_call(
        kernel,
        grid=(-(-columns // chunk),),
        out_shape=[jax.ShapeDtypeStruct(shape, BF)] * 2,
        in_specs=[pl.BlockSpec(memory_space=pltpu.SMEM), whole_block(a)]
        + [
            pl.BlockSpec((tokens, chunk), lambda i, j=j: (0, j * (columns // chunk) + i if joined else i))
            for j in range(count)
        ],
        out_specs=[out, out],
        scratch_shapes=[
            pltpu.VMEM((features, tokens), BF),
            pltpu.VMEM((count, 4 * z, rows, chunk), BF),
        ],
        compiler_params=pltpu.CompilerParams(vmem_limit_bytes=60 * 2**20),
        cost_estimate=LONG,
        name="grad_stacks",
    )(at, a, *(parts * count if joined else parts))


class Places:
    def __init__(self):
        self.wide, self.narrow = lax.axis_size("wide"), lax.axis_size("narrow")
        self.z = self.wide // 4
        w = lax.axis_index("wide")
        self.w, self.x = w, lax.axis_index("narrow")
        self.at_z, self.at_y, self.at_c = w // 4, (w // 2) % 2, w % 2
        self.z_bits = [1 << i for i in range(self.z.bit_length() - 1)]
        self.x_bits = [1 << i for i in range(self.narrow.bit_length() - 1)]
        x_masks = [(0, bit) for bit in self.x_bits]
        self.orders = ([(1, 0)] + x_masks, x_masks + [(1, 0)])

    def swap(self, value, flip):
        pairs = []
        for w in range(self.wide):
            for x in range(self.narrow):
                dz, dy, dc, dx = flip(w % 2)
                to = (w // 4 ^ dz) * 4 + (w // 2 % 2 ^ dy) * 2 + (w % 2 ^ dc)
                pairs.append((w * self.narrow + x, to * self.narrow + (x ^ dx)))
        return lax.ppermute(value, ALL, pairs)

    def step_flip(self, i):
        return lambda core: (0, self.orders[core][i][0], 0, self.orders[core][i][1])

    def masks(self, core):
        out = [(0, 0)]
        for dy, dx in self.orders[core]:
            out = out + [(y ^ dy, x ^ dx) for y, x in out]
        return out

    def all_bits(self):
        out = [(0, (bit, 0, 0, 0), self.at_z // bit % 2) for bit in self.z_bits]
        out.append((1, (0, 1, 0, 0), self.at_y))
        out += [(3, (0, 0, 0, bit), self.x // bit % 2) for bit in self.x_bits]
        out.append((2, (0, 0, 1, 0), self.at_c))
        return out

    def open_small(self, value):
        return value[None, None, None, None]

    def gather_bits(self, value, bits):
        for axis, flip, bit in bits:
            other = self.swap(value, lambda core: flip)
            low = jnp.where(bit == 0, value, other)
            high = jnp.where(bit == 0, other, value)
            value = jnp.concatenate([low, high], axis)
        return value

    def add_narrow(self, value):
        for bit in self.x_bits:
            value = value + self.swap(value, lambda core: (0, 0, 0, bit))
        return value

    def scatter_chip_row(self, value):
        value = value.reshape(self.z, 2, 2, *value.shape[1:])
        other = self.swap(take(value, 2, 1 - self.at_c), lambda core: (0, 0, 1, 0))
        value = take(value, 2, self.at_c) + other
        other = self.swap(take(value, 1, 1 - self.at_y), lambda core: (0, 1, 0, 0))
        return take(value, 1, self.at_y) + other

    def scatter_z(self, value):
        for bit in reversed(self.z_bits):
            value = value.reshape(2, bit, *value.shape[1:])
            here = self.at_z // bit % 2
            other = self.swap(take(value, 0, 1 - here), lambda core: (bit, 0, 0, 0))
            value = take(value, 0, here) + other
        return value[0]

    def trade_narrow(self, value):
        if self.narrow != 2:
            return lax.all_to_all(value, "narrow", 0, 0, tiled=True)
        other = self.swap(take(value, 0, 1 - self.x), lambda core: (0, 0, 0, 1))
        own = take(value, 0, self.x)
        return jnp.stack([pick([own, other], self.x), pick([other, own], self.x)])


def pick(parts, index):
    if len(parts) == 1:
        return parts[0]
    if len(parts) == 2:
        return jnp.where(index == 0, parts[0], parts[1])
    return lax.dynamic_index_in_dim(jnp.stack(parts), index, 0, keepdims=False)


def take(value, axis, index):
    return lax.dynamic_index_in_dim(value, index, axis, keepdims=False)


def after(value, *before):
    return lax.optimization_barrier((value,) + before)[0]


def assemble(places, parts):
    half, z, rows, columns = parts[0].shape
    joined = columns % 128 == 0
    masks = [places.masks(0), places.masks(1)]

    def kernel(at, s0, s1, t0, t1, out, held, sem, out_sem):
        core, y, x, here_z = at[0], at[1], at[2], at[3]
        copies = []
        for i, src in enumerate((s0, s1, t0, t1)):
            owner = core ^ (i // 2)
            for j in range(half):
                k = j + half * (i % 2)
                dy = jnp.where(owner == 0, masks[0][k][0], masks[1][k][0])
                dx = jnp.where(owner == 0, masks[0][k][1], masks[1][k][1])
                for d in range(z):
                    if joined:
                        lanes = pl.ds(pl.multiple_of((x ^ dx) * columns, 128), columns)
                        to = held.at[here_z ^ d, y ^ dy, owner, :, lanes]
                    else:
                        to = held.at[x ^ dx, here_z ^ d, y ^ dy, owner]
                    copies.append(pltpu.make_async_copy(src.at[j, d], to, sem.at[len(copies)]))
        for copy in copies:
            copy.start()
        for copy in copies:
            copy.wait()
        whole = pltpu.make_async_copy(held, out, out_sem)
        whole.start()
        whole.wait()

    shape = (places.narrow, z, 2, 2, rows, columns)
    if joined:
        shape = (z, 2, 2, rows, places.narrow * columns)
    at = jnp.stack([places.at_c, places.at_y, places.x, places.at_z]).astype(jnp.int32)
    return pl.pallas_call(
        kernel,
        out_shape=jax.ShapeDtypeStruct(shape, BF),
        in_specs=[pl.BlockSpec(memory_space=pltpu.SMEM)] + [pl.BlockSpec(memory_space=pl.ANY)] * 4,
        out_specs=pl.BlockSpec(memory_space=pl.ANY),
        scratch_shapes=[
            pltpu.VMEM(shape, BF),
            pltpu.SemaphoreType.DMA((4 * half * z,)),
            pltpu.SemaphoreType.DMA,
        ],
        compiler_params=pltpu.CompilerParams(vmem_limit_bytes=60 * 2**20),
        cost_estimate=LONG,
        name="assemble",
    )(at, *parts)


def join(parts):
    counts = [p.shape[0] for p in parts]

    def kernel(*refs):
        first = 0
        for ref, count in zip(refs[:-1], counts):
            refs[-1][first : first + count] = ref[...]
            first += count

    shape = jax.ShapeDtypeStruct((sum(counts), *parts[0].shape[1:]), BF)
    return pl.pallas_call(
        kernel,
        grid=(1,),
        out_shape=shape,
        in_specs=[whole_block(p) for p in parts],
        out_specs=whole_block(shape),
        compiler_params=pltpu.CompilerParams(vmem_limit_bytes=60 * 2**20),
        cost_estimate=SHORT,
        name="join",
    )(*parts)


def add_stacks(terms, half):
    shape = (half, *terms[0].shape[1:])

    def kernel(*refs):
        total = refs[0][...].astype(F32)
        for ref in refs[1:-1]:
            total += ref[...].astype(F32)
        refs[-1][...] = total.astype(BF)

    deep = 2 if shape[1] % 2 == 0 else 1
    block = (1, deep, *shape[2:])
    return pl.pallas_call(
        kernel,
        grid=(half, shape[1] // deep),
        out_shape=jax.ShapeDtypeStruct(shape, BF),
        in_specs=[pl.BlockSpec(block, lambda i, j: (half + i, j, 0, 0))] * len(terms),
        out_specs=pl.BlockSpec(block, lambda i, j: (i, j, 0, 0)),
        compiler_params=pltpu.CompilerParams(vmem_limit_bytes=60 * 2**20),
        cost_estimate=SHORT,
        name="add_stacks",
    )(*terms)


def add_slabs(places, terms, z_terms, first, count, divisor=None):
    rows, columns = terms[0].shape[2:]
    late = [(at, term) for at, term in z_terms if at <= first < at + term.shape[0]]

    def kernel(at_ref, *refs):
        out, refs = refs[-1], refs[:-1]
        total = None
        for i, ref in enumerate(refs[: len(terms) + len(late)]):
            value = (ref[0, 0] if i < len(terms) else ref[0]).astype(F32)
            total = value if total is None else total + value
        if divisor is not None:
            total = total / refs[-1][0]
        out[0] = total.astype(out.dtype)

    in_specs = [
        pl.BlockSpec((1, 1, rows, columns), lambda i, at: (0, at[0] ^ (first + i), 0, 0))
        for _ in terms
    ]
    in_specs += [
        pl.BlockSpec((1, rows, columns), lambda i, at, f=first - at_first: (f + i, 0, 0))
        for at_first, _ in late
    ]
    args = [*terms, *[term for _, term in late]]
    if divisor is not None:
        in_specs.append(pl.BlockSpec(memory_space=pltpu.SMEM))
        args.append(divisor.reshape(1))
    kind = BF if divisor is None else F32
    return pl.pallas_call(
        kernel,
        grid_spec=pltpu.PrefetchScalarGridSpec(
            num_scalar_prefetch=1,
            grid=(count,),
            in_specs=in_specs,
            out_specs=pl.BlockSpec((1, rows, columns), lambda i, at: (i, 0, 0)),
        ),
        out_shape=jax.ShapeDtypeStruct((count, rows, columns), kind),
        compiler_params=pltpu.CompilerParams(vmem_limit_bytes=60 * 2**20),
        cost_estimate=SHORT,
        name="add_slabs",
    )(places.at_z.astype(jnp.int32).reshape(1), *args)


class Slots:
    def __init__(self, places):
        self.places = places
        self.before, self.now, self.ready = (), [], []

    def tie(self, value):
        return after(value, *self.before, *self.ready)

    def note(self, *values):
        self.now += values

    def next(self, *values):
        self.note(*values)
        self.before, self.now, self.ready = tuple(self.now), [], []

    def send(self, value, flip):
        value = after(value, *self.before)
        self.ready.append(value)
        return self.follow(value, flip)

    def follow(self, value, flip):
        other = self.places.swap(value, flip)
        self.note(other)
        return other


class Gather:
    def __init__(self, slots, shard):
        self.slots, self.places = slots, slots.places
        self.rows = self.places.wide * shard.shape[0]
        self.parts = [shard[None]]

    def all_z(self):
        for d in range(1, self.places.z):
            self.parts.append(self.slots.send(self.parts[0], lambda core: (d, 0, 0, 0)))

    def step(self, i, exchange):
        joined = join([p.reshape(-1, *p.shape[-2:]) for p in self.parts])
        self.parts = [joined]
        self.parts.append(exchange(joined, self.places.step_flip(i)))

    def first(self):
        for i in range(len(self.places.orders[0]) - 1):
            self.step(i, self.slots.follow if i else self.slots.send)

    def last(self):
        self.step(len(self.places.orders[0]) - 1, self.slots.send)

    def cores(self):
        parts = [p.reshape(-1, self.places.z, *p.shape[-2:]) for p in self.parts]
        self.parts = parts + [self.slots.send(p, lambda core: (0, 0, 1, 0)) for p in parts]

    def whole(self):
        whole = assemble(self.places, self.slots.tie(tuple(self.parts)))
        return whole.reshape(-1, self.rows, whole.shape[-1])


class Scatter:
    def __init__(self, slots, a, parts):
        self.slots, self.places = slots, slots.places
        stack, self.to_core = grad_stacks(self.places, a, parts)
        self.terms, self.z_terms, self.half = [stack], [], stack.shape[0]

    def cores(self, exchange):
        self.terms.append(exchange(self.to_core, lambda core: (0, 0, 1, 0)))

    def step(self, i, exchange):
        self.half //= 2
        send = add_stacks(self.terms, self.half)
        self.terms.append(exchange(send, self.places.step_flip(i)))

    def first(self):
        self.step(len(self.places.orders[0]) - 1, self.slots.send)

    def last(self):
        for i in reversed(range(len(self.places.orders[0]) - 1)):
            chained = i < len(self.places.orders[0]) - 2
            self.step(i, self.slots.follow if chained else self.slots.send)

    def step_z(self, *bits):
        for i, bit in enumerate(bits):
            exchange = self.slots.follow if i else self.slots.send
            send = add_slabs(self.places, self.terms, self.z_terms, bit, bit)
            self.z_terms.append((0, exchange(send, lambda core: (bit, 0, 0, 0))))

    def direct_z(self):
        for d in reversed(range(1, self.places.z)):
            send = add_slabs(self.places, self.terms, self.z_terms, d, 1)
            self.z_terms.append((0, self.slots.send(send, lambda core: (d, 0, 0, 0))))

    def result(self, divisor):
        divisor = self.slots.tie(divisor)
        return add_slabs(self.places, self.terms, self.z_terms, 0, 1, divisor)[0]


def dot(a, b, dims, out=F32):
    return lax.dot_general(a, b, (dims, ((), ())), preferred_element_type=F32).astype(out)


def split(a, count):
    width = a.shape[1] // count
    return [a[:, n * width : (n + 1) * width] for n in range(count)]


def on_device(
    inputs,
    cotangent,
    class_ids,
    step_ids,
    image_counts,
    w_qkv,
    w_out,
    w_gate,
    w_up,
    w_down,
    ada_weight,
    ada_bias,
    class_table,
    norm_gains,
):
    places = Places()
    wide, narrow, at_w, at_n = places.wide, places.narrow, places.w, places.x
    images, length, width = inputs.shape
    tables, sums = head_tables(length), head_sums()
    gains = jnp.tile(norm_gains, (1, H))
    local_count = image_counts[0]

    tokens = images * length

    def flat(v):
        return v.reshape(tokens, -1)

    def deep(v):
        return v.reshape(images, length, -1)

    t = Slots(places)
    z_low, z_high = places.z_bits[:1], places.z_bits[1:]
    z_down = z_high[::-1]
    qkv, out, gate, up, down = [
        Gather(t, shard) for shard in (w_qkv, w_out, w_gate, w_up, w_down)
    ]

    qkv.all_z()
    small = [class_ids, step_ids, image_counts, ada_bias]
    small = jnp.concatenate([v.astype(F32) for v in small])[None]
    bits = places.all_bits()
    small = places.gather_bits(places.open_small(small), bits)
    small = small.reshape(wide * narrow, -1)
    t.next(small)

    qkv.first()
    out.all_z()
    small = t.tie(small)
    ids = small[:, : 2 * images].reshape(-1, 2, images).transpose(0, 2, 1).reshape(-1, 2)
    ids = ids.astype(jnp.int32)
    real_count = jnp.sum(small[:, 2 * images])
    bias = small[:, 2 * images + 1 :].reshape(-1)
    rows_here, cols_here = class_table.shape
    class_hot = ids[:, :1] - at_n * rows_here == jnp.arange(rows_here, dtype=jnp.int32)[None, :]
    picked = dot(class_hot.astype(BF), class_table, ((1,), (0,)))
    column = at_w * cols_here + jnp.arange(cols_here, dtype=jnp.int32)
    half_width = width // 2
    frequency = jnp.exp(-math.log(10000.0) * (column % half_width).astype(F32) / half_width)
    angles = ids[:, 1:].astype(F32) * frequency[None, :]
    wave = jnp.where(column[None, :] < half_width, jnp.cos(angles), jnp.sin(angles))
    condition = places.add_narrow(picked) + wave
    cond_act = jax.nn.silu(condition).astype(BF)
    t.next(cond_act)

    qkv.last()
    gate.all_z()
    mod_part = dot(t.tie(cond_act), ada_weight, ((1,), (0,)))
    mod_part = places.scatter_chip_row(mod_part.reshape(wide, narrow, images, -1))
    t.next(mod_part, *tables, sums)

    qkv.cores()
    out.first()
    gate.first()
    mod_part = places.trade_narrow(places.scatter_z(t.tie(mod_part)))
    t.next(mod_part)

    out.last()
    gate.last()
    up.all_z()
    qkv_b = qkv.whole()
    modulation = t.tie(mod_part).transpose(1, 0, 2).reshape(images, -1) + bias
    pieces = modulation.reshape(images, 6, width)
    normed, _ = layer_norm(inputs.astype(F32))
    attn_in = flat((normed * (1.0 + pieces[:, 1:2]) + pieces[:, 0:1]).astype(BF))
    t.next(attn_in, qkv_b)

    out.cores()
    gate.cores()
    up.first()
    packed = project(t.tie(attn_in), qkv_b)
    t.next(*packed)

    up.last()
    down.all_z()
    packed = t.tie(packed)
    queries, key_rows, value_rows, mixed = attention_forward(packed, gains, tables, sums, images)
    slot_real = (jnp.arange(images, dtype=jnp.int32) < local_count).astype(F32)
    grad_y = cotangent.astype(F32) * slot_real[:, None, None]
    d_mlp = split(flat((pieces[:, 5:6] * grad_y).astype(BF)), narrow)
    t.next(mixed, *d_mlp)

    up.cores()
    down.first()
    out_b = out.whole()
    attn_out, hidden_one, mlp_in = attention_tail(mixed, out_b, flat(inputs), pieces, images)
    gate_b = gate.whole()[0]
    t.next(mlp_in, gate_b)

    down.last()
    up_b = up.whole()[0]
    gate_val, up_val, hidden_mid = gated(mlp_in, gate_b, up_b)
    t.next(hidden_mid)

    down.cores()
    g_down = Scatter(t, t.tie(hidden_mid), d_mlp)
    t.next(g_down.to_core)

    g_down.cores(t.send)
    down_b = down.whole()
    t.next(down_b)

    g_down.first()
    d_gate, d_up, d_mlp_in = gated_back(t.tie(d_mlp), down_b, gate_val, up_val, gate_b, up_b)
    t.next(d_mlp_in)

    g_down.last()
    g_gate = Scatter(t, mlp_in, [t.tie(d_gate)])
    g_gate.cores(t.follow)
    d_hidden, d_mixed, sums_b, *d_attn = middle_back(
        t.tie(d_mlp_in), hidden_one, attn_out, flat(cotangent), pieces, out_b, image_counts, images
    )
    t.next(d_mixed)

    g_gate.first()
    g_down.step_z(*z_down)
    g_up = Scatter(t, mlp_in, [t.tie(d_up)])
    g_up.cores(t.follow)
    g_out = Scatter(t, mixed, t.tie(d_attn))
    t.next(g_out.to_core)

    g_gate.last()
    g_up.first()
    g_out.cores(t.send)
    g_down.step_z(*z_low)
    d_packed, gain_terms = attention_backward(
        packed, queries, key_rows, value_rows, t.tie(d_mixed), gains, tables, sums, images
    )
    t.next(*d_packed)

    g_up.last()
    g_out.first()
    g_gate.step_z(*z_down)
    g_qkv = Scatter(t, attn_in, t.tie(d_packed))
    g_qkv.cores(t.follow)
    block_output, sums_gate = block_tail(
        after(hidden_mid, g_qkv.to_core),
        down_b,
        hidden_one,
        flat(cotangent),
        pieces,
        image_counts,
        images,
    )
    t.next(sums_gate)

    g_qkv.first()
    g_out.last()
    g_up.step_z(*z_down)
    g_gate.step_z(*z_low)
    d_tokens, sums_a = block_head_back(
        t.tie(d_packed), d_hidden, flat(inputs), pieces, qkv_b, images
    )
    grad_gains = gain_terms.sum(0).reshape(2, H, HD).sum(1).reshape(1, -1)
    gains_high = grad_gains.astype(BF)
    gains_low = (grad_gains - gains_high.astype(F32)).astype(BF)
    rest = jnp.zeros((images - 2, 2 * HD), BF)
    grad_gains = jnp.concatenate([gains_high, gains_low, rest], axis=0)
    d_modulation = jnp.concatenate([sums_a, sums_b[:, 2:], sums_b[:, :2], sums_gate], axis=1)
    d_modulation = d_modulation.astype(BF).reshape(images, -1)
    d_modulation = jnp.concatenate([d_modulation, grad_gains], axis=1)
    t.next(d_modulation)

    g_qkv.last()
    g_up.step_z(*z_low)
    g_out.step_z(*z_down)
    d_all = places.open_small(t.tie(d_modulation))
    d_all = places.gather_bits(d_all, bits[: len(places.z_bits)])
    t.next(d_all)

    g_qkv.direct_z()
    g_out.step_z(*z_low)
    d_all = places.gather_bits(t.tie(d_all), bits[len(places.z_bits) :])
    d_all = d_all.reshape(wide * narrow * images, -1)
    gain_sum = d_all[:, 6 * width : 6 * width + 2 * HD].astype(F32)
    gain_sum = jnp.sum(gain_sum, axis=0).reshape(2, HD) / real_count
    d_mod = d_all[:, : 6 * width]
    ada_cols = ada_weight.shape[1]
    d_mod_here = lax.dynamic_slice_in_dim(d_mod, at_n * ada_cols, ada_cols, 1)
    g_ada = dot(cond_act, d_mod_here, ((0,), (0,))) / real_count
    bias_cols = ada_bias.shape[0]
    bias_at = (at_w * narrow + at_n) * bias_cols
    g_bias = jnp.sum(lax.dynamic_slice_in_dim(d_mod, bias_at, bias_cols, 1).astype(F32), axis=0)
    g_bias = g_bias / real_count
    d_cond_act = places.add_narrow(dot(d_mod_here, ada_weight, ((1,), (1,))))
    cond_sigmoid = jax.nn.sigmoid(condition)
    d_condition = d_cond_act * cond_sigmoid * (1.0 + condition * (1.0 - cond_sigmoid))
    g_table = jnp.dot(class_hot.astype(F32).T, d_condition, precision=HIGHEST) / real_count
    r_out, r_gate, r_up, r_down = [g.result(real_count) for g in (g_out, g_gate, g_up, g_down)]
    at, late = g_qkv.z_terms[-1]
    g_qkv.z_terms[-1] = (at, after(late, g_ada, g_table, r_out, r_gate, r_up, r_down))
    r_qkv = g_qkv.result(real_count)

    return (
        deep(block_output),
        deep(d_tokens),
        r_qkv,
        r_out,
        r_gate,
        r_up,
        r_down,
        g_ada,
        g_bias,
        g_table,
        gain_sum,
    )


def solution(mesh):
    split = P("wide", "narrow")
    images = P(ALL, None, None)
    return jax.shard_map(
        on_device,
        mesh=mesh,
        in_specs=(
            images,
            images,
            P(ALL),
            P(ALL),
            P(ALL),
            split,
            split,
            split,
            split,
            split,
            split,
            P(ALL),
            P("narrow", "wide"),
            P(),
        ),
        out_specs=(
            images,
            images,
            split,
            split,
            split,
            split,
            split,
            split,
            P(ALL),
            P("narrow", "wide"),
            P(),
        ),
        check_vma=False,
    )
```

```python
import math

import jax
import jax.numpy as jnp
from jax import lax
from jax.experimental import pallas as pl
from jax.experimental.pallas import tpu as pltpu
from jax.sharding import PartitionSpec as P

H = 16
HD = 72
CLASSES = 1000
GRID = 16

EPSILON = 1e-06
HIGHEST = lax.Precision.HIGHEST
ALL = ("wide", "narrow")
BF = jnp.bfloat16
F32 = jnp.float32
LONG = pl.CostEstimate(flops=10**12, bytes_accessed=1, transcendentals=0)
SHORT = pl.CostEstimate(flops=1, bytes_accessed=1, transcendentals=0)


def layer_norm(values):
    centre = values - jnp.mean(values, axis=-1, keepdims=True)
    inverse = lax.rsqrt(jnp.mean(centre * centre, axis=-1, keepdims=True) + EPSILON)
    return (centre * inverse, inverse)


def head_tables(length):
    quarter = HD // 4
    lane = jnp.arange(H * HD, dtype=jnp.int32) % HD
    frequency = 10000.0 ** (-(lane % quarter).astype(F32) / quarter)
    patch = jnp.arange(length, dtype=jnp.int32)[:, None]
    place = jnp.where(lane[None, :] < 2 * quarter, patch // GRID, patch % GRID)
    angles = place.astype(F32) * frequency[None, :]
    cosine, sine = jnp.cos(angles), jnp.sin(angles)
    first = (lane // quarter % 2 == 0)[None, :]
    return [cosine, jnp.where(first, -sine, 0.0), jnp.where(first, 0.0, sine)]


def head_sums():
    lane = lax.broadcasted_iota(jnp.int32, (H * HD, 128), 0) // HD
    return (lane == lax.broadcasted_iota(jnp.int32, (H * HD, 128), 1)).astype(BF)


def exact_dot(a, b, dims):
    total = None
    for _ in range(3):
        term = a.astype(BF)
        a = a - term.astype(F32)
        part = lax.dot_general(term, b, (dims, ((), ())), preferred_element_type=F32)
        total = part if total is None else total + part
    return total


def head_mean(values, sums):
    mean = exact_dot(values, sums, ((1,), (0,))) * (1.0 / HD)
    return exact_dot(mean, sums, ((1,), (1,)))


def shifted(values, cosine, above, below, sign):
    quarter, width = HD // 4, values.shape[1]
    up = pltpu.roll(values, width - quarter, 1)
    down = pltpu.roll(values, quarter, 1)
    return values * cosine + sign * (up * above + down * below)


def window(head):
    first, last = head * HD // 128 * 128, ((head + 1) * HD + 127) // 128 * 128
    return first, last


def only(values, head):
    first, last = window(head)
    part = values[:, first:last]
    lane = first + lax.broadcasted_iota(jnp.int32, (1, last - first), 1)
    mine = ((lane >= head * HD) & (lane < (head + 1) * HD)).astype(values.dtype)
    return part * mine


class Tiles:
    def __init__(self, store):
        self.store, self.held = store, {}

    def add(self, head, value):
        first, last = window(head)
        for tile in range(first // 128, last // 128):
            part = value[:, tile * 128 - first : tile * 128 - first + 128]
            self.held[tile] = self.held[tile] + part if tile in self.held else part
        done = (head + 1) * HD // 128
        for tile in sorted(self.held):
            if tile < done or head == H - 1:
                self.store(tile * 128, self.held.pop(tile))


def mm(a, b, dims):
    return lax.dot_general(a, b, (dims, ((), ())), preferred_element_type=F32)


def only_turned(values, head):
    first, last = window(head)
    part = values[first:last, :]
    row = first + lax.broadcasted_iota(jnp.int32, (last - first, 1), 0)
    mine = ((row >= head * HD) & (row < (head + 1) * HD)).astype(values.dtype)
    return part * mine


def softmax_of(queries, keys_turned, head):
    first, last = window(head)
    scores = mm(only(queries, head), keys_turned[first:last, :], ((1,), (0,))) * (HD ** (-0.5))
    exponent = jnp.exp(scores - jnp.max(scores, axis=1, keepdims=True))
    return exponent / jnp.sum(exponent, axis=1, keepdims=True)


def attention_forward(packed, gains, tables, sums, images):
    tokens = packed[0].shape[0]
    length, width, blocks = tokens // images, H * HD, len(packed)

    def kernel(*refs):
        parts, refs = refs[:blocks], refs[blocks:]
        gain, cosine, above, below, sums_ref, q_ref, k_ref, v_ref, mixed_ref, k_turned = refs
        whole = jnp.concatenate([p[...] for p in parts], axis=1)
        sums_here = sums_ref[...]
        for i, ref in enumerate((q_ref, k_ref)):
            raw = whole[:, i * width : (i + 1) * width]
            normed = raw * lax.rsqrt(head_mean(raw * raw, sums_here) + EPSILON)
            turned = shifted(normed * gain[i : i + 1, :], cosine[...], above[...], below[...], 1.0)
            ref[...] = turned.astype(BF)
        v_ref[...] = whole[:, 2 * width :].astype(BF)

        def store(first, value):
            mixed_ref[:, first : first + 128] = value.astype(BF)

        k_turned[...] = k_ref[...].T
        mixed = Tiles(store)
        for head in range(H):
            attention = softmax_of(q_ref, k_turned, head).astype(BF)
            mixed.add(head, mm(attention, only(v_ref, head), ((1,), (0,))))

    def rows(n):
        return pl.BlockSpec((length, n), lambda i: (i, 0))

    def all_of(a):
        return pl.BlockSpec(a.shape, lambda i: (0, 0))

    out = jax.ShapeDtypeStruct((tokens, width), BF)
    return pl.pallas_call(
        kernel,
        grid=(images,),
        out_shape=[out] * 4,
        in_specs=[rows(p.shape[1]) for p in packed] + [all_of(a) for a in (gains, *tables, sums)],
        out_specs=[rows(width)] * 4,
        scratch_shapes=[pltpu.VMEM((width, length), BF)],
        compiler_params=pltpu.CompilerParams(vmem_limit_bytes=60 * 2**20),
        cost_estimate=LONG,
        name="attention_forward",
    )(*packed, gains, *tables, sums)


def attention_backward(packed, queries, keys, values, d_mixed, gains, tables, sums, images):
    tokens = queries.shape[0]
    length, width, blocks = tokens // images, H * HD, len(packed)
    block = packed[0].shape[1]

    def kernel(*refs):
        parts, refs = refs[:blocks], refs[blocks:]
        q_ref, k_ref, v_ref, d_ref, gain, cosine, above, below, sums_ref = refs[:9]
        outs, refs = refs[9 : 9 + blocks], refs[9 + blocks :]
        gain_ref, d_q_turned, d_k, d_v, q_turned, k_turned, d_turned = refs

        def store_to(ref):
            def store(first, value):
                ref[:, first : first + 128] = value

            return store

        for ref, turned in ((q_ref, q_turned), (k_ref, k_turned), (d_ref, d_turned)):
            turned[...] = ref[...].T
        all_k, all_v = [Tiles(store_to(ref)) for ref in (d_k, d_v)]
        rows_q = {}
        for head in range(H):
            first, last = window(head)
            scores = mm(only(k_ref, head), q_turned[first:last, :], ((1,), (0,))) * (HD ** (-0.5))
            exponent = jnp.exp(scores - jnp.max(scores, axis=0, keepdims=True))
            soft = exponent / jnp.sum(exponent, axis=0, keepdims=True)
            all_v.add(head, mm(soft.astype(BF), only(d_ref, head), ((1,), (0,))))
            d_soft = mm(only(v_ref, head), d_turned[first:last, :], ((1,), (0,)))
            inner = jnp.sum(soft * d_soft, axis=0, keepdims=True)
            d_scores = (soft * (d_soft - inner) * (HD ** (-0.5))).astype(BF)
            all_k.add(head, mm(d_scores, only(q_ref, head), ((1,), (0,))))
            part = mm(only_turned(k_turned, head), d_scores, ((1,), (0,)))
            for tile in range(first // 128, last // 128):
                rows = part[tile * 128 - first : tile * 128 - first + 128]
                rows_q[tile] = rows_q[tile] + rows if tile in rows_q else rows
            for tile in sorted(rows_q):
                if tile < (head + 1) * HD // 128 or head == H - 1:
                    d_q_turned[tile * 128 : tile * 128 + 128, :] = rows_q.pop(tile)
        whole = jnp.concatenate([p[...] for p in parts], axis=1)
        sums_here = sums_ref[...]
        done = []
        for i, value in enumerate((d_q_turned[...].T, d_k[...])):
            raw = whole[:, i * width : (i + 1) * width]
            inverse = lax.rsqrt(head_mean(raw * raw, sums_here) + EPSILON)
            normed = raw * inverse
            scaled = shifted(value, cosine[...], above[...], below[...], -1.0)
            gain_ref[0, i : i + 1, :] = jnp.sum(scaled * normed, axis=0, keepdims=True)
            incoming = scaled * gain[i : i + 1, :]
            mean = head_mean(incoming * normed, sums_here)
            done.append((inverse * (incoming - normed * mean)).astype(BF))
        done.append(d_v[...].astype(BF))
        done = jnp.concatenate(done, axis=1)
        for j, out in enumerate(outs):
            out[...] = done[:, j * block : (j + 1) * block]

    def rows(n):
        return pl.BlockSpec((length, n), lambda i: (i, 0))

    def all_of(a):
        return pl.BlockSpec(a.shape, lambda i: (0, 0))

    outs = pl.pallas_call(
        kernel,
        grid=(images,),
        out_shape=[jax.ShapeDtypeStruct((tokens, block), BF)] * blocks
        + [jax.ShapeDtypeStruct((images, 2, width), F32)],
        in_specs=[rows(block)] * blocks
        + [rows(width)] * 4
        + [all_of(a) for a in (gains, *tables, sums)],
        out_specs=[rows(block)] * blocks + [pl.BlockSpec((1, 2, width), lambda i: (i, 0, 0))],
        scratch_shapes=[pltpu.VMEM((width, length), F32)]
        + [pltpu.VMEM((length, width), F32)] * 2
        + [pltpu.VMEM((width, length), BF)] * 3,
        compiler_params=pltpu.CompilerParams(vmem_limit_bytes=60 * 2**20),
        cost_estimate=LONG,
        name="attention_backward",
    )(*packed, queries, keys, values, d_mixed, gains, *tables, sums)
    return outs[:blocks], outs[blocks]

def whole_block(a):
    return pl.BlockSpec(a.shape, lambda *i: (0,) * a.ndim)


def chunk_of(columns, most):
    count = -(-columns // most)
    return columns if count == 1 else -(-columns // (128 * count)) * 128


def project(a, blocks):
    tokens, depth = a.shape
    count, _, columns = blocks.shape
    chunk = chunk_of(columns, 640)

    def kernel(a_ref, *refs):
        for w_ref, out_ref in zip(refs[:count], refs[count:]):
            out_ref[...] = mm(a_ref[...], w_ref[...], ((1,), (0,)))

    return pl.pallas_call(
        kernel,
        grid=(-(-columns // chunk),),
        out_shape=[jax.ShapeDtypeStruct((tokens, columns), F32)] * count,
        in_specs=[whole_block(a)]
        + [pl.BlockSpec((None, depth, chunk), lambda i, j=j: (j, 0, i)) for j in range(count)],
        out_specs=[pl.BlockSpec((tokens, chunk), lambda i: (0, i))] * count,
        compiler_params=pltpu.CompilerParams(vmem_limit_bytes=60 * 2**20),
        cost_estimate=LONG,
        name="project",
    )(a, *[blocks] * count)


def gated(a, w_gate, w_up):
    tokens, depth = a.shape
    columns = w_gate.shape[1]
    chunk = 512

    def kernel(a_ref, g_ref, u_ref, gate_ref, up_ref, mid_ref):
        gate = mm(a_ref[...], g_ref[...], ((1,), (0,)))
        up = mm(a_ref[...], u_ref[...], ((1,), (0,)))
        gate_ref[...] = gate
        up_ref[...] = up
        mid_ref[...] = (gate * jax.nn.sigmoid(gate) * up).astype(BF)

    weight = pl.BlockSpec((depth, chunk), lambda i: (0, i))
    out = pl.BlockSpec((tokens, chunk), lambda i: (0, i))
    return pl.pallas_call(
        kernel,
        grid=(columns // chunk,),
        out_shape=[jax.ShapeDtypeStruct((tokens, columns), t) for t in (F32, F32, BF)],
        in_specs=[whole_block(a), weight, weight],
        out_specs=[out] * 3,
        compiler_params=pltpu.CompilerParams(vmem_limit_bytes=60 * 2**20),
        cost_estimate=LONG,
        name="gated",
    )(a, w_gate, w_up)


def gated_back(d_parts, down, gate_val, up_val, w_gate, w_up):
    tokens, columns = gate_val.shape
    depth, count, chunk = w_gate.shape[0], down.shape[0], 512

    def kernel(*refs):
        d_refs, w_refs, refs = refs[:count], refs[count : 2 * count], refs[2 * count :]
        gate_ref, up_ref, g_ref, u_ref, d_gate_ref, d_up_ref, in_ref = refs
        d_mid = None
        for d_ref, w_ref in zip(d_refs, w_refs):
            term = mm(d_ref[...], w_ref[...], ((1,), (1,)))
            d_mid = term if d_mid is None else d_mid + term
        gate, up = gate_ref[...], up_ref[...]
        sigmoid = jax.nn.sigmoid(gate)
        silu = gate * sigmoid
        d_gate = (d_mid * up * (sigmoid + silu * (1.0 - sigmoid))).astype(BF)
        d_up = (d_mid * silu).astype(BF)
        d_gate_ref[...] = d_gate
        d_up_ref[...] = d_up
        term = mm(d_gate, g_ref[...], ((1,), (1,))) + mm(d_up, u_ref[...], ((1,), (1,)))

        @pl.when(pl.program_id(0) == 0)
        def _():
            in_ref[...] = term

        @pl.when(pl.program_id(0) > 0)
        def _():
            in_ref[...] += term

    width = down.shape[2]
    token = pl.BlockSpec((tokens, chunk), lambda i: (0, i))
    weight = pl.BlockSpec((depth, chunk), lambda i: (0, i))
    return pl.pallas_call(
        kernel,
        grid=(columns // chunk,),
        out_shape=[jax.ShapeDtypeStruct((tokens, columns), BF)] * 2
        + [jax.ShapeDtypeStruct((tokens, depth), F32)],
        in_specs=[whole_block(d) for d in d_parts]
        + [pl.BlockSpec((None, chunk, width), lambda i, j=j: (j, i, 0)) for j in range(count)]
        + [token, token, weight, weight],
        out_specs=[token, token, pl.BlockSpec((tokens, depth), lambda i: (0, 0))],
        compiler_params=pltpu.CompilerParams(vmem_limit_bytes=60 * 2**20),
        cost_estimate=LONG,
        name="gated_back",
    )(*d_parts, *[down] * count, gate_val, up_val, w_gate, w_up)


def normal(values):
    centre = values - jnp.mean(values, axis=1, keepdims=True)
    inverse = lax.rsqrt(jnp.mean(centre * centre, axis=1, keepdims=True) + EPSILON)
    return centre * inverse, inverse


def normal_back(gradient, normed, inverse):
    mean = jnp.mean(gradient, axis=1, keepdims=True)
    return inverse * (
        gradient - mean - normed * jnp.mean(gradient * normed, axis=1, keepdims=True)
    )


def per_image(kernel, images, by_image, whole, outs, vmem, name, scalar=None):
    def spec(rows, rest):
        return pl.BlockSpec((rows, *rest), lambda i: (i,) + (0,) * len(rest))

    in_specs = [spec(a.shape[0] // images, a.shape[1:]) for a in by_image]
    in_specs += [whole_block(a) for a in whole]
    args = [*by_image, *whole]
    if scalar is not None:
        in_specs.append(pl.BlockSpec(memory_space=pltpu.SMEM))
        args.append(scalar)
    return pl.pallas_call(
        kernel,
        grid=(images,),
        out_shape=[jax.ShapeDtypeStruct((images * rows, *rest), t) for rows, rest, t in outs],
        in_specs=in_specs,
        out_specs=[spec(rows, rest) for rows, rest, _ in outs],
        compiler_params=pltpu.CompilerParams(vmem_limit_bytes=60 * 2**20),
        cost_estimate=LONG,
        name=name,
    )(*args)


def attention_tail(mixed, out_b, inputs, pieces, images):
    tokens, width = mixed.shape

    def kernel(mixed_ref, in_ref, piece, *refs):
        w_ref, attn_ref, hidden_ref, mlp_ref = refs
        attn = [mm(mixed_ref[...], w_ref[j], ((1,), (0,))) for j in range(out_b.shape[0])]
        attn = jnp.concatenate(attn, axis=1)
        attn_ref[...] = attn
        hidden = in_ref[...].astype(F32) + piece[0, 2:3, :] * attn
        hidden_ref[...] = hidden
        normed, _ = normal(hidden)
        mlp_ref[...] = (normed * (1.0 + piece[0, 4:5, :]) + piece[0, 3:4, :]).astype(BF)

    rows = tokens // images
    outs = [(rows, (width,), F32), (rows, (width,), F32), (rows, (width,), BF)]
    return per_image(kernel, images, [mixed, inputs, pieces], [out_b], outs, 32, "attention_tail")


def block_tail(hidden_mid, down_b, hidden_one, cotangent, pieces, count, images):
    tokens, width = hidden_one.shape

    def kernel(mid_ref, hidden_ref, cot_ref, piece, *refs):
        w_ref, count_ref, out_ref, gate_ref = refs
        mlp = [mm(mid_ref[...], w_ref[j], ((1,), (0,))) for j in range(down_b.shape[0])]
        mlp = jnp.concatenate(mlp, axis=1)
        out_ref[...] = (hidden_ref[...] + piece[0, 5:6, :] * mlp).astype(BF)
        real = (pl.program_id(0) < count_ref[0]).astype(F32)
        grad = cot_ref[...].astype(F32) * real
        gate_ref[0] = jnp.sum(grad * mlp, axis=0, keepdims=True)

    rows = tokens // images
    outs = [(rows, (width,), BF), (1, (1, width), F32)]
    by_image = [hidden_mid, hidden_one, cotangent, pieces]
    return per_image(kernel, images, by_image, [down_b], outs, 40, "block_tail", count)


def middle_back(d_mlp_in, hidden_one, attn_out, cotangent, pieces, out_b, count, images):
    tokens, width = d_mlp_in.shape
    blocks, _, columns = out_b.shape

    def kernel(in_ref, hidden_ref, attn_ref, cot_ref, piece, *refs):
        w_ref, count_ref, refs = refs[0], refs[1], refs[2:]
        d_hidden_ref, d_mixed_ref, sums_ref = refs[:3]
        d_in = in_ref[...]
        normed, inverse = normal(hidden_ref[...])
        sums_ref[0, 0:1] = jnp.sum(d_in, axis=0, keepdims=True)
        sums_ref[0, 1:2] = jnp.sum(d_in * normed, axis=0, keepdims=True)
        real = (pl.program_id(0) < count_ref[0]).astype(F32)
        grad = cot_ref[...].astype(F32) * real
        d_hidden = grad + normal_back(d_in * (1.0 + piece[0, 4:5, :]), normed, inverse)
        d_hidden_ref[...] = d_hidden
        sums_ref[0, 2:3] = jnp.sum(d_hidden * attn_ref[...], axis=0, keepdims=True)
        d_attn = (piece[0, 2:3, :] * d_hidden).astype(BF)
        d_mixed = None
        for j, out in enumerate(refs[3:]):
            part = d_attn[:, j * columns : (j + 1) * columns]
            out[...] = part
            term = mm(part, w_ref[j], ((1,), (1,)))
            d_mixed = term if d_mixed is None else d_mixed + term
        d_mixed_ref[...] = d_mixed.astype(BF)

    rows = tokens // images
    outs = [(rows, (width,), F32), (rows, (width,), BF), (1, (3, width), F32)]
    outs += [(rows, (columns,), BF)] * blocks
    by_image = [d_mlp_in, hidden_one, attn_out, cotangent, pieces]
    return per_image(kernel, images, by_image, [out_b], outs, 40, "middle_back", count)


def block_head_back(d_packed, d_hidden, inputs, pieces, qkv_b, images):
    tokens, width = d_hidden.shape
    blocks = qkv_b.shape[0]

    def kernel(*refs):
        d_refs, (d_hidden_ref, in_ref, piece) = refs[:blocks], refs[blocks : blocks + 3]
        w_ref, out_ref, sums_ref = refs[blocks + 3 :]
        d_in = None
        for j, d in enumerate(d_refs):
            term = mm(d[...], w_ref[j], ((1,), (1,)))
            d_in = term if d_in is None else d_in + term
        normed, inverse = normal(in_ref[...].astype(F32))
        sums_ref[0, 0:1] = jnp.sum(d_in, axis=0, keepdims=True)
        sums_ref[0, 1:2] = jnp.sum(d_in * normed, axis=0, keepdims=True)
        back = normal_back(d_in * (1.0 + piece[0, 1:2, :]), normed, inverse)
        out_ref[...] = (d_hidden_ref[...] + back).astype(BF)

    outs = [(tokens // images, (width,), BF), (1, (2, width), F32)]
    by_image = [*d_packed, d_hidden, inputs, pieces]
    return per_image(kernel, images, by_image, [qkv_b], outs, 48, "block_head_back")


def grad_stacks(places, a, parts):
    tokens, features = a.shape
    z, count = places.z, places.narrow
    joined = len(parts) < count
    columns = parts[0].shape[1] // (count if joined else 1)
    rows = features // (4 * z)
    chunk = chunk_of(columns, 900)
    masks = [places.masks(0), places.masks(1)]
    total = len(masks[0])

    def kernel(at, a_ref, *refs):
        d_refs, (own_ref, send_ref, turned, product) = refs[:count], refs[count:]

        @pl.when(pl.program_id(0) == 0)
        def _():
            turned[...] = a_ref[...].T

        for i, d_ref in enumerate(d_refs):
            whole = mm(turned[...], d_ref[...], ((1,), (0,)))
            for k in range(4 * z):
                product[i, k] = whole[k * rows : (k + 1) * rows].astype(BF)
        core, y, x = at[0], at[1], at[2]
        for out, owner in ((own_ref, core), (send_ref, 1 - core)):
            for j in range(total):
                dy = jnp.where(owner == 0, masks[0][j][0], masks[1][j][0])
                dx = jnp.where(owner == 0, masks[0][j][1], masks[1][j][1])
                for k in range(z):
                    out[j, k] = product[x ^ dx, (k * 2 + (y ^ dy)) * 2 + owner]

    at = jnp.stack([places.at_c, places.at_y, places.x]).astype(jnp.int32)
    shape = (total, z, rows, columns)
    out = pl.BlockSpec((total, z, rows, chunk), lambda i: (0, 0, 0, i))
    return pl.pallas_call(
        kernel,
        grid=(-(-columns // chunk),),
        out_shape=[jax.ShapeDtypeStruct(shape, BF)] * 2,
        in_specs=[pl.BlockSpec(memory_space=pltpu.SMEM), whole_block(a)]
        + [
            pl.BlockSpec((tokens, chunk), lambda i, j=j: (0, j * (columns // chunk) + i if joined else i))
            for j in range(count)
        ],
        out_specs=[out, out],
        scratch_shapes=[
            pltpu.VMEM((features, tokens), BF),
            pltpu.VMEM((count, 4 * z, rows, chunk), BF),
        ],
        compiler_params=pltpu.CompilerParams(vmem_limit_bytes=60 * 2**20),
        cost_estimate=LONG,
        name="grad_stacks",
    )(at, a, *(parts * count if joined else parts))


class Places:
    def __init__(self):
        self.wide, self.narrow = lax.axis_size("wide"), lax.axis_size("narrow")
        self.z = self.wide // 4
        w = lax.axis_index("wide")
        self.w, self.x = w, lax.axis_index("narrow")
        self.at_z, self.at_y, self.at_c = w // 4, (w // 2) % 2, w % 2
        self.z_bits = [1 << i for i in range(self.z.bit_length() - 1)]
        self.x_bits = [1 << i for i in range(self.narrow.bit_length() - 1)]
        x_masks = [(0, bit) for bit in self.x_bits]
        self.orders = ([(1, 0)] + x_masks, x_masks + [(1, 0)])

    def swap(self, value, flip):
        pairs = []
        for w in range(self.wide):
            for x in range(self.narrow):
                dz, dy, dc, dx = flip(w % 2)
                to = (w // 4 ^ dz) * 4 + (w // 2 % 2 ^ dy) * 2 + (w % 2 ^ dc)
                pairs.append((w * self.narrow + x, to * self.narrow + (x ^ dx)))
        return lax.ppermute(value, ALL, pairs)

    def step_flip(self, i):
        return lambda core: (0, self.orders[core][i][0], 0, self.orders[core][i][1])

    def masks(self, core):
        out = [(0, 0)]
        for dy, dx in self.orders[core]:
            out = out + [(y ^ dy, x ^ dx) for y, x in out]
        return out

    def all_bits(self):
        out = [(0, (bit, 0, 0, 0), self.at_z // bit % 2) for bit in self.z_bits]
        out.append((1, (0, 1, 0, 0), self.at_y))
        out += [(3, (0, 0, 0, bit), self.x // bit % 2) for bit in self.x_bits]
        out.append((2, (0, 0, 1, 0), self.at_c))
        return out

    def open_small(self, value):
        return value[None, None, None, None]

    def gather_bits(self, value, bits):
        for axis, flip, bit in bits:
            other = self.swap(value, lambda core: flip)
            low = jnp.where(bit == 0, value, other)
            high = jnp.where(bit == 0, other, value)
            value = jnp.concatenate([low, high], axis)
        return value

    def add_narrow(self, value):
        for bit in self.x_bits:
            value = value + self.swap(value, lambda core: (0, 0, 0, bit))
        return value

    def scatter_chip_row(self, value):
        value = value.reshape(self.z, 2, 2, *value.shape[1:])
        other = self.swap(take(value, 2, 1 - self.at_c), lambda core: (0, 0, 1, 0))
        value = take(value, 2, self.at_c) + other
        other = self.swap(take(value, 1, 1 - self.at_y), lambda core: (0, 1, 0, 0))
        return take(value, 1, self.at_y) + other

    def scatter_z(self, value):
        for bit in reversed(self.z_bits):
            value = value.reshape(2, bit, *value.shape[1:])
            here = self.at_z // bit % 2
            other = self.swap(take(value, 0, 1 - here), lambda core: (bit, 0, 0, 0))
            value = take(value, 0, here) + other
        return value[0]

    def trade_narrow(self, value):
        if self.narrow != 2:
            return lax.all_to_all(value, "narrow", 0, 0, tiled=True)
        other = self.swap(take(value, 0, 1 - self.x), lambda core: (0, 0, 0, 1))
        own = take(value, 0, self.x)
        return jnp.stack([pick([own, other], self.x), pick([other, own], self.x)])


def pick(parts, index):
    if len(parts) == 1:
        return parts[0]
    if len(parts) == 2:
        return jnp.where(index == 0, parts[0], parts[1])
    return lax.dynamic_index_in_dim(jnp.stack(parts), index, 0, keepdims=False)


def take(value, axis, index):
    return lax.dynamic_index_in_dim(value, index, axis, keepdims=False)


def after(value, *before):
    return lax.optimization_barrier((value,) + before)[0]


def assemble(places, parts):
    half, z, rows, columns = parts[0].shape
    joined = columns % 128 == 0
    masks = [places.masks(0), places.masks(1)]

    def kernel(at, s0, s1, t0, t1, out, held, sem, out_sem):
        core, y, x, here_z = at[0], at[1], at[2], at[3]
        copies = []
        for i, src in enumerate((s0, s1, t0, t1)):
            owner = core ^ (i // 2)
            for j in range(half):
                k = j + half * (i % 2)
                dy = jnp.where(owner == 0, masks[0][k][0], masks[1][k][0])
                dx = jnp.where(owner == 0, masks[0][k][1], masks[1][k][1])
                for d in range(z):
                    if joined:
                        lanes = pl.ds(pl.multiple_of((x ^ dx) * columns, 128), columns)
                        to = held.at[here_z ^ d, y ^ dy, owner, :, lanes]
                    else:
                        to = held.at[x ^ dx, here_z ^ d, y ^ dy, owner]
                    copies.append(pltpu.make_async_copy(src.at[j, d], to, sem.at[len(copies)]))
        for copy in copies:
            copy.start()
        for copy in copies:
            copy.wait()
        whole = pltpu.make_async_copy(held, out, out_sem)
        whole.start()
        whole.wait()

    shape = (places.narrow, z, 2, 2, rows, columns)
    if joined:
        shape = (z, 2, 2, rows, places.narrow * columns)
    at = jnp.stack([places.at_c, places.at_y, places.x, places.at_z]).astype(jnp.int32)
    return pl.pallas_call(
        kernel,
        out_shape=jax.ShapeDtypeStruct(shape, BF),
        in_specs=[pl.BlockSpec(memory_space=pltpu.SMEM)] + [pl.BlockSpec(memory_space=pl.ANY)] * 4,
        out_specs=pl.BlockSpec(memory_space=pl.ANY),
        scratch_shapes=[
            pltpu.VMEM(shape, BF),
            pltpu.SemaphoreType.DMA((4 * half * z,)),
            pltpu.SemaphoreType.DMA,
        ],
        compiler_params=pltpu.CompilerParams(vmem_limit_bytes=60 * 2**20),
        cost_estimate=LONG,
        name="assemble",
    )(at, *parts)


def turn(places, a):
    tokens, features = a.shape
    slabs = 4 * places.z
    rows = features // slabs

    def kernel(at, a_ref, mine_ref, other_ref, turned):
        whole = a_ref[...].astype(F32).T
        for k in range(slabs):
            turned[k] = whole[k * rows : (k + 1) * rows].astype(BF)
        for k in range(slabs // 2):
            mine_ref[k] = turned[2 * k + at[0]]
            other_ref[k] = turned[2 * k + 1 - at[0]]

    out = jax.ShapeDtypeStruct((slabs // 2, rows, tokens), BF)
    return pl.pallas_call(
        kernel,
        grid=(1,),
        out_shape=[out, out],
        in_specs=[pl.BlockSpec(memory_space=pltpu.SMEM), whole_block(a)],
        out_specs=[whole_block(out)] * 2,
        scratch_shapes=[pltpu.VMEM((slabs, rows, tokens), BF)],
        compiler_params=pltpu.CompilerParams(vmem_limit_bytes=60 * 2**20),
        cost_estimate=LONG,
        name="turn",
    )(places.at_c.astype(jnp.int32).reshape(1), a)


def chip_stacks(places, turned, parts):
    slabs, rows, tokens = turned[0].shape
    z, count = places.z, places.narrow
    joined = len(parts[0]) < count
    columns = parts[0][0].shape[1] // (count if joined else 1)
    chunk = chunk_of(columns, 900)
    masks = [places.masks(0), places.masks(1)]
    half = len(masks[0]) // 2

    def kernel(at, own_ref, got_ref, *refs):
        d_refs, (keep_ref, send_ref, product) = refs[: 2 * count], refs[2 * count :]
        for i in range(count):
            whole = mm(own_ref[...], d_refs[i][...], ((1,), (0,)))
            whole += mm(got_ref[...], d_refs[count + i][...], ((1,), (0,)))
            for k in range(slabs):
                product[i, k] = whole[k * rows : (k + 1) * rows].astype(BF)
        core, y, x = at[0], at[1], at[2]
        for j in range(2 * half):
            dy = jnp.where(core == 0, masks[0][j][0], masks[1][j][0])
            dx = jnp.where(core == 0, masks[0][j][1], masks[1][j][1])
            out = keep_ref if j < half else send_ref
            for k in range(z):
                out[j % half, k] = product[x ^ dx, k * 2 + (y ^ dy)]

    at = jnp.stack([places.at_c, places.at_y, places.x]).astype(jnp.int32)
    flat = [a.reshape(slabs * rows, tokens) for a in turned]
    out = pl.BlockSpec((half, z, rows, chunk), lambda i: (0, 0, 0, i))
    specs = [
        pl.BlockSpec((tokens, chunk), lambda i, j=j: (0, j * (columns // chunk) + i if joined else i))
        for j in range(count)
    ]
    args = [p for part in parts for p in (list(part) * count if joined else part)]
    return pl.pallas_call(
        kernel,
        grid=(-(-columns // chunk),),
        out_shape=[jax.ShapeDtypeStruct((half, z, rows, columns), BF)] * 2,
        in_specs=[pl.BlockSpec(memory_space=pltpu.SMEM)] + [whole_block(a) for a in flat] + specs * 2,
        out_specs=[out, out],
        scratch_shapes=[pltpu.VMEM((count, slabs, rows, chunk), BF)],
        compiler_params=pltpu.CompilerParams(vmem_limit_bytes=60 * 2**20),
        cost_estimate=LONG,
        name="chip_stacks",
    )(at, *flat, *args)


def join(parts):
    counts = [p.shape[0] for p in parts]

    def kernel(*refs):
        first = 0
        for ref, count in zip(refs[:-1], counts):
            refs[-1][first : first + count] = ref[...]
            first += count

    shape = jax.ShapeDtypeStruct((sum(counts), *parts[0].shape[1:]), BF)
    return pl.pallas_call(
        kernel,
        grid=(1,),
        out_shape=shape,
        in_specs=[whole_block(p) for p in parts],
        out_specs=whole_block(shape),
        compiler_params=pltpu.CompilerParams(vmem_limit_bytes=60 * 2**20),
        cost_estimate=SHORT,
        name="join",
    )(*parts)


def add_stacks(terms, half):
    shape = (half, *terms[0].shape[1:])

    def kernel(*refs):
        total = refs[0][...].astype(F32)
        for ref in refs[1:-1]:
            total += ref[...].astype(F32)
        refs[-1][...] = total.astype(BF)

    deep = 2 if shape[1] % 2 == 0 else 1
    block = (1, deep, *shape[2:])
    return pl.pallas_call(
        kernel,
        grid=(half, shape[1] // deep),
        out_shape=jax.ShapeDtypeStruct(shape, BF),
        in_specs=[pl.BlockSpec(block, lambda i, j: (half + i, j, 0, 0))] * len(terms),
        out_specs=pl.BlockSpec(block, lambda i, j: (i, j, 0, 0)),
        compiler_params=pltpu.CompilerParams(vmem_limit_bytes=60 * 2**20),
        cost_estimate=SHORT,
        name="add_stacks",
    )(*terms)


def add_slabs(places, terms, z_terms, first, count, divisor=None):
    rows, columns = terms[0].shape[2:]
    late = [(at, term) for at, term in z_terms if at <= first < at + term.shape[0]]

    def kernel(at_ref, *refs):
        out, refs = refs[-1], refs[:-1]
        total = None
        for i, ref in enumerate(refs[: len(terms) + len(late)]):
            value = (ref[0, 0] if i < len(terms) else ref[0]).astype(F32)
            total = value if total is None else total + value
        if divisor is not None:
            total = total / refs[-1][0]
        out[0] = total.astype(out.dtype)

    in_specs = [
        pl.BlockSpec((1, 1, rows, columns), lambda i, at: (0, at[0] ^ (first + i), 0, 0))
        for _ in terms
    ]
    in_specs += [
        pl.BlockSpec((1, rows, columns), lambda i, at, f=first - at_first: (f + i, 0, 0))
        for at_first, _ in late
    ]
    args = [*terms, *[term for _, term in late]]
    if divisor is not None:
        in_specs.append(pl.BlockSpec(memory_space=pltpu.SMEM))
        args.append(divisor.reshape(1))
    kind = BF if divisor is None else F32
    return pl.pallas_call(
        kernel,
        grid_spec=pltpu.PrefetchScalarGridSpec(
            num_scalar_prefetch=1,
            grid=(count,),
            in_specs=in_specs,
            out_specs=pl.BlockSpec((1, rows, columns), lambda i, at: (i, 0, 0)),
        ),
        out_shape=jax.ShapeDtypeStruct((count, rows, columns), kind),
        compiler_params=pltpu.CompilerParams(vmem_limit_bytes=60 * 2**20),
        cost_estimate=SHORT,
        name="add_slabs",
    )(places.at_z.astype(jnp.int32).reshape(1), *args)


class Slots:
    def __init__(self, places):
        self.places = places
        self.before, self.now, self.ready = (), [], []

    def tie(self, value):
        return after(value, *self.before, *self.ready)

    def note(self, *values):
        self.now += values

    def next(self, *values):
        self.note(*values)
        self.before, self.now, self.ready = tuple(self.now), [], []

    def send(self, value, flip):
        value = after(value, *self.before)
        self.ready.append(value)
        return self.follow(value, flip)

    def follow(self, value, flip):
        other = self.places.swap(value, flip)
        self.note(other)
        return other


class Gather:
    def __init__(self, slots, shard):
        self.slots, self.places = slots, slots.places
        self.rows = self.places.wide * shard.shape[0]
        self.parts = [shard[None]]

    def all_z(self):
        for d in range(1, self.places.z):
            self.parts.append(self.slots.send(self.parts[0], lambda core: (d, 0, 0, 0)))

    def step(self, i, exchange):
        joined = join([p.reshape(-1, *p.shape[-2:]) for p in self.parts])
        self.parts = [joined]
        self.parts.append(exchange(joined, self.places.step_flip(i)))

    def first(self):
        for i in range(len(self.places.orders[0]) - 1):
            self.step(i, self.slots.follow if i else self.slots.send)

    def last(self):
        self.step(len(self.places.orders[0]) - 1, self.slots.send)

    def cores(self):
        parts = [p.reshape(-1, self.places.z, *p.shape[-2:]) for p in self.parts]
        self.parts = parts + [self.slots.send(p, lambda core: (0, 0, 1, 0)) for p in parts]

    def whole(self):
        whole = assemble(self.places, self.slots.tie(tuple(self.parts)))
        return whole.reshape(-1, self.rows, whole.shape[-1])


class Scatter:
    def __init__(self, slots, a, parts):
        self.slots, self.places = slots, slots.places
        stack, self.to_core = grad_stacks(self.places, a, parts)
        self.terms, self.z_terms, self.half = [stack], [], stack.shape[0]

    def cores(self, exchange):
        self.terms.append(exchange(self.to_core, lambda core: (0, 0, 1, 0)))

    def hold(self):
        self.terms[0] = self.slots.tie(self.terms[0])

    def step(self, i, exchange):
        self.half //= 2
        send = add_stacks(self.terms, self.half)
        self.terms.append(exchange(send, self.places.step_flip(i)))

    def first(self):
        self.step(len(self.places.orders[0]) - 1, self.slots.send)

    def last(self):
        for i in reversed(range(len(self.places.orders[0]) - 1)):
            chained = i < len(self.places.orders[0]) - 2
            self.step(i, self.slots.follow if chained else self.slots.send)

    def step_z(self, *bits):
        for i, bit in enumerate(bits):
            exchange = self.slots.follow if i else self.slots.send
            send = add_slabs(self.places, self.terms, self.z_terms, bit, bit)
            self.z_terms.append((0, exchange(send, lambda core: (bit, 0, 0, 0))))

    def direct_z(self):
        for d in reversed(range(1, self.places.z)):
            send = add_slabs(self.places, self.terms, self.z_terms, d, 1)
            self.z_terms.append((0, self.slots.send(send, lambda core: (d, 0, 0, 0))))

    def result(self, divisor):
        divisor = self.slots.tie(divisor)
        return add_slabs(self.places, self.terms, self.z_terms, 0, 1, divisor)[0]


class ChipScatter(Scatter):
    def __init__(self, slots, turned, parts):
        self.slots, self.places = slots, slots.places
        keep, self.ready = chip_stacks(self.places, turned, parts)
        self.terms, self.z_terms, self.half = [keep], [], keep.shape[0]

    def first(self):
        flip = self.places.step_flip(len(self.places.orders[0]) - 1)
        self.terms.append(self.slots.send(self.ready, flip))


def to_core(core):
    return (0, 0, 1, 0)


def dot(a, b, dims, out=F32):
    return lax.dot_general(a, b, (dims, ((), ())), preferred_element_type=F32).astype(out)


def split(a, count):
    width = a.shape[1] // count
    return [a[:, n * width : (n + 1) * width] for n in range(count)]


def on_device(
    inputs,
    cotangent,
    class_ids,
    step_ids,
    image_counts,
    w_qkv,
    w_out,
    w_gate,
    w_up,
    w_down,
    ada_weight,
    ada_bias,
    class_table,
    norm_gains,
):
    places = Places()
    wide, narrow, at_w, at_n = places.wide, places.narrow, places.w, places.x
    images, length, width = inputs.shape
    tables, sums = head_tables(length), head_sums()
    gains = jnp.tile(norm_gains, (1, H))
    local_count = image_counts[0]

    tokens = images * length

    def flat(v):
        return v.reshape(tokens, -1)

    def deep(v):
        return v.reshape(images, length, -1)

    t = Slots(places)
    z_low, z_high = places.z_bits[:1], places.z_bits[1:]
    z_down = z_high[::-1]
    qkv, out, gate, up, down = [
        Gather(t, shard) for shard in (w_qkv, w_out, w_gate, w_up, w_down)
    ]

    qkv.all_z()
    small = [class_ids, step_ids, image_counts, ada_bias]
    small = jnp.concatenate([v.astype(F32) for v in small])[None]
    bits = places.all_bits()
    small = places.gather_bits(places.open_small(small), bits)
    small = small.reshape(wide * narrow, -1)
    t.next(small)

    qkv.first()
    out.all_z()
    small = t.tie(small)
    ids = small[:, : 2 * images].reshape(-1, 2, images).transpose(0, 2, 1).reshape(-1, 2)
    ids = ids.astype(jnp.int32)
    real_count = jnp.sum(small[:, 2 * images])
    bias = small[:, 2 * images + 1 :].reshape(-1)
    rows_here, cols_here = class_table.shape
    class_hot = ids[:, :1] - at_n * rows_here == jnp.arange(rows_here, dtype=jnp.int32)[None, :]
    picked = dot(class_hot.astype(BF), class_table, ((1,), (0,)))
    column = at_w * cols_here + jnp.arange(cols_here, dtype=jnp.int32)
    half_width = width // 2
    frequency = jnp.exp(-math.log(10000.0) * (column % half_width).astype(F32) / half_width)
    angles = ids[:, 1:].astype(F32) * frequency[None, :]
    wave = jnp.where(column[None, :] < half_width, jnp.cos(angles), jnp.sin(angles))
    condition = places.add_narrow(picked) + wave
    cond_act = jax.nn.silu(condition).astype(BF)
    t.next(cond_act)

    qkv.last()
    gate.all_z()
    mod_part = dot(t.tie(cond_act), ada_weight, ((1,), (0,)))
    mod_part = places.scatter_chip_row(mod_part.reshape(wide, narrow, images, -1))
    t.next(mod_part, *tables, sums)

    qkv.cores()
    out.first()
    gate.first()
    mod_part = places.trade_narrow(places.scatter_z(t.tie(mod_part)))
    t.next(mod_part)

    out.last()
    gate.last()
    up.all_z()
    qkv_b = qkv.whole()
    modulation = t.tie(mod_part).transpose(1, 0, 2).reshape(images, -1) + bias
    pieces = modulation.reshape(images, 6, width)
    normed, _ = layer_norm(inputs.astype(F32))
    attn_in = flat((normed * (1.0 + pieces[:, 1:2]) + pieces[:, 0:1]).astype(BF))
    t.next(attn_in, qkv_b)

    out.cores()
    gate.cores()
    up.first()
    packed = project(t.tie(attn_in), qkv_b)
    attn_turned, attn_other = turn(places, t.tie(attn_in))
    t.next(*packed, attn_other)

    attn_turned = [attn_turned, t.send(attn_other, to_core)]
    up.last()
    down.all_z()
    packed = t.tie(packed)
    queries, key_rows, value_rows, mixed = attention_forward(packed, gains, tables, sums, images)
    slot_real = (jnp.arange(images, dtype=jnp.int32) < local_count).astype(F32)
    grad_y = cotangent.astype(F32) * slot_real[:, None, None]
    d_mlp = split(flat((pieces[:, 5:6] * grad_y).astype(BF)), narrow)
    t.next(mixed, *d_mlp)

    up.cores()
    down.first()
    out_b = out.whole()
    attn_out, hidden_one, mlp_in = attention_tail(mixed, out_b, flat(inputs), pieces, images)
    gate_b = gate.whole()[0]
    mlp_turned, mlp_other = turn(places, mlp_in)
    t.next(mlp_in, gate_b, mlp_other)

    mlp_turned = [mlp_turned, t.send(mlp_other, to_core)]
    down.last()
    up_b = up.whole()[0]
    gate_val, up_val, hidden_mid = gated(mlp_in, gate_b, up_b)
    t.next(hidden_mid)

    down.cores()
    g_down = Scatter(t, t.tie(hidden_mid), d_mlp)
    t.next(g_down.to_core)

    g_down.cores(t.send)
    down_b = down.whole()
    t.next(down_b)

    g_down.first()
    d_gate, d_up, d_mlp_in = gated_back(t.tie(d_mlp), down_b, gate_val, up_val, gate_b, up_b)
    t.next(d_mlp_in)

    g_down.last()
    d_gate_got = t.send(d_gate, to_core)
    d_up_got = t.send(d_up, to_core)
    d_hidden, d_mixed, sums_b, *d_attn = middle_back(
        t.tie(d_mlp_in), hidden_one, attn_out, flat(cotangent), pieces, out_b, image_counts, images
    )
    g_gate = ChipScatter(t, mlp_turned, [[after(d_gate, d_mixed)], [d_gate_got]])
    t.next(g_gate.ready)

    g_gate.first()
    g_down.hold()
    g_down.step_z(*z_down)
    g_up = ChipScatter(t, mlp_turned, [[t.tie(d_up)], [d_up_got]])
    g_out = Scatter(t, mixed, t.tie(d_attn))
    t.next(g_up.ready, g_out.to_core)

    g_up.first()
    g_gate.last()
    g_out.cores(t.send)
    g_down.step_z(*z_low)
    d_packed, gain_terms = attention_backward(
        packed, queries, key_rows, value_rows, t.tie(d_mixed), gains, tables, sums, images
    )
    t.next(*d_packed)

    d_packed_got = [
        t.send(d.reshape(-1, 8, d.shape[1]), to_core).reshape(d.shape) for d in d_packed
    ]
    for grad in (g_up, g_out, g_gate):
        grad.hold()
    g_up.last()
    g_out.first()
    g_gate.step_z(*z_down)
    g_qkv = ChipScatter(t, attn_turned, [t.tie(d_packed), d_packed_got])
    block_output, sums_gate = block_tail(
        after(hidden_mid, g_qkv.ready),
        down_b,
        hidden_one,
        flat(cotangent),
        pieces,
        image_counts,
        images,
    )
    t.next(sums_gate)

    g_qkv.first()
    for grad in (g_out, g_up, g_gate):
        grad.hold()
    g_out.last()
    g_up.step_z(*z_down)
    g_gate.step_z(*z_low)
    d_tokens, sums_a = block_head_back(
        t.tie(d_packed), d_hidden, flat(inputs), pieces, qkv_b, images
    )
    grad_gains = gain_terms.sum(0).reshape(2, H, HD).sum(1).reshape(1, -1)
    gains_high = grad_gains.astype(BF)
    gains_low = (grad_gains - gains_high.astype(F32)).astype(BF)
    rest = jnp.zeros((images - 2, 2 * HD), BF)
    grad_gains = jnp.concatenate([gains_high, gains_low, rest], axis=0)
    d_modulation = jnp.concatenate([sums_a, sums_b[:, 2:], sums_b[:, :2], sums_gate], axis=1)
    d_modulation = d_modulation.astype(BF).reshape(images, -1)
    d_modulation = jnp.concatenate([d_modulation, grad_gains], axis=1)
    t.next(d_modulation)

    g_qkv.last()
    for grad in (g_up, g_out):
        grad.hold()
    g_up.step_z(*z_low)
    g_out.step_z(*z_down)
    d_all = places.open_small(t.tie(d_modulation))
    d_all = places.gather_bits(d_all, bits[: len(places.z_bits)])
    t.next(d_all)

    g_qkv.direct_z()
    g_out.step_z(*z_low)
    d_all = places.gather_bits(t.tie(d_all), bits[len(places.z_bits) :])
    d_all = d_all.reshape(wide * narrow * images, -1)
    gain_sum = d_all[:, 6 * width : 6 * width + 2 * HD].astype(F32)
    gain_sum = jnp.sum(gain_sum, axis=0).reshape(2, HD) / real_count
    d_mod = d_all[:, : 6 * width]
    ada_cols = ada_weight.shape[1]
    d_mod_here = lax.dynamic_slice_in_dim(d_mod, at_n * ada_cols, ada_cols, 1)
    g_ada = dot(cond_act, d_mod_here, ((0,), (0,))) / real_count
    bias_cols = ada_bias.shape[0]
    bias_at = (at_w * narrow + at_n) * bias_cols
    g_bias = jnp.sum(lax.dynamic_slice_in_dim(d_mod, bias_at, bias_cols, 1).astype(F32), axis=0)
    g_bias = g_bias / real_count
    d_cond_act = places.add_narrow(dot(d_mod_here, ada_weight, ((1,), (1,))))
    cond_sigmoid = jax.nn.sigmoid(condition)
    d_condition = d_cond_act * cond_sigmoid * (1.0 + condition * (1.0 - cond_sigmoid))
    g_table = jnp.dot(class_hot.astype(F32).T, d_condition, precision=HIGHEST) / real_count
    r_out, r_gate, r_up, r_down = [g.result(real_count) for g in (g_out, g_gate, g_up, g_down)]
    at, late = g_qkv.z_terms[-1]
    g_qkv.z_terms[-1] = (at, after(late, g_ada, g_table, r_out, r_gate, r_up, r_down))
    r_qkv = g_qkv.result(real_count)

    return (
        deep(block_output),
        deep(d_tokens),
        r_qkv,
        r_out,
        r_gate,
        r_up,
        r_down,
        g_ada,
        g_bias,
        g_table,
        gain_sum,
    )


def solution(mesh):
    split = P("wide", "narrow")
    images = P(ALL, None, None)
    return jax.shard_map(
        on_device,
        mesh=mesh,
        in_specs=(
            images,
            images,
            P(ALL),
            P(ALL),
            P(ALL),
            split,
            split,
            split,
            split,
            split,
            split,
            P(ALL),
            P("narrow", "wide"),
            P(),
        ),
        out_specs=(
            images,
            images,
            split,
            split,
            split,
            split,
            split,
            split,
            P(ALL),
            P("narrow", "wide"),
            P(),
        ),
        check_vma=False,
    )
```

```python
import math

import jax
import jax.numpy as jnp
from jax import lax
from jax.experimental import pallas as pl
from jax.experimental.pallas import tpu as pltpu
from jax.sharding import PartitionSpec as P

H = 16
HD = 72
CLASSES = 1000
GRID = 16

EPSILON = 1e-06
HIGHEST = lax.Precision.HIGHEST
ALL = ("wide", "narrow")
BF = jnp.bfloat16
F32 = jnp.float32
LONG = pl.CostEstimate(flops=10**12, bytes_accessed=1, transcendentals=0)
SHORT = pl.CostEstimate(flops=1, bytes_accessed=1, transcendentals=0)


def layer_norm(values):
    centre = values - jnp.mean(values, axis=-1, keepdims=True)
    inverse = lax.rsqrt(jnp.mean(centre * centre, axis=-1, keepdims=True) + EPSILON)
    return (centre * inverse, inverse)


def head_tables(length):
    quarter = HD // 4
    lane = jnp.arange(H * HD, dtype=jnp.int32) % HD
    frequency = 10000.0 ** (-(lane % quarter).astype(F32) / quarter)
    patch = jnp.arange(length, dtype=jnp.int32)[:, None]
    place = jnp.where(lane[None, :] < 2 * quarter, patch // GRID, patch % GRID)
    angles = place.astype(F32) * frequency[None, :]
    cosine, sine = jnp.cos(angles), jnp.sin(angles)
    first = (lane // quarter % 2 == 0)[None, :]
    return [cosine, jnp.where(first, -sine, 0.0), jnp.where(first, 0.0, sine)]


def head_sums():
    lane = lax.broadcasted_iota(jnp.int32, (H * HD, 128), 0) // HD
    return (lane == lax.broadcasted_iota(jnp.int32, (H * HD, 128), 1)).astype(BF)


def exact_dot(a, b, dims):
    total = None
    for _ in range(3):
        term = a.astype(BF)
        a = a - term.astype(F32)
        part = lax.dot_general(term, b, (dims, ((), ())), preferred_element_type=F32)
        total = part if total is None else total + part
    return total


def head_mean(values, sums):
    mean = exact_dot(values, sums, ((1,), (0,))) * (1.0 / HD)
    return exact_dot(mean, sums, ((1,), (1,)))


def shifted(values, cosine, above, below, sign):
    quarter, width = HD // 4, values.shape[1]
    up = pltpu.roll(values, width - quarter, 1)
    down = pltpu.roll(values, quarter, 1)
    return values * cosine + sign * (up * above + down * below)


def window(head):
    first, last = head * HD // 128 * 128, ((head + 1) * HD + 127) // 128 * 128
    return first, last


def only(values, head):
    first, last = window(head)
    part = values[:, first:last]
    lane = first + lax.broadcasted_iota(jnp.int32, (1, last - first), 1)
    mine = ((lane >= head * HD) & (lane < (head + 1) * HD)).astype(values.dtype)
    return part * mine


class Tiles:
    def __init__(self, store):
        self.store, self.held = store, {}

    def add(self, head, value):
        first, last = window(head)
        for tile in range(first // 128, last // 128):
            part = value[:, tile * 128 - first : tile * 128 - first + 128]
            self.held[tile] = self.held[tile] + part if tile in self.held else part
        done = (head + 1) * HD // 128
        for tile in sorted(self.held):
            if tile < done or head == H - 1:
                self.store(tile * 128, self.held.pop(tile))


def mm(a, b, dims):
    return lax.dot_general(a, b, (dims, ((), ())), preferred_element_type=F32)


def only_turned(values, head):
    first, last = window(head)
    part = values[first:last, :]
    row = first + lax.broadcasted_iota(jnp.int32, (last - first, 1), 0)
    mine = ((row >= head * HD) & (row < (head + 1) * HD)).astype(values.dtype)
    return part * mine


def softmax_of(queries, keys_turned, head):
    first, last = window(head)
    scores = mm(only(queries, head), keys_turned[first:last, :], ((1,), (0,))) * (HD ** (-0.5))
    exponent = jnp.exp(scores - jnp.max(scores, axis=1, keepdims=True))
    return exponent / jnp.sum(exponent, axis=1, keepdims=True)


def attention_forward(packed, gains, tables, sums, images):
    tokens = packed[0].shape[0]
    length, width, blocks = tokens // images, H * HD, len(packed)

    def kernel(*refs):
        parts, refs = refs[:blocks], refs[blocks:]
        gain, cosine, above, below, sums_ref, q_ref, k_ref, v_ref, mixed_ref, k_turned = refs
        whole = jnp.concatenate([p[...] for p in parts], axis=1)
        sums_here = sums_ref[...]
        for i, ref in enumerate((q_ref, k_ref)):
            raw = whole[:, i * width : (i + 1) * width]
            normed = raw * lax.rsqrt(head_mean(raw * raw, sums_here) + EPSILON)
            turned = shifted(normed * gain[i : i + 1, :], cosine[...], above[...], below[...], 1.0)
            ref[...] = turned.astype(BF)
        v_ref[...] = whole[:, 2 * width :].astype(BF)

        def store(first, value):
            mixed_ref[:, first : first + 128] = value.astype(BF)

        k_turned[...] = k_ref[...].T
        mixed = Tiles(store)
        for head in range(H):
            attention = softmax_of(q_ref, k_turned, head).astype(BF)
            mixed.add(head, mm(attention, only(v_ref, head), ((1,), (0,))))

    def rows(n):
        return pl.BlockSpec((length, n), lambda i: (i, 0))

    def all_of(a):
        return pl.BlockSpec(a.shape, lambda i: (0, 0))

    out = jax.ShapeDtypeStruct((tokens, width), BF)
    return pl.pallas_call(
        kernel,
        grid=(images,),
        out_shape=[out] * 4,
        in_specs=[rows(p.shape[1]) for p in packed] + [all_of(a) for a in (gains, *tables, sums)],
        out_specs=[rows(width)] * 4,
        scratch_shapes=[pltpu.VMEM((width, length), BF)],
        compiler_params=pltpu.CompilerParams(vmem_limit_bytes=60 * 2**20),
        cost_estimate=LONG,
        name="attention_forward",
    )(*packed, gains, *tables, sums)


def attention_backward(packed, queries, keys, values, d_mixed, gains, tables, sums, images):
    tokens = queries.shape[0]
    length, width, blocks = tokens // images, H * HD, len(packed)
    block = packed[0].shape[1]

    def kernel(*refs):
        parts, refs = refs[:blocks], refs[blocks:]
        q_ref, k_ref, v_ref, d_ref, gain, cosine, above, below, sums_ref = refs[:9]
        outs, refs = refs[9 : 9 + blocks], refs[9 + blocks :]
        gain_ref, d_q_turned, d_k, d_v, q_turned, k_turned, d_turned = refs

        def store_to(ref):
            def store(first, value):
                ref[:, first : first + 128] = value

            return store

        for ref, turned in ((q_ref, q_turned), (k_ref, k_turned), (d_ref, d_turned)):
            turned[...] = ref[...].T
        all_k, all_v = [Tiles(store_to(ref)) for ref in (d_k, d_v)]
        rows_q = {}
        for head in range(H):
            first, last = window(head)
            scores = mm(only(k_ref, head), q_turned[first:last, :], ((1,), (0,))) * (HD ** (-0.5))
            exponent = jnp.exp(scores - jnp.max(scores, axis=0, keepdims=True))
            soft = exponent / jnp.sum(exponent, axis=0, keepdims=True)
            all_v.add(head, mm(soft.astype(BF), only(d_ref, head), ((1,), (0,))))
            d_soft = mm(only(v_ref, head), d_turned[first:last, :], ((1,), (0,)))
            inner = jnp.sum(soft * d_soft, axis=0, keepdims=True)
            d_scores = (soft * (d_soft - inner) * (HD ** (-0.5))).astype(BF)
            all_k.add(head, mm(d_scores, only(q_ref, head), ((1,), (0,))))
            part = mm(only_turned(k_turned, head), d_scores, ((1,), (0,)))
            for tile in range(first // 128, last // 128):
                rows = part[tile * 128 - first : tile * 128 - first + 128]
                rows_q[tile] = rows_q[tile] + rows if tile in rows_q else rows
            for tile in sorted(rows_q):
                if tile < (head + 1) * HD // 128 or head == H - 1:
                    d_q_turned[tile * 128 : tile * 128 + 128, :] = rows_q.pop(tile)
        whole = jnp.concatenate([p[...] for p in parts], axis=1)
        sums_here = sums_ref[...]
        done = []
        for i, value in enumerate((d_q_turned[...].T, d_k[...])):
            raw = whole[:, i * width : (i + 1) * width]
            inverse = lax.rsqrt(head_mean(raw * raw, sums_here) + EPSILON)
            normed = raw * inverse
            scaled = shifted(value, cosine[...], above[...], below[...], -1.0)
            gain_ref[0, i : i + 1, :] = jnp.sum(scaled * normed, axis=0, keepdims=True)
            incoming = scaled * gain[i : i + 1, :]
            mean = head_mean(incoming * normed, sums_here)
            done.append((inverse * (incoming - normed * mean)).astype(BF))
        done.append(d_v[...].astype(BF))
        done = jnp.concatenate(done, axis=1)
        for j, out in enumerate(outs):
            out[...] = done[:, j * block : (j + 1) * block]

    def rows(n):
        return pl.BlockSpec((length, n), lambda i: (i, 0))

    def all_of(a):
        return pl.BlockSpec(a.shape, lambda i: (0, 0))

    outs = pl.pallas_call(
        kernel,
        grid=(images,),
        out_shape=[jax.ShapeDtypeStruct((tokens, block), BF)] * blocks
        + [jax.ShapeDtypeStruct((images, 2, width), F32)],
        in_specs=[rows(block)] * blocks
        + [rows(width)] * 4
        + [all_of(a) for a in (gains, *tables, sums)],
        out_specs=[rows(block)] * blocks + [pl.BlockSpec((1, 2, width), lambda i: (i, 0, 0))],
        scratch_shapes=[pltpu.VMEM((width, length), F32)]
        + [pltpu.VMEM((length, width), F32)] * 2
        + [pltpu.VMEM((width, length), BF)] * 3,
        compiler_params=pltpu.CompilerParams(vmem_limit_bytes=60 * 2**20),
        cost_estimate=LONG,
        name="attention_backward",
    )(*packed, queries, keys, values, d_mixed, gains, *tables, sums)
    return outs[:blocks], outs[blocks]

def whole_block(a):
    return pl.BlockSpec(a.shape, lambda *i: (0,) * a.ndim)


def chunk_of(columns, most):
    count = -(-columns // most)
    return columns if count == 1 else -(-columns // (128 * count)) * 128


def project(a, blocks):
    tokens, depth = a.shape
    count, _, columns = blocks.shape
    chunk = chunk_of(columns, 640)

    def kernel(a_ref, *refs):
        for w_ref, out_ref in zip(refs[:count], refs[count:]):
            out_ref[...] = mm(a_ref[...], w_ref[...], ((1,), (0,)))

    return pl.pallas_call(
        kernel,
        grid=(-(-columns // chunk),),
        out_shape=[jax.ShapeDtypeStruct((tokens, columns), F32)] * count,
        in_specs=[whole_block(a)]
        + [pl.BlockSpec((None, depth, chunk), lambda i, j=j: (j, 0, i)) for j in range(count)],
        out_specs=[pl.BlockSpec((tokens, chunk), lambda i: (0, i))] * count,
        compiler_params=pltpu.CompilerParams(vmem_limit_bytes=60 * 2**20),
        cost_estimate=LONG,
        name="project",
    )(a, *[blocks] * count)


def gated(a, w_gate, w_up):
    tokens, depth = a.shape
    columns = w_gate.shape[1]
    chunk = 512

    def kernel(a_ref, g_ref, u_ref, gate_ref, up_ref, mid_ref):
        gate = mm(a_ref[...], g_ref[...], ((1,), (0,)))
        up = mm(a_ref[...], u_ref[...], ((1,), (0,)))
        gate_ref[...] = gate
        up_ref[...] = up
        mid_ref[...] = (gate * jax.nn.sigmoid(gate) * up).astype(BF)

    weight = pl.BlockSpec((depth, chunk), lambda i: (0, i))
    out = pl.BlockSpec((tokens, chunk), lambda i: (0, i))
    return pl.pallas_call(
        kernel,
        grid=(columns // chunk,),
        out_shape=[jax.ShapeDtypeStruct((tokens, columns), t) for t in (F32, F32, BF)],
        in_specs=[whole_block(a), weight, weight],
        out_specs=[out] * 3,
        compiler_params=pltpu.CompilerParams(vmem_limit_bytes=60 * 2**20),
        cost_estimate=LONG,
        name="gated",
    )(a, w_gate, w_up)


def gated_back(d_parts, down, gate_val, up_val, w_gate, w_up):
    tokens, columns = gate_val.shape
    depth, count, chunk = w_gate.shape[0], down.shape[0], 512

    def kernel(*refs):
        d_refs, w_refs, refs = refs[:count], refs[count : 2 * count], refs[2 * count :]
        gate_ref, up_ref, g_ref, u_ref, d_gate_ref, d_up_ref, in_ref = refs
        d_mid = None
        for d_ref, w_ref in zip(d_refs, w_refs):
            term = mm(d_ref[...], w_ref[...], ((1,), (1,)))
            d_mid = term if d_mid is None else d_mid + term
        gate, up = gate_ref[...], up_ref[...]
        sigmoid = jax.nn.sigmoid(gate)
        silu = gate * sigmoid
        d_gate = (d_mid * up * (sigmoid + silu * (1.0 - sigmoid))).astype(BF)
        d_up = (d_mid * silu).astype(BF)
        d_gate_ref[...] = d_gate
        d_up_ref[...] = d_up
        term = mm(d_gate, g_ref[...], ((1,), (1,))) + mm(d_up, u_ref[...], ((1,), (1,)))

        @pl.when(pl.program_id(0) == 0)
        def _():
            in_ref[...] = term

        @pl.when(pl.program_id(0) > 0)
        def _():
            in_ref[...] += term

    width = down.shape[2]
    token = pl.BlockSpec((tokens, chunk), lambda i: (0, i))
    weight = pl.BlockSpec((depth, chunk), lambda i: (0, i))
    return pl.pallas_call(
        kernel,
        grid=(columns // chunk,),
        out_shape=[jax.ShapeDtypeStruct((tokens, columns), BF)] * 2
        + [jax.ShapeDtypeStruct((tokens, depth), F32)],
        in_specs=[whole_block(d) for d in d_parts]
        + [pl.BlockSpec((None, chunk, width), lambda i, j=j: (j, i, 0)) for j in range(count)]
        + [token, token, weight, weight],
        out_specs=[token, token, pl.BlockSpec((tokens, depth), lambda i: (0, 0))],
        compiler_params=pltpu.CompilerParams(vmem_limit_bytes=60 * 2**20),
        cost_estimate=LONG,
        name="gated_back",
    )(*d_parts, *[down] * count, gate_val, up_val, w_gate, w_up)


def normal(values):
    centre = values - jnp.mean(values, axis=1, keepdims=True)
    inverse = lax.rsqrt(jnp.mean(centre * centre, axis=1, keepdims=True) + EPSILON)
    return centre * inverse, inverse


def normal_back(gradient, normed, inverse):
    mean = jnp.mean(gradient, axis=1, keepdims=True)
    return inverse * (
        gradient - mean - normed * jnp.mean(gradient * normed, axis=1, keepdims=True)
    )


def per_image(kernel, images, by_image, whole, outs, vmem, name, scalar=None):
    def spec(rows, rest):
        return pl.BlockSpec((rows, *rest), lambda i: (i,) + (0,) * len(rest))

    in_specs = [spec(a.shape[0] // images, a.shape[1:]) for a in by_image]
    in_specs += [whole_block(a) for a in whole]
    args = [*by_image, *whole]
    if scalar is not None:
        in_specs.append(pl.BlockSpec(memory_space=pltpu.SMEM))
        args.append(scalar)
    return pl.pallas_call(
        kernel,
        grid=(images,),
        out_shape=[jax.ShapeDtypeStruct((images * rows, *rest), t) for rows, rest, t in outs],
        in_specs=in_specs,
        out_specs=[spec(rows, rest) for rows, rest, _ in outs],
        compiler_params=pltpu.CompilerParams(vmem_limit_bytes=60 * 2**20),
        cost_estimate=LONG,
        name=name,
    )(*args)


def attention_tail(mixed, out_b, inputs, pieces, images):
    tokens, width = mixed.shape

    def kernel(mixed_ref, in_ref, piece, *refs):
        w_ref, attn_ref, hidden_ref, mlp_ref = refs
        attn = [mm(mixed_ref[...], w_ref[j], ((1,), (0,))) for j in range(out_b.shape[0])]
        attn = jnp.concatenate(attn, axis=1)
        attn_ref[...] = attn
        hidden = in_ref[...].astype(F32) + piece[0, 2:3, :] * attn
        hidden_ref[...] = hidden
        normed, _ = normal(hidden)
        mlp_ref[...] = (normed * (1.0 + piece[0, 4:5, :]) + piece[0, 3:4, :]).astype(BF)

    rows = tokens // images
    outs = [(rows, (width,), F32), (rows, (width,), F32), (rows, (width,), BF)]
    return per_image(kernel, images, [mixed, inputs, pieces], [out_b], outs, 32, "attention_tail")


def block_tail(hidden_mid, down_b, hidden_one, cotangent, pieces, count, images):
    tokens, width = hidden_one.shape

    def kernel(mid_ref, hidden_ref, cot_ref, piece, *refs):
        w_ref, count_ref, out_ref, gate_ref = refs
        mlp = [mm(mid_ref[...], w_ref[j], ((1,), (0,))) for j in range(down_b.shape[0])]
        mlp = jnp.concatenate(mlp, axis=1)
        out_ref[...] = (hidden_ref[...] + piece[0, 5:6, :] * mlp).astype(BF)
        real = (pl.program_id(0) < count_ref[0]).astype(F32)
        grad = cot_ref[...].astype(F32) * real
        gate_ref[0] = jnp.sum(grad * mlp, axis=0, keepdims=True)

    rows = tokens // images
    outs = [(rows, (width,), BF), (1, (1, width), F32)]
    by_image = [hidden_mid, hidden_one, cotangent, pieces]
    return per_image(kernel, images, by_image, [down_b], outs, 40, "block_tail", count)


def middle_back(d_mlp_in, hidden_one, attn_out, cotangent, pieces, out_b, count, images):
    tokens, width = d_mlp_in.shape
    blocks, _, columns = out_b.shape

    def kernel(in_ref, hidden_ref, attn_ref, cot_ref, piece, *refs):
        w_ref, count_ref, refs = refs[0], refs[1], refs[2:]
        d_hidden_ref, d_mixed_ref, sums_ref = refs[:3]
        d_in = in_ref[...]
        normed, inverse = normal(hidden_ref[...])
        sums_ref[0, 0:1] = jnp.sum(d_in, axis=0, keepdims=True)
        sums_ref[0, 1:2] = jnp.sum(d_in * normed, axis=0, keepdims=True)
        real = (pl.program_id(0) < count_ref[0]).astype(F32)
        grad = cot_ref[...].astype(F32) * real
        d_hidden = grad + normal_back(d_in * (1.0 + piece[0, 4:5, :]), normed, inverse)
        d_hidden_ref[...] = d_hidden
        sums_ref[0, 2:3] = jnp.sum(d_hidden * attn_ref[...], axis=0, keepdims=True)
        d_attn = (piece[0, 2:3, :] * d_hidden).astype(BF)
        d_mixed = None
        for j, out in enumerate(refs[3:]):
            part = d_attn[:, j * columns : (j + 1) * columns]
            out[...] = part
            term = mm(part, w_ref[j], ((1,), (1,)))
            d_mixed = term if d_mixed is None else d_mixed + term
        d_mixed_ref[...] = d_mixed.astype(BF)

    rows = tokens // images
    outs = [(rows, (width,), F32), (rows, (width,), BF), (1, (3, width), F32)]
    outs += [(rows, (columns,), BF)] * blocks
    by_image = [d_mlp_in, hidden_one, attn_out, cotangent, pieces]
    return per_image(kernel, images, by_image, [out_b], outs, 40, "middle_back", count)


def block_head_back(d_packed, d_hidden, inputs, pieces, qkv_b, images):
    tokens, width = d_hidden.shape
    blocks = qkv_b.shape[0]

    def kernel(*refs):
        d_refs, (d_hidden_ref, in_ref, piece) = refs[:blocks], refs[blocks : blocks + 3]
        w_ref, out_ref, sums_ref = refs[blocks + 3 :]
        d_in = None
        for j, d in enumerate(d_refs):
            term = mm(d[...], w_ref[j], ((1,), (1,)))
            d_in = term if d_in is None else d_in + term
        normed, inverse = normal(in_ref[...].astype(F32))
        sums_ref[0, 0:1] = jnp.sum(d_in, axis=0, keepdims=True)
        sums_ref[0, 1:2] = jnp.sum(d_in * normed, axis=0, keepdims=True)
        back = normal_back(d_in * (1.0 + piece[0, 1:2, :]), normed, inverse)
        out_ref[...] = (d_hidden_ref[...] + back).astype(BF)

    outs = [(tokens // images, (width,), BF), (1, (2, width), F32)]
    by_image = [*d_packed, d_hidden, inputs, pieces]
    return per_image(kernel, images, by_image, [qkv_b], outs, 48, "block_head_back")


def grad_stacks(places, a, parts):
    tokens, features = a.shape
    z, count = places.z, places.narrow
    joined = len(parts) < count
    columns = parts[0].shape[1] // (count if joined else 1)
    rows = features // (4 * z)
    chunk = chunk_of(columns, 900)
    masks = [places.masks(0), places.masks(1)]
    total = len(masks[0])

    def kernel(at, a_ref, *refs):
        d_refs, (own_ref, send_ref, turned, product) = refs[:count], refs[count:]

        @pl.when(pl.program_id(0) == 0)
        def _():
            turned[...] = a_ref[...].T

        for i, d_ref in enumerate(d_refs):
            whole = mm(turned[...], d_ref[...], ((1,), (0,)))
            for k in range(4 * z):
                product[i, k] = whole[k * rows : (k + 1) * rows].astype(BF)
        core, y, x = at[0], at[1], at[2]
        for out, owner in ((own_ref, core), (send_ref, 1 - core)):
            for j in range(total):
                dy = jnp.where(owner == 0, masks[0][j][0], masks[1][j][0])
                dx = jnp.where(owner == 0, masks[0][j][1], masks[1][j][1])
                for k in range(z):
                    out[j, k] = product[x ^ dx, (k * 2 + (y ^ dy)) * 2 + owner]

    at = jnp.stack([places.at_c, places.at_y, places.x]).astype(jnp.int32)
    shape = (total, z, rows, columns)
    out = pl.BlockSpec((total, z, rows, chunk), lambda i: (0, 0, 0, i))
    return pl.pallas_call(
        kernel,
        grid=(-(-columns // chunk),),
        out_shape=[jax.ShapeDtypeStruct(shape, BF)] * 2,
        in_specs=[pl.BlockSpec(memory_space=pltpu.SMEM), whole_block(a)]
        + [
            pl.BlockSpec((tokens, chunk), lambda i, j=j: (0, j * (columns // chunk) + i if joined else i))
            for j in range(count)
        ],
        out_specs=[out, out],
        scratch_shapes=[
            pltpu.VMEM((features, tokens), BF),
            pltpu.VMEM((count, 4 * z, rows, chunk), BF),
        ],
        compiler_params=pltpu.CompilerParams(vmem_limit_bytes=60 * 2**20),
        cost_estimate=LONG,
        name="grad_stacks",
    )(at, a, *(parts * count if joined else parts))


class Places:
    def __init__(self):
        self.wide, self.narrow = lax.axis_size("wide"), lax.axis_size("narrow")
        self.z = self.wide // 4
        w = lax.axis_index("wide")
        self.w, self.x = w, lax.axis_index("narrow")
        self.at_z, self.at_y, self.at_c = w // 4, (w // 2) % 2, w % 2
        self.z_bits = [1 << i for i in range(self.z.bit_length() - 1)]
        self.x_bits = [1 << i for i in range(self.narrow.bit_length() - 1)]
        x_masks = [(0, bit) for bit in self.x_bits]
        self.orders = ([(1, 0)] + x_masks, x_masks + [(1, 0)])

    def swap(self, value, flip):
        pairs = []
        for w in range(self.wide):
            for x in range(self.narrow):
                dz, dy, dc, dx = flip(w % 2)
                to = (w // 4 ^ dz) * 4 + (w // 2 % 2 ^ dy) * 2 + (w % 2 ^ dc)
                pairs.append((w * self.narrow + x, to * self.narrow + (x ^ dx)))
        return lax.ppermute(value, ALL, pairs)

    def step_flip(self, i):
        return lambda core: (0, self.orders[core][i][0], 0, self.orders[core][i][1])

    def masks(self, core):
        out = [(0, 0)]
        for dy, dx in self.orders[core]:
            out = out + [(y ^ dy, x ^ dx) for y, x in out]
        return out

    def all_bits(self):
        out = [(0, (bit, 0, 0, 0), self.at_z // bit % 2) for bit in self.z_bits]
        out.append((1, (0, 1, 0, 0), self.at_y))
        out += [(3, (0, 0, 0, bit), self.x // bit % 2) for bit in self.x_bits]
        out.append((2, (0, 0, 1, 0), self.at_c))
        return out

    def open_small(self, value):
        return value[None, None, None, None]

    def gather_bits(self, value, bits):
        for axis, flip, bit in bits:
            other = self.swap(value, lambda core: flip)
            low = jnp.where(bit == 0, value, other)
            high = jnp.where(bit == 0, other, value)
            value = jnp.concatenate([low, high], axis)
        return value

    def add_narrow(self, value):
        for bit in self.x_bits:
            value = value + self.swap(value, lambda core: (0, 0, 0, bit))
        return value

    def scatter_chip_row(self, value):
        value = value.reshape(self.z, 2, 2, *value.shape[1:])
        other = self.swap(take(value, 2, 1 - self.at_c), lambda core: (0, 0, 1, 0))
        value = take(value, 2, self.at_c) + other
        other = self.swap(take(value, 1, 1 - self.at_y), lambda core: (0, 1, 0, 0))
        return take(value, 1, self.at_y) + other

    def scatter_z(self, value):
        for bit in reversed(self.z_bits):
            value = value.reshape(2, bit, *value.shape[1:])
            here = self.at_z // bit % 2
            other = self.swap(take(value, 0, 1 - here), lambda core: (bit, 0, 0, 0))
            value = take(value, 0, here) + other
        return value[0]

    def trade_narrow(self, value):
        if self.narrow != 2:
            return lax.all_to_all(value, "narrow", 0, 0, tiled=True)
        other = self.swap(take(value, 0, 1 - self.x), lambda core: (0, 0, 0, 1))
        own = take(value, 0, self.x)
        return jnp.stack([pick([own, other], self.x), pick([other, own], self.x)])


def pick(parts, index):
    if len(parts) == 1:
        return parts[0]
    if len(parts) == 2:
        return jnp.where(index == 0, parts[0], parts[1])
    return lax.dynamic_index_in_dim(jnp.stack(parts), index, 0, keepdims=False)


def take(value, axis, index):
    return lax.dynamic_index_in_dim(value, index, axis, keepdims=False)


def after(value, *before):
    return lax.optimization_barrier((value,) + before)[0]


def assemble(places, parts):
    half, z, rows, columns = parts[0].shape
    joined = columns % 128 == 0
    masks = [places.masks(0), places.masks(1)]

    def kernel(at, s0, s1, t0, t1, out, held, sem, out_sem):
        core, y, x, here_z = at[0], at[1], at[2], at[3]
        copies = []
        for i, src in enumerate((s0, s1, t0, t1)):
            owner = core ^ (i // 2)
            for j in range(half):
                k = j + half * (i % 2)
                dy = jnp.where(owner == 0, masks[0][k][0], masks[1][k][0])
                dx = jnp.where(owner == 0, masks[0][k][1], masks[1][k][1])
                for d in range(z):
                    if joined:
                        lanes = pl.ds(pl.multiple_of((x ^ dx) * columns, 128), columns)
                        to = held.at[here_z ^ d, y ^ dy, owner, :, lanes]
                    else:
                        to = held.at[x ^ dx, here_z ^ d, y ^ dy, owner]
                    copies.append(pltpu.make_async_copy(src.at[j, d], to, sem.at[len(copies)]))
        for copy in copies:
            copy.start()
        for copy in copies:
            copy.wait()
        whole = pltpu.make_async_copy(held, out, out_sem)
        whole.start()
        whole.wait()

    shape = (places.narrow, z, 2, 2, rows, columns)
    if joined:
        shape = (z, 2, 2, rows, places.narrow * columns)
    at = jnp.stack([places.at_c, places.at_y, places.x, places.at_z]).astype(jnp.int32)
    return pl.pallas_call(
        kernel,
        out_shape=jax.ShapeDtypeStruct(shape, BF),
        in_specs=[pl.BlockSpec(memory_space=pltpu.SMEM)] + [pl.BlockSpec(memory_space=pl.ANY)] * 4,
        out_specs=pl.BlockSpec(memory_space=pl.ANY),
        scratch_shapes=[
            pltpu.VMEM(shape, BF),
            pltpu.SemaphoreType.DMA((4 * half * z,)),
            pltpu.SemaphoreType.DMA,
        ],
        compiler_params=pltpu.CompilerParams(vmem_limit_bytes=60 * 2**20),
        cost_estimate=LONG,
        name="assemble",
    )(at, *parts)


def turn(places, a):
    tokens, features = a.shape
    slabs = 4 * places.z
    rows = features // slabs

    def kernel(at, a_ref, mine_ref, other_ref, turned):
        whole = a_ref[...].astype(F32).T
        for k in range(slabs):
            turned[k] = whole[k * rows : (k + 1) * rows].astype(BF)
        for k in range(slabs // 2):
            mine_ref[k] = turned[2 * k + at[0]]
            other_ref[k] = turned[2 * k + 1 - at[0]]

    out = jax.ShapeDtypeStruct((slabs // 2, rows, tokens), BF)
    return pl.pallas_call(
        kernel,
        grid=(1,),
        out_shape=[out, out],
        in_specs=[pl.BlockSpec(memory_space=pltpu.SMEM), whole_block(a)],
        out_specs=[whole_block(out)] * 2,
        scratch_shapes=[pltpu.VMEM((slabs, rows, tokens), BF)],
        compiler_params=pltpu.CompilerParams(vmem_limit_bytes=60 * 2**20),
        cost_estimate=LONG,
        name="turn",
    )(places.at_c.astype(jnp.int32).reshape(1), a)


def chip_stacks(places, turned, parts):
    slabs, rows, tokens = turned[0].shape
    z, count = places.z, places.narrow
    joined = len(parts[0]) < count
    columns = parts[0][0].shape[1] // (count if joined else 1)
    chunk = chunk_of(columns, 900)
    masks = [places.masks(0), places.masks(1)]
    half = len(masks[0]) // 2

    def kernel(at, own_ref, got_ref, *refs):
        d_refs, (keep_ref, send_ref, product) = refs[: 2 * count], refs[2 * count :]
        for i in range(count):
            whole = mm(own_ref[...], d_refs[i][...], ((1,), (0,)))
            whole += mm(got_ref[...], d_refs[count + i][...], ((1,), (0,)))
            for k in range(slabs):
                product[i, k] = whole[k * rows : (k + 1) * rows].astype(BF)
        core, y, x = at[0], at[1], at[2]
        for j in range(2 * half):
            dy = jnp.where(core == 0, masks[0][j][0], masks[1][j][0])
            dx = jnp.where(core == 0, masks[0][j][1], masks[1][j][1])
            out = keep_ref if j < half else send_ref
            for k in range(z):
                out[j % half, k] = product[x ^ dx, k * 2 + (y ^ dy)]

    at = jnp.stack([places.at_c, places.at_y, places.x]).astype(jnp.int32)
    flat = [a.reshape(slabs * rows, tokens) for a in turned]
    out = pl.BlockSpec((half, z, rows, chunk), lambda i: (0, 0, 0, i))
    specs = [
        pl.BlockSpec((tokens, chunk), lambda i, j=j: (0, j * (columns // chunk) + i if joined else i))
        for j in range(count)
    ]
    args = [p for part in parts for p in (list(part) * count if joined else part)]
    return pl.pallas_call(
        kernel,
        grid=(-(-columns // chunk),),
        out_shape=[jax.ShapeDtypeStruct((half, z, rows, columns), BF)] * 2,
        in_specs=[pl.BlockSpec(memory_space=pltpu.SMEM)] + [whole_block(a) for a in flat] + specs * 2,
        out_specs=[out, out],
        scratch_shapes=[pltpu.VMEM((count, slabs, rows, chunk), BF)],
        compiler_params=pltpu.CompilerParams(vmem_limit_bytes=60 * 2**20),
        cost_estimate=LONG,
        name="chip_stacks",
    )(at, *flat, *args)


def join(parts):
    counts = [p.shape[0] for p in parts]

    def kernel(*refs):
        first = 0
        for ref, count in zip(refs[:-1], counts):
            refs[-1][first : first + count] = ref[...]
            first += count

    shape = jax.ShapeDtypeStruct((sum(counts), *parts[0].shape[1:]), BF)
    return pl.pallas_call(
        kernel,
        grid=(1,),
        out_shape=shape,
        in_specs=[whole_block(p) for p in parts],
        out_specs=whole_block(shape),
        compiler_params=pltpu.CompilerParams(vmem_limit_bytes=60 * 2**20),
        cost_estimate=SHORT,
        name="join",
    )(*parts)


def add_stacks(terms, half):
    shape = (half, *terms[0].shape[1:])

    def kernel(*refs):
        total = refs[0][...].astype(F32)
        for ref in refs[1:-1]:
            total += ref[...].astype(F32)
        refs[-1][...] = total.astype(BF)

    deep = 2 if shape[1] % 2 == 0 else 1
    block = (1, deep, *shape[2:])
    return pl.pallas_call(
        kernel,
        grid=(half, shape[1] // deep),
        out_shape=jax.ShapeDtypeStruct(shape, BF),
        in_specs=[pl.BlockSpec(block, lambda i, j: (half + i, j, 0, 0))] * len(terms),
        out_specs=pl.BlockSpec(block, lambda i, j: (i, j, 0, 0)),
        compiler_params=pltpu.CompilerParams(vmem_limit_bytes=60 * 2**20),
        cost_estimate=SHORT,
        name="add_stacks",
    )(*terms)


def add_slabs(places, terms, z_terms, first, count, divisor=None):
    rows, columns = terms[0].shape[2:]
    late = [(at, term) for at, term in z_terms if at <= first < at + term.shape[0]]

    def kernel(at_ref, *refs):
        out, refs = refs[-1], refs[:-1]
        total = None
        for i, ref in enumerate(refs[: len(terms) + len(late)]):
            value = (ref[0, 0] if i < len(terms) else ref[0]).astype(F32)
            total = value if total is None else total + value
        if divisor is not None:
            total = total / refs[-1][0]
        out[0] = total.astype(out.dtype)

    in_specs = [
        pl.BlockSpec((1, 1, rows, columns), lambda i, at: (0, at[0] ^ (first + i), 0, 0))
        for _ in terms
    ]
    in_specs += [
        pl.BlockSpec((1, rows, columns), lambda i, at, f=first - at_first: (f + i, 0, 0))
        for at_first, _ in late
    ]
    args = [*terms, *[term for _, term in late]]
    if divisor is not None:
        in_specs.append(pl.BlockSpec(memory_space=pltpu.SMEM))
        args.append(divisor.reshape(1))
    kind = BF if divisor is None else F32
    return pl.pallas_call(
        kernel,
        grid_spec=pltpu.PrefetchScalarGridSpec(
            num_scalar_prefetch=1,
            grid=(count,),
            in_specs=in_specs,
            out_specs=pl.BlockSpec((1, rows, columns), lambda i, at: (i, 0, 0)),
        ),
        out_shape=jax.ShapeDtypeStruct((count, rows, columns), kind),
        compiler_params=pltpu.CompilerParams(vmem_limit_bytes=60 * 2**20),
        cost_estimate=SHORT,
        name="add_slabs",
    )(places.at_z.astype(jnp.int32).reshape(1), *args)


class Slots:
    def __init__(self, places):
        self.places = places
        self.before, self.now, self.ready = (), [], []

    def tie(self, value):
        return after(value, *self.before, *self.ready)

    def note(self, *values):
        self.now += values

    def next(self, *values):
        self.note(*values)
        self.before, self.now, self.ready = tuple(self.now), [], []

    def send(self, value, flip):
        value = after(value, *self.before)
        self.ready.append(value)
        return self.follow(value, flip)

    def follow(self, value, flip):
        other = self.places.swap(value, flip)
        self.note(other)
        return other


class Gather:
    def __init__(self, slots, shard):
        self.slots, self.places = slots, slots.places
        self.rows = self.places.wide * shard.shape[0]
        self.parts = [shard[None]]

    def all_z(self):
        for d in range(1, self.places.z):
            self.parts.append(self.slots.send(self.parts[0], lambda core: (d, 0, 0, 0)))

    def step(self, i, exchange):
        joined = join([p.reshape(-1, *p.shape[-2:]) for p in self.parts])
        self.parts = [joined]
        self.parts.append(exchange(joined, self.places.step_flip(i)))

    def first(self):
        for i in range(len(self.places.orders[0]) - 1):
            self.step(i, self.slots.follow if i else self.slots.send)

    def last(self):
        self.step(len(self.places.orders[0]) - 1, self.slots.send)

    def cores(self):
        parts = [p.reshape(-1, self.places.z, *p.shape[-2:]) for p in self.parts]
        self.parts = parts + [self.slots.send(p, lambda core: (0, 0, 1, 0)) for p in parts]

    def whole(self):
        whole = assemble(self.places, self.slots.tie(tuple(self.parts)))
        return whole.reshape(-1, self.rows, whole.shape[-1])


class Scatter:
    def __init__(self, slots, a, parts):
        self.slots, self.places = slots, slots.places
        stack, self.to_core = grad_stacks(self.places, a, parts)
        self.terms, self.z_terms, self.half = [stack], [], stack.shape[0]

    def cores(self, exchange):
        self.terms.append(exchange(self.to_core, lambda core: (0, 0, 1, 0)))

    def hold(self):
        self.terms[0] = self.slots.tie(self.terms[0])

    def step(self, i, exchange):
        self.half //= 2
        send = add_stacks(self.terms, self.half)
        self.terms.append(exchange(send, self.places.step_flip(i)))

    def first(self):
        self.step(len(self.places.orders[0]) - 1, self.slots.send)

    def last(self):
        for i in reversed(range(len(self.places.orders[0]) - 1)):
            chained = i < len(self.places.orders[0]) - 2
            self.step(i, self.slots.follow if chained else self.slots.send)

    def step_z(self, *bits):
        for i, bit in enumerate(bits):
            exchange = self.slots.follow if i else self.slots.send
            send = add_slabs(self.places, self.terms, self.z_terms, bit, bit)
            self.z_terms.append((0, exchange(send, lambda core: (bit, 0, 0, 0))))

    def direct_z(self):
        for d in reversed(range(1, self.places.z)):
            send = add_slabs(self.places, self.terms, self.z_terms, d, 1)
            self.z_terms.append((0, self.slots.send(send, lambda core: (d, 0, 0, 0))))

    def result(self, divisor):
        divisor = self.slots.tie(divisor)
        return add_slabs(self.places, self.terms, self.z_terms, 0, 1, divisor)[0]


class ChipScatter(Scatter):
    def __init__(self, slots, turned, parts):
        self.slots, self.places = slots, slots.places
        keep, self.ready = chip_stacks(self.places, turned, parts)
        self.terms, self.z_terms, self.half = [keep], [], keep.shape[0]

    def first(self):
        flip = self.places.step_flip(len(self.places.orders[0]) - 1)
        self.terms.append(self.slots.send(self.ready, flip))


def to_core(core):
    return (0, 0, 1, 0)


def dot(a, b, dims, out=F32):
    return lax.dot_general(a, b, (dims, ((), ())), preferred_element_type=F32).astype(out)


def split(a, count):
    width = a.shape[1] // count
    return [a[:, n * width : (n + 1) * width] for n in range(count)]


def on_device(
    inputs,
    cotangent,
    class_ids,
    step_ids,
    image_counts,
    w_qkv,
    w_out,
    w_gate,
    w_up,
    w_down,
    ada_weight,
    ada_bias,
    class_table,
    norm_gains,
):
    places = Places()
    wide, narrow, at_w, at_n = places.wide, places.narrow, places.w, places.x
    images, length, width = inputs.shape
    tables, sums = head_tables(length), head_sums()
    gains = jnp.tile(norm_gains, (1, H))
    local_count = image_counts[0]

    tokens = images * length

    def flat(v):
        return v.reshape(tokens, -1)

    def deep(v):
        return v.reshape(images, length, -1)

    t = Slots(places)
    z_low, z_high = places.z_bits[:1], places.z_bits[1:]
    z_down = z_high[::-1]
    qkv, out, gate, up, down = [
        Gather(t, shard) for shard in (w_qkv, w_out, w_gate, w_up, w_down)
    ]

    qkv.all_z()
    small = [class_ids, step_ids, image_counts, ada_bias]
    small = jnp.concatenate([v.astype(F32) for v in small])[None]
    bits = places.all_bits()
    small = places.gather_bits(places.open_small(small), bits)
    small = small.reshape(wide * narrow, -1)
    t.next(small)

    qkv.first()
    out.all_z()
    small = t.tie(small)
    ids = small[:, : 2 * images].reshape(-1, 2, images).transpose(0, 2, 1).reshape(-1, 2)
    ids = ids.astype(jnp.int32)
    real_count = jnp.sum(small[:, 2 * images])
    bias = small[:, 2 * images + 1 :].reshape(-1)
    rows_here, cols_here = class_table.shape
    class_hot = ids[:, :1] - at_n * rows_here == jnp.arange(rows_here, dtype=jnp.int32)[None, :]
    picked = dot(class_hot.astype(BF), class_table, ((1,), (0,)))
    column = at_w * cols_here + jnp.arange(cols_here, dtype=jnp.int32)
    half_width = width // 2
    frequency = jnp.exp(-math.log(10000.0) * (column % half_width).astype(F32) / half_width)
    angles = ids[:, 1:].astype(F32) * frequency[None, :]
    wave = jnp.where(column[None, :] < half_width, jnp.cos(angles), jnp.sin(angles))
    condition = places.add_narrow(picked) + wave
    cond_act = jax.nn.silu(condition).astype(BF)
    t.next(cond_act)

    qkv.last()
    gate.all_z()
    mod_part = dot(t.tie(cond_act), ada_weight, ((1,), (0,)))
    mod_part = places.scatter_chip_row(mod_part.reshape(wide, narrow, images, -1))
    t.next(mod_part, *tables, sums)

    qkv.cores()
    out.first()
    gate.first()
    mod_part = places.trade_narrow(places.scatter_z(t.tie(mod_part)))
    t.next(mod_part)

    out.last()
    gate.last()
    up.all_z()
    qkv_b = qkv.whole()
    modulation = t.tie(mod_part).transpose(1, 0, 2).reshape(images, -1) + bias
    pieces = modulation.reshape(images, 6, width)
    normed, _ = layer_norm(inputs.astype(F32))
    attn_in = flat((normed * (1.0 + pieces[:, 1:2]) + pieces[:, 0:1]).astype(BF))
    t.next(attn_in, qkv_b)

    out.cores()
    gate.cores()
    up.first()
    packed = project(t.tie(attn_in), qkv_b)
    attn_turned, attn_other = turn(places, t.tie(attn_in))
    t.next(*packed, attn_other)

    attn_turned = [attn_turned, t.send(attn_other, to_core)]
    up.last()
    down.all_z()
    packed = t.tie(packed)
    queries, key_rows, value_rows, mixed = attention_forward(packed, gains, tables, sums, images)
    slot_real = (jnp.arange(images, dtype=jnp.int32) < local_count).astype(F32)
    grad_y = cotangent.astype(F32) * slot_real[:, None, None]
    d_mlp = split(flat((pieces[:, 5:6] * grad_y).astype(BF)), narrow)
    t.next(mixed, *d_mlp)

    up.cores()
    down.first()
    out_b = out.whole()
    attn_out, hidden_one, mlp_in = attention_tail(mixed, out_b, flat(inputs), pieces, images)
    gate_b = gate.whole()[0]
    mlp_turned, mlp_other = turn(places, mlp_in)
    t.next(mlp_in, gate_b, mlp_other)

    mlp_turned = [mlp_turned, t.send(mlp_other, to_core)]
    down.last()
    up_b = up.whole()[0]
    gate_val, up_val, hidden_mid = gated(mlp_in, gate_b, up_b)
    t.next(hidden_mid)

    down.cores()
    g_down = Scatter(t, t.tie(hidden_mid), d_mlp)
    t.next(g_down.to_core)

    g_down.cores(t.send)
    down_b = down.whole()
    t.next(down_b)

    g_down.first()
    d_gate, d_up, d_mlp_in = gated_back(t.tie(d_mlp), down_b, gate_val, up_val, gate_b, up_b)
    t.next(d_mlp_in)

    g_down.last()
    d_gate_got = t.send(d_gate, to_core)
    d_up_got = t.send(d_up, to_core)
    d_hidden, d_mixed, sums_b, *d_attn = middle_back(
        t.tie(d_mlp_in), hidden_one, attn_out, flat(cotangent), pieces, out_b, image_counts, images
    )
    g_gate = ChipScatter(t, mlp_turned, [[after(d_gate, d_mixed)], [d_gate_got]])
    t.next(g_gate.ready)

    g_gate.first()
    g_down.hold()
    g_down.step_z(*z_down)
    g_up = ChipScatter(t, mlp_turned, [[t.tie(d_up)], [d_up_got]])
    g_out = Scatter(t, mixed, t.tie(d_attn))
    block_output, sums_gate = block_tail(
        t.tie(hidden_mid), down_b, hidden_one, flat(cotangent), pieces, image_counts, images
    )
    t.next(g_up.ready, g_out.to_core, sums_gate)

    g_up.first()
    g_gate.last()
    g_out.cores(t.send)
    g_down.step_z(*z_low)
    d_packed, gain_terms = attention_backward(
        packed, queries, key_rows, value_rows, t.tie(d_mixed), gains, tables, sums, images
    )
    t.next(*d_packed)

    d_packed_got = [
        t.send(d.reshape(-1, 8, d.shape[1]), to_core).reshape(d.shape) for d in d_packed
    ]
    for grad in (g_up, g_out, g_gate):
        grad.hold()
    g_up.last()
    g_out.first()
    g_gate.step_z(*z_down)
    g_qkv = ChipScatter(t, attn_turned, [t.tie(d_packed), d_packed_got])
    t.next(g_qkv.ready)

    g_qkv.first()
    for grad in (g_out, g_up, g_gate):
        grad.hold()
    g_out.last()
    g_up.step_z(*z_down)
    g_gate.step_z(*z_low)
    d_tokens, sums_a = block_head_back(
        t.tie(d_packed), d_hidden, flat(inputs), pieces, qkv_b, images
    )
    grad_gains = gain_terms.sum(0).reshape(2, H, HD).sum(1).reshape(1, -1)
    gains_high = grad_gains.astype(BF)
    gains_low = (grad_gains - gains_high.astype(F32)).astype(BF)
    rest = jnp.zeros((images - 2, 2 * HD), BF)
    grad_gains = jnp.concatenate([gains_high, gains_low, rest], axis=0)
    d_modulation = jnp.concatenate([sums_a, sums_b[:, 2:], sums_b[:, :2], sums_gate], axis=1)
    d_modulation = d_modulation.astype(BF).reshape(images, -1)
    d_modulation = jnp.concatenate([d_modulation, grad_gains], axis=1)
    t.next(d_modulation)

    g_qkv.last()
    for grad in (g_up, g_out):
        grad.hold()
    g_up.step_z(*z_low)
    g_out.step_z(*z_down)
    d_all = places.open_small(t.tie(d_modulation))
    d_all = places.gather_bits(d_all, bits[: len(places.z_bits)])
    t.next(d_all)

    g_qkv.direct_z()
    g_out.step_z(*z_low)
    d_all = places.gather_bits(t.tie(d_all), bits[len(places.z_bits) :])
    d_all = d_all.reshape(wide * narrow * images, -1)
    gain_sum = d_all[:, 6 * width : 6 * width + 2 * HD].astype(F32)
    gain_sum = jnp.sum(gain_sum, axis=0).reshape(2, HD) / real_count
    d_mod = d_all[:, : 6 * width]
    ada_cols = ada_weight.shape[1]
    d_mod_here = lax.dynamic_slice_in_dim(d_mod, at_n * ada_cols, ada_cols, 1)
    g_ada = dot(cond_act, d_mod_here, ((0,), (0,))) / real_count
    bias_cols = ada_bias.shape[0]
    bias_at = (at_w * narrow + at_n) * bias_cols
    g_bias = jnp.sum(lax.dynamic_slice_in_dim(d_mod, bias_at, bias_cols, 1).astype(F32), axis=0)
    g_bias = g_bias / real_count
    d_cond_act = places.add_narrow(dot(d_mod_here, ada_weight, ((1,), (1,))))
    cond_sigmoid = jax.nn.sigmoid(condition)
    d_condition = d_cond_act * cond_sigmoid * (1.0 + condition * (1.0 - cond_sigmoid))
    g_table = jnp.dot(class_hot.astype(F32).T, d_condition, precision=HIGHEST) / real_count
    r_out, r_gate, r_up, r_down = [g.result(real_count) for g in (g_out, g_gate, g_up, g_down)]
    at, late = g_qkv.z_terms[-1]
    g_qkv.z_terms[-1] = (at, after(late, g_ada, g_table, r_out, r_gate, r_up, r_down))
    r_qkv = g_qkv.result(real_count)

    return (
        deep(block_output),
        deep(d_tokens),
        r_qkv,
        r_out,
        r_gate,
        r_up,
        r_down,
        g_ada,
        g_bias,
        g_table,
        gain_sum,
    )


def solution(mesh):
    split = P("wide", "narrow")
    images = P(ALL, None, None)
    return jax.shard_map(
        on_device,
        mesh=mesh,
        in_specs=(
            images,
            images,
            P(ALL),
            P(ALL),
            P(ALL),
            split,
            split,
            split,
            split,
            split,
            split,
            P(ALL),
            P("narrow", "wide"),
            P(),
        ),
        out_specs=(
            images,
            images,
            split,
            split,
            split,
            split,
            split,
            split,
            P(ALL),
            P("narrow", "wide"),
            P(),
        ),
        check_vma=False,
    )
```

```python
import math

import jax
import jax.numpy as jnp
from jax import lax
from jax.experimental import pallas as pl
from jax.experimental.pallas import tpu as pltpu
from jax.sharding import PartitionSpec as P

H = 16
HD = 72
CLASSES = 1000
GRID = 16

EPSILON = 1e-06
HIGHEST = lax.Precision.HIGHEST
ALL = ("wide", "narrow")
BF = jnp.bfloat16
F32 = jnp.float32
LONG = pl.CostEstimate(flops=10**12, bytes_accessed=1, transcendentals=0)
SHORT = pl.CostEstimate(flops=1, bytes_accessed=1, transcendentals=0)


def layer_norm(values):
    centre = values - jnp.mean(values, axis=-1, keepdims=True)
    inverse = lax.rsqrt(jnp.mean(centre * centre, axis=-1, keepdims=True) + EPSILON)
    return (centre * inverse, inverse)


def head_tables(length):
    quarter = HD // 4
    lane = jnp.arange(H * HD, dtype=jnp.int32) % HD
    frequency = 10000.0 ** (-(lane % quarter).astype(F32) / quarter)
    patch = jnp.arange(length, dtype=jnp.int32)[:, None]
    place = jnp.where(lane[None, :] < 2 * quarter, patch // GRID, patch % GRID)
    angles = place.astype(F32) * frequency[None, :]
    cosine, sine = jnp.cos(angles), jnp.sin(angles)
    first = (lane // quarter % 2 == 0)[None, :]
    return [cosine, jnp.where(first, -sine, 0.0), jnp.where(first, 0.0, sine)]


def head_sums():
    lane = lax.broadcasted_iota(jnp.int32, (H * HD, 128), 0) // HD
    return (lane == lax.broadcasted_iota(jnp.int32, (H * HD, 128), 1)).astype(BF)


def exact_dot(a, b, dims):
    total = None
    for _ in range(3):
        term = a.astype(BF)
        a = a - term.astype(F32)
        part = lax.dot_general(term, b, (dims, ((), ())), preferred_element_type=F32)
        total = part if total is None else total + part
    return total


def head_mean(values, sums):
    mean = exact_dot(values, sums, ((1,), (0,))) * (1.0 / HD)
    return exact_dot(mean, sums, ((1,), (1,)))


def shifted(values, cosine, above, below, sign):
    quarter, width = HD // 4, values.shape[1]
    up = pltpu.roll(values, width - quarter, 1)
    down = pltpu.roll(values, quarter, 1)
    return values * cosine + sign * (up * above + down * below)


def window(head):
    first, last = head * HD // 128 * 128, ((head + 1) * HD + 127) // 128 * 128
    return first, last


def only(values, head):
    first, last = window(head)
    part = values[:, first:last]
    lane = first + lax.broadcasted_iota(jnp.int32, (1, last - first), 1)
    mine = ((lane >= head * HD) & (lane < (head + 1) * HD)).astype(values.dtype)
    return part * mine


class Tiles:
    def __init__(self, store):
        self.store, self.held = store, {}

    def add(self, head, value):
        first, last = window(head)
        for tile in range(first // 128, last // 128):
            part = value[:, tile * 128 - first : tile * 128 - first + 128]
            self.held[tile] = self.held[tile] + part if tile in self.held else part
        done = (head + 1) * HD // 128
        for tile in sorted(self.held):
            if tile < done or head == H - 1:
                self.store(tile * 128, self.held.pop(tile))


def mm(a, b, dims):
    return lax.dot_general(a, b, (dims, ((), ())), preferred_element_type=F32)


def only_turned(values, head):
    first, last = window(head)
    part = values[first:last, :]
    row = first + lax.broadcasted_iota(jnp.int32, (last - first, 1), 0)
    mine = ((row >= head * HD) & (row < (head + 1) * HD)).astype(values.dtype)
    return part * mine


def softmax_of(queries, keys_turned, head):
    first, last = window(head)
    scores = mm(only(queries, head), keys_turned[first:last, :], ((1,), (0,))) * (HD ** (-0.5))
    exponent = jnp.exp(scores - jnp.max(scores, axis=1, keepdims=True))
    return exponent / jnp.sum(exponent, axis=1, keepdims=True)


def attention_forward(packed, gains, tables, sums, images):
    tokens = packed[0].shape[0]
    length, width, blocks = tokens // images, H * HD, len(packed)

    def kernel(*refs):
        parts, refs = refs[:blocks], refs[blocks:]
        gain, cosine, above, below, sums_ref, q_ref, k_ref, v_ref, mixed_ref, k_turned = refs
        whole = jnp.concatenate([p[...] for p in parts], axis=1)
        sums_here = sums_ref[...]
        for i, ref in enumerate((q_ref, k_ref)):
            raw = whole[:, i * width : (i + 1) * width]
            normed = raw * lax.rsqrt(head_mean(raw * raw, sums_here) + EPSILON)
            turned = shifted(normed * gain[i : i + 1, :], cosine[...], above[...], below[...], 1.0)
            ref[...] = turned.astype(BF)
        v_ref[...] = whole[:, 2 * width :].astype(BF)

        def store(first, value):
            mixed_ref[:, first : first + 128] = value.astype(BF)

        k_turned[...] = k_ref[...].T
        mixed = Tiles(store)
        for head in range(H):
            attention = softmax_of(q_ref, k_turned, head).astype(BF)
            mixed.add(head, mm(attention, only(v_ref, head), ((1,), (0,))))

    def rows(n):
        return pl.BlockSpec((length, n), lambda i: (i, 0))

    def all_of(a):
        return pl.BlockSpec(a.shape, lambda i: (0, 0))

    out = jax.ShapeDtypeStruct((tokens, width), BF)
    return pl.pallas_call(
        kernel,
        grid=(images,),
        out_shape=[out] * 4,
        in_specs=[rows(p.shape[1]) for p in packed] + [all_of(a) for a in (gains, *tables, sums)],
        out_specs=[rows(width)] * 4,
        scratch_shapes=[pltpu.VMEM((width, length), BF)],
        compiler_params=pltpu.CompilerParams(vmem_limit_bytes=60 * 2**20),
        cost_estimate=LONG,
        name="attention_forward",
    )(*packed, gains, *tables, sums)


def attention_backward(packed, queries, keys, values, d_mixed, gains, tables, sums, images):
    tokens = queries.shape[0]
    length, width, blocks = tokens // images, H * HD, len(packed)
    block = packed[0].shape[1]

    def kernel(*refs):
        parts, refs = refs[:blocks], refs[blocks:]
        q_ref, k_ref, v_ref, d_ref, gain, cosine, above, below, sums_ref = refs[:9]
        outs, refs = refs[9 : 9 + blocks], refs[9 + blocks :]
        gain_ref, d_q_turned, d_k, d_v, q_turned, k_turned, d_turned = refs

        def store_to(ref):
            def store(first, value):
                ref[:, first : first + 128] = value

            return store

        for ref, turned in ((q_ref, q_turned), (k_ref, k_turned), (d_ref, d_turned)):
            turned[...] = ref[...].T
        all_k, all_v = [Tiles(store_to(ref)) for ref in (d_k, d_v)]
        rows_q = {}
        for head in range(H):
            first, last = window(head)
            scores = mm(only(k_ref, head), q_turned[first:last, :], ((1,), (0,))) * (HD ** (-0.5))
            exponent = jnp.exp(scores - jnp.max(scores, axis=0, keepdims=True))
            soft = exponent / jnp.sum(exponent, axis=0, keepdims=True)
            all_v.add(head, mm(soft.astype(BF), only(d_ref, head), ((1,), (0,))))
            d_soft = mm(only(v_ref, head), d_turned[first:last, :], ((1,), (0,)))
            inner = jnp.sum(soft * d_soft, axis=0, keepdims=True)
            d_scores = (soft * (d_soft - inner) * (HD ** (-0.5))).astype(BF)
            all_k.add(head, mm(d_scores, only(q_ref, head), ((1,), (0,))))
            part = mm(only_turned(k_turned, head), d_scores, ((1,), (0,)))
            for tile in range(first // 128, last // 128):
                rows = part[tile * 128 - first : tile * 128 - first + 128]
                rows_q[tile] = rows_q[tile] + rows if tile in rows_q else rows
            for tile in sorted(rows_q):
                if tile < (head + 1) * HD // 128 or head == H - 1:
                    d_q_turned[tile * 128 : tile * 128 + 128, :] = rows_q.pop(tile)
        whole = jnp.concatenate([p[...] for p in parts], axis=1)
        sums_here = sums_ref[...]
        done = []
        for i, value in enumerate((d_q_turned[...].T, d_k[...])):
            raw = whole[:, i * width : (i + 1) * width]
            inverse = lax.rsqrt(head_mean(raw * raw, sums_here) + EPSILON)
            normed = raw * inverse
            scaled = shifted(value, cosine[...], above[...], below[...], -1.0)
            gain_ref[0, i : i + 1, :] = jnp.sum(scaled * normed, axis=0, keepdims=True)
            incoming = scaled * gain[i : i + 1, :]
            mean = head_mean(incoming * normed, sums_here)
            done.append((inverse * (incoming - normed * mean)).astype(BF))
        done.append(d_v[...].astype(BF))
        done = jnp.concatenate(done, axis=1)
        for j, out in enumerate(outs):
            out[...] = done[:, j * block : (j + 1) * block]

    def rows(n):
        return pl.BlockSpec((length, n), lambda i: (i, 0))

    def all_of(a):
        return pl.BlockSpec(a.shape, lambda i: (0, 0))

    outs = pl.pallas_call(
        kernel,
        grid=(images,),
        out_shape=[jax.ShapeDtypeStruct((tokens, block), BF)] * blocks
        + [jax.ShapeDtypeStruct((images, 2, width), F32)],
        in_specs=[rows(block)] * blocks
        + [rows(width)] * 4
        + [all_of(a) for a in (gains, *tables, sums)],
        out_specs=[rows(block)] * blocks + [pl.BlockSpec((1, 2, width), lambda i: (i, 0, 0))],
        scratch_shapes=[pltpu.VMEM((width, length), F32)]
        + [pltpu.VMEM((length, width), F32)] * 2
        + [pltpu.VMEM((width, length), BF)] * 3,
        compiler_params=pltpu.CompilerParams(vmem_limit_bytes=60 * 2**20),
        cost_estimate=LONG,
        name="attention_backward",
    )(*packed, queries, keys, values, d_mixed, gains, *tables, sums)
    return outs[:blocks], outs[blocks]

def whole_block(a):
    return pl.BlockSpec(a.shape, lambda *i: (0,) * a.ndim)


def chunk_of(columns, most):
    count = -(-columns // most)
    return columns if count == 1 else -(-columns // (128 * count)) * 128


def project(a, blocks):
    tokens, depth = a.shape
    count, _, columns = blocks.shape
    chunk = chunk_of(columns, 640)

    def kernel(a_ref, *refs):
        for w_ref, out_ref in zip(refs[:count], refs[count:]):
            out_ref[...] = mm(a_ref[...], w_ref[...], ((1,), (0,)))

    return pl.pallas_call(
        kernel,
        grid=(-(-columns // chunk),),
        out_shape=[jax.ShapeDtypeStruct((tokens, columns), F32)] * count,
        in_specs=[whole_block(a)]
        + [pl.BlockSpec((None, depth, chunk), lambda i, j=j: (j, 0, i)) for j in range(count)],
        out_specs=[pl.BlockSpec((tokens, chunk), lambda i: (0, i))] * count,
        compiler_params=pltpu.CompilerParams(vmem_limit_bytes=60 * 2**20),
        cost_estimate=LONG,
        name="project",
    )(a, *[blocks] * count)


def gated(a, w_gate, w_up):
    tokens, depth = a.shape
    columns = w_gate.shape[1]
    chunk = 512

    def kernel(a_ref, g_ref, u_ref, gate_ref, up_ref, mid_ref):
        gate = mm(a_ref[...], g_ref[...], ((1,), (0,)))
        up = mm(a_ref[...], u_ref[...], ((1,), (0,)))
        gate_ref[...] = gate
        up_ref[...] = up
        mid_ref[...] = (gate * jax.nn.sigmoid(gate) * up).astype(BF)

    weight = pl.BlockSpec((depth, chunk), lambda i: (0, i))
    out = pl.BlockSpec((tokens, chunk), lambda i: (0, i))
    return pl.pallas_call(
        kernel,
        grid=(columns // chunk,),
        out_shape=[jax.ShapeDtypeStruct((tokens, columns), t) for t in (F32, F32, BF)],
        in_specs=[whole_block(a), weight, weight],
        out_specs=[out] * 3,
        compiler_params=pltpu.CompilerParams(vmem_limit_bytes=60 * 2**20),
        cost_estimate=LONG,
        name="gated",
    )(a, w_gate, w_up)


def gated_back(d_parts, down, gate_val, up_val, w_gate, w_up):
    tokens, columns = gate_val.shape
    depth, count, chunk = w_gate.shape[0], down.shape[0], 512

    def kernel(*refs):
        d_refs, w_refs, refs = refs[:count], refs[count : 2 * count], refs[2 * count :]
        gate_ref, up_ref, g_ref, u_ref, d_gate_ref, d_up_ref, in_ref = refs
        d_mid = None
        for d_ref, w_ref in zip(d_refs, w_refs):
            term = mm(d_ref[...], w_ref[...], ((1,), (1,)))
            d_mid = term if d_mid is None else d_mid + term
        gate, up = gate_ref[...], up_ref[...]
        sigmoid = jax.nn.sigmoid(gate)
        silu = gate * sigmoid
        d_gate = (d_mid * up * (sigmoid + silu * (1.0 - sigmoid))).astype(BF)
        d_up = (d_mid * silu).astype(BF)
        d_gate_ref[...] = d_gate
        d_up_ref[...] = d_up
        term = mm(d_gate, g_ref[...], ((1,), (1,))) + mm(d_up, u_ref[...], ((1,), (1,)))

        @pl.when(pl.program_id(0) == 0)
        def _():
            in_ref[...] = term

        @pl.when(pl.program_id(0) > 0)
        def _():
            in_ref[...] += term

    width = down.shape[2]
    token = pl.BlockSpec((tokens, chunk), lambda i: (0, i))
    weight = pl.BlockSpec((depth, chunk), lambda i: (0, i))
    return pl.pallas_call(
        kernel,
        grid=(columns // chunk,),
        out_shape=[jax.ShapeDtypeStruct((tokens, columns), BF)] * 2
        + [jax.ShapeDtypeStruct((tokens, depth), F32)],
        in_specs=[whole_block(d) for d in d_parts]
        + [pl.BlockSpec((None, chunk, width), lambda i, j=j: (j, i, 0)) for j in range(count)]
        + [token, token, weight, weight],
        out_specs=[token, token, pl.BlockSpec((tokens, depth), lambda i: (0, 0))],
        compiler_params=pltpu.CompilerParams(vmem_limit_bytes=60 * 2**20),
        cost_estimate=LONG,
        name="gated_back",
    )(*d_parts, *[down] * count, gate_val, up_val, w_gate, w_up)


def normal(values):
    centre = values - jnp.mean(values, axis=1, keepdims=True)
    inverse = lax.rsqrt(jnp.mean(centre * centre, axis=1, keepdims=True) + EPSILON)
    return centre * inverse, inverse


def normal_back(gradient, normed, inverse):
    mean = jnp.mean(gradient, axis=1, keepdims=True)
    return inverse * (
        gradient - mean - normed * jnp.mean(gradient * normed, axis=1, keepdims=True)
    )


def per_image(kernel, images, by_image, whole, outs, vmem, name, scalar=None):
    def spec(rows, rest):
        return pl.BlockSpec((rows, *rest), lambda i: (i,) + (0,) * len(rest))

    in_specs = [spec(a.shape[0] // images, a.shape[1:]) for a in by_image]
    in_specs += [whole_block(a) for a in whole]
    args = [*by_image, *whole]
    if scalar is not None:
        in_specs.append(pl.BlockSpec(memory_space=pltpu.SMEM))
        args.append(scalar)
    return pl.pallas_call(
        kernel,
        grid=(images,),
        out_shape=[jax.ShapeDtypeStruct((images * rows, *rest), t) for rows, rest, t in outs],
        in_specs=in_specs,
        out_specs=[spec(rows, rest) for rows, rest, _ in outs],
        compiler_params=pltpu.CompilerParams(vmem_limit_bytes=60 * 2**20),
        cost_estimate=LONG,
        name=name,
    )(*args)


def attention_tail(mixed, out_b, inputs, pieces, images):
    tokens, width = mixed.shape

    def kernel(mixed_ref, in_ref, piece, *refs):
        w_ref, attn_ref, hidden_ref, mlp_ref = refs
        attn = [mm(mixed_ref[...], w_ref[j], ((1,), (0,))) for j in range(out_b.shape[0])]
        attn = jnp.concatenate(attn, axis=1)
        attn_ref[...] = attn
        hidden = in_ref[...].astype(F32) + piece[0, 2:3, :] * attn
        hidden_ref[...] = hidden
        normed, _ = normal(hidden)
        mlp_ref[...] = (normed * (1.0 + piece[0, 4:5, :]) + piece[0, 3:4, :]).astype(BF)

    rows = tokens // images
    outs = [(rows, (width,), F32), (rows, (width,), F32), (rows, (width,), BF)]
    return per_image(kernel, images, [mixed, inputs, pieces], [out_b], outs, 32, "attention_tail")


def block_tail(hidden_mid, down_b, hidden_one, cotangent, pieces, count, images):
    tokens, width = hidden_one.shape

    def kernel(mid_ref, hidden_ref, cot_ref, piece, *refs):
        w_ref, count_ref, out_ref, gate_ref = refs
        mlp = [mm(mid_ref[...], w_ref[j], ((1,), (0,))) for j in range(down_b.shape[0])]
        mlp = jnp.concatenate(mlp, axis=1)
        out_ref[...] = (hidden_ref[...] + piece[0, 5:6, :] * mlp).astype(BF)
        real = (pl.program_id(0) < count_ref[0]).astype(F32)
        grad = cot_ref[...].astype(F32) * real
        gate_ref[0] = jnp.sum(grad * mlp, axis=0, keepdims=True)

    rows = tokens // images
    outs = [(rows, (width,), BF), (1, (1, width), F32)]
    by_image = [hidden_mid, hidden_one, cotangent, pieces]
    return per_image(kernel, images, by_image, [down_b], outs, 40, "block_tail", count)


def middle_back(d_mlp_in, hidden_one, attn_out, cotangent, pieces, out_b, count, images):
    tokens, width = d_mlp_in.shape
    blocks, _, columns = out_b.shape

    def kernel(in_ref, hidden_ref, attn_ref, cot_ref, piece, *refs):
        w_ref, count_ref, refs = refs[0], refs[1], refs[2:]
        d_hidden_ref, d_mixed_ref, sums_ref = refs[:3]
        d_in = in_ref[...]
        normed, inverse = normal(hidden_ref[...])
        sums_ref[0, 0:1] = jnp.sum(d_in, axis=0, keepdims=True)
        sums_ref[0, 1:2] = jnp.sum(d_in * normed, axis=0, keepdims=True)
        real = (pl.program_id(0) < count_ref[0]).astype(F32)
        grad = cot_ref[...].astype(F32) * real
        d_hidden = grad + normal_back(d_in * (1.0 + piece[0, 4:5, :]), normed, inverse)
        d_hidden_ref[...] = d_hidden
        sums_ref[0, 2:3] = jnp.sum(d_hidden * attn_ref[...], axis=0, keepdims=True)
        d_attn = (piece[0, 2:3, :] * d_hidden).astype(BF)
        d_mixed = None
        for j, out in enumerate(refs[3:]):
            part = d_attn[:, j * columns : (j + 1) * columns]
            out[...] = part
            term = mm(part, w_ref[j], ((1,), (1,)))
            d_mixed = term if d_mixed is None else d_mixed + term
        d_mixed_ref[...] = d_mixed.astype(BF)

    rows = tokens // images
    outs = [(rows, (width,), F32), (rows, (width,), BF), (1, (3, width), F32)]
    outs += [(rows, (columns,), BF)] * blocks
    by_image = [d_mlp_in, hidden_one, attn_out, cotangent, pieces]
    return per_image(kernel, images, by_image, [out_b], outs, 40, "middle_back", count)


def block_head_back(d_packed, d_hidden, inputs, pieces, qkv_b, images):
    tokens, width = d_hidden.shape
    blocks = qkv_b.shape[0]

    def kernel(*refs):
        d_refs, (d_hidden_ref, in_ref, piece) = refs[:blocks], refs[blocks : blocks + 3]
        w_ref, out_ref, sums_ref = refs[blocks + 3 :]
        d_in = None
        for j, d in enumerate(d_refs):
            term = mm(d[...], w_ref[j], ((1,), (1,)))
            d_in = term if d_in is None else d_in + term
        normed, inverse = normal(in_ref[...].astype(F32))
        sums_ref[0, 0:1] = jnp.sum(d_in, axis=0, keepdims=True)
        sums_ref[0, 1:2] = jnp.sum(d_in * normed, axis=0, keepdims=True)
        back = normal_back(d_in * (1.0 + piece[0, 1:2, :]), normed, inverse)
        out_ref[...] = (d_hidden_ref[...] + back).astype(BF)

    outs = [(tokens // images, (width,), BF), (1, (2, width), F32)]
    by_image = [*d_packed, d_hidden, inputs, pieces]
    return per_image(kernel, images, by_image, [qkv_b], outs, 48, "block_head_back")


def grad_stacks(places, a, parts):
    tokens, features = a.shape
    z, count = places.z, places.narrow
    joined = len(parts) < count
    columns = parts[0].shape[1] // (count if joined else 1)
    rows = features // (4 * z)
    chunk = chunk_of(columns, 900)
    masks = [places.masks(0), places.masks(1)]
    total = len(masks[0])

    def kernel(at, a_ref, *refs):
        d_refs, (own_ref, send_ref, turned, product) = refs[:count], refs[count:]

        @pl.when(pl.program_id(0) == 0)
        def _():
            turned[...] = a_ref[...].T

        for i, d_ref in enumerate(d_refs):
            whole = mm(turned[...], d_ref[...], ((1,), (0,)))
            for k in range(4 * z):
                product[i, k] = whole[k * rows : (k + 1) * rows].astype(BF)
        core, y, x = at[0], at[1], at[2]
        for out, owner in ((own_ref, core), (send_ref, 1 - core)):
            for j in range(total):
                dy = jnp.where(owner == 0, masks[0][j][0], masks[1][j][0])
                dx = jnp.where(owner == 0, masks[0][j][1], masks[1][j][1])
                for k in range(z):
                    out[j, k] = product[x ^ dx, (k * 2 + (y ^ dy)) * 2 + owner]

    at = jnp.stack([places.at_c, places.at_y, places.x]).astype(jnp.int32)
    shape = (total, z, rows, columns)
    out = pl.BlockSpec((total, z, rows, chunk), lambda i: (0, 0, 0, i))
    return pl.pallas_call(
        kernel,
        grid=(-(-columns // chunk),),
        out_shape=[jax.ShapeDtypeStruct(shape, BF)] * 2,
        in_specs=[pl.BlockSpec(memory_space=pltpu.SMEM), whole_block(a)]
        + [
            pl.BlockSpec((tokens, chunk), lambda i, j=j: (0, j * (columns // chunk) + i if joined else i))
            for j in range(count)
        ],
        out_specs=[out, out],
        scratch_shapes=[
            pltpu.VMEM((features, tokens), BF),
            pltpu.VMEM((count, 4 * z, rows, chunk), BF),
        ],
        compiler_params=pltpu.CompilerParams(vmem_limit_bytes=60 * 2**20),
        cost_estimate=LONG,
        name="grad_stacks",
    )(at, a, *(parts * count if joined else parts))


class Places:
    def __init__(self):
        self.wide, self.narrow = lax.axis_size("wide"), lax.axis_size("narrow")
        self.z = self.wide // 4
        w = lax.axis_index("wide")
        self.w, self.x = w, lax.axis_index("narrow")
        self.at_z, self.at_y, self.at_c = w // 4, (w // 2) % 2, w % 2
        self.z_bits = [1 << i for i in range(self.z.bit_length() - 1)]
        self.x_bits = [1 << i for i in range(self.narrow.bit_length() - 1)]
        x_masks = [(0, bit) for bit in self.x_bits]
        self.orders = ([(1, 0)] + x_masks, x_masks + [(1, 0)])

    def swap(self, value, flip):
        pairs = []
        for w in range(self.wide):
            for x in range(self.narrow):
                dz, dy, dc, dx = flip(w % 2)
                to = (w // 4 ^ dz) * 4 + (w // 2 % 2 ^ dy) * 2 + (w % 2 ^ dc)
                pairs.append((w * self.narrow + x, to * self.narrow + (x ^ dx)))
        return lax.ppermute(value, ALL, pairs)

    def step_flip(self, i):
        return lambda core: (0, self.orders[core][i][0], 0, self.orders[core][i][1])

    def masks(self, core):
        out = [(0, 0)]
        for dy, dx in self.orders[core]:
            out = out + [(y ^ dy, x ^ dx) for y, x in out]
        return out

    def all_bits(self):
        out = [(0, (bit, 0, 0, 0), self.at_z // bit % 2) for bit in self.z_bits]
        out.append((1, (0, 1, 0, 0), self.at_y))
        out += [(3, (0, 0, 0, bit), self.x // bit % 2) for bit in self.x_bits]
        out.append((2, (0, 0, 1, 0), self.at_c))
        return out

    def open_small(self, value):
        return value[None, None, None, None]

    def gather_bits(self, value, bits):
        for axis, flip, bit in bits:
            other = self.swap(value, lambda core: flip)
            low = jnp.where(bit == 0, value, other)
            high = jnp.where(bit == 0, other, value)
            value = jnp.concatenate([low, high], axis)
        return value

    def add_narrow(self, value):
        for bit in self.x_bits:
            value = value + self.swap(value, lambda core: (0, 0, 0, bit))
        return value

    def scatter_chip_row(self, value):
        value = value.reshape(self.z, 2, 2, *value.shape[1:])
        other = self.swap(take(value, 2, 1 - self.at_c), lambda core: (0, 0, 1, 0))
        value = take(value, 2, self.at_c) + other
        other = self.swap(take(value, 1, 1 - self.at_y), lambda core: (0, 1, 0, 0))
        return take(value, 1, self.at_y) + other

    def scatter_z(self, value):
        for bit in reversed(self.z_bits):
            value = value.reshape(2, bit, *value.shape[1:])
            here = self.at_z // bit % 2
            other = self.swap(take(value, 0, 1 - here), lambda core: (bit, 0, 0, 0))
            value = take(value, 0, here) + other
        return value[0]

    def trade_narrow(self, value):
        if self.narrow != 2:
            return lax.all_to_all(value, "narrow", 0, 0, tiled=True)
        other = self.swap(take(value, 0, 1 - self.x), lambda core: (0, 0, 0, 1))
        own = take(value, 0, self.x)
        return jnp.stack([pick([own, other], self.x), pick([other, own], self.x)])


def pick(parts, index):
    if len(parts) == 1:
        return parts[0]
    if len(parts) == 2:
        return jnp.where(index == 0, parts[0], parts[1])
    return lax.dynamic_index_in_dim(jnp.stack(parts), index, 0, keepdims=False)


def take(value, axis, index):
    return lax.dynamic_index_in_dim(value, index, axis, keepdims=False)


def after(value, *before):
    return lax.optimization_barrier((value,) + before)[0]


def assemble(places, parts):
    half, z, rows, columns = parts[0].shape
    joined = columns % 128 == 0
    masks = [places.masks(0), places.masks(1)]

    def kernel(at, s0, s1, t0, t1, out, held, sem, out_sem):
        core, y, x, here_z = at[0], at[1], at[2], at[3]
        copies = []
        for i, src in enumerate((s0, s1, t0, t1)):
            owner = core ^ (i // 2)
            for j in range(half):
                k = j + half * (i % 2)
                dy = jnp.where(owner == 0, masks[0][k][0], masks[1][k][0])
                dx = jnp.where(owner == 0, masks[0][k][1], masks[1][k][1])
                for d in range(z):
                    if joined:
                        lanes = pl.ds(pl.multiple_of((x ^ dx) * columns, 128), columns)
                        to = held.at[here_z ^ d, y ^ dy, owner, :, lanes]
                    else:
                        to = held.at[x ^ dx, here_z ^ d, y ^ dy, owner]
                    copies.append(pltpu.make_async_copy(src.at[j, d], to, sem.at[len(copies)]))
        for copy in copies:
            copy.start()
        for copy in copies:
            copy.wait()
        whole = pltpu.make_async_copy(held, out, out_sem)
        whole.start()
        whole.wait()

    shape = (places.narrow, z, 2, 2, rows, columns)
    if joined:
        shape = (z, 2, 2, rows, places.narrow * columns)
    at = jnp.stack([places.at_c, places.at_y, places.x, places.at_z]).astype(jnp.int32)
    return pl.pallas_call(
        kernel,
        out_shape=jax.ShapeDtypeStruct(shape, BF),
        in_specs=[pl.BlockSpec(memory_space=pltpu.SMEM)] + [pl.BlockSpec(memory_space=pl.ANY)] * 4,
        out_specs=pl.BlockSpec(memory_space=pl.ANY),
        scratch_shapes=[
            pltpu.VMEM(shape, BF),
            pltpu.SemaphoreType.DMA((4 * half * z,)),
            pltpu.SemaphoreType.DMA,
        ],
        compiler_params=pltpu.CompilerParams(vmem_limit_bytes=60 * 2**20),
        cost_estimate=LONG,
        name="assemble",
    )(at, *parts)


def turn(places, a):
    tokens, features = a.shape
    slabs = 4 * places.z
    rows = features // slabs

    def kernel(at, a_ref, mine_ref, other_ref, turned):
        whole = a_ref[...].astype(F32).T
        for k in range(slabs):
            turned[k] = whole[k * rows : (k + 1) * rows].astype(BF)
        for k in range(slabs // 2):
            mine_ref[k] = turned[2 * k + at[0]]
            other_ref[k] = turned[2 * k + 1 - at[0]]

    out = jax.ShapeDtypeStruct((slabs // 2, rows, tokens), BF)
    return pl.pallas_call(
        kernel,
        grid=(1,),
        out_shape=[out, out],
        in_specs=[pl.BlockSpec(memory_space=pltpu.SMEM), whole_block(a)],
        out_specs=[whole_block(out)] * 2,
        scratch_shapes=[pltpu.VMEM((slabs, rows, tokens), BF)],
        compiler_params=pltpu.CompilerParams(vmem_limit_bytes=60 * 2**20),
        cost_estimate=LONG,
        name="turn",
    )(places.at_c.astype(jnp.int32).reshape(1), a)


def chip_stacks(places, turned, parts):
    slabs, rows, tokens = turned[0].shape
    z, count = places.z, places.narrow
    joined = len(parts[0]) < count
    columns = parts[0][0].shape[1] // (count if joined else 1)
    chunk = chunk_of(columns, 900)
    masks = [places.masks(0), places.masks(1)]
    half = len(masks[0]) // 2

    def kernel(at, own_ref, got_ref, *refs):
        d_refs, (keep_ref, send_ref, product) = refs[: 2 * count], refs[2 * count :]
        for i in range(count):
            whole = mm(own_ref[...], d_refs[i][...], ((1,), (0,)))
            whole += mm(got_ref[...], d_refs[count + i][...], ((1,), (0,)))
            for k in range(slabs):
                product[i, k] = whole[k * rows : (k + 1) * rows].astype(BF)
        core, y, x = at[0], at[1], at[2]
        for j in range(2 * half):
            dy = jnp.where(core == 0, masks[0][j][0], masks[1][j][0])
            dx = jnp.where(core == 0, masks[0][j][1], masks[1][j][1])
            out = keep_ref if j < half else send_ref
            for k in range(z):
                out[j % half, k] = product[x ^ dx, k * 2 + (y ^ dy)]

    at = jnp.stack([places.at_c, places.at_y, places.x]).astype(jnp.int32)
    flat = [a.reshape(slabs * rows, tokens) for a in turned]
    out = pl.BlockSpec((half, z, rows, chunk), lambda i: (0, 0, 0, i))
    specs = [
        pl.BlockSpec((tokens, chunk), lambda i, j=j: (0, j * (columns // chunk) + i if joined else i))
        for j in range(count)
    ]
    args = [p for part in parts for p in (list(part) * count if joined else part)]
    return pl.pallas_call(
        kernel,
        grid=(-(-columns // chunk),),
        out_shape=[jax.ShapeDtypeStruct((half, z, rows, columns), BF)] * 2,
        in_specs=[pl.BlockSpec(memory_space=pltpu.SMEM)] + [whole_block(a) for a in flat] + specs * 2,
        out_specs=[out, out],
        scratch_shapes=[pltpu.VMEM((count, slabs, rows, chunk), BF)],
        compiler_params=pltpu.CompilerParams(vmem_limit_bytes=60 * 2**20),
        cost_estimate=LONG,
        name="chip_stacks",
    )(at, *flat, *args)


def join(parts):
    counts = [p.shape[0] for p in parts]

    def kernel(*refs):
        first = 0
        for ref, count in zip(refs[:-1], counts):
            refs[-1][first : first + count] = ref[...]
            first += count

    shape = jax.ShapeDtypeStruct((sum(counts), *parts[0].shape[1:]), BF)
    return pl.pallas_call(
        kernel,
        grid=(1,),
        out_shape=shape,
        in_specs=[whole_block(p) for p in parts],
        out_specs=whole_block(shape),
        compiler_params=pltpu.CompilerParams(vmem_limit_bytes=60 * 2**20),
        cost_estimate=SHORT,
        name="join",
    )(*parts)


def add_stacks(terms, half):
    shape = (half, *terms[0].shape[1:])

    def kernel(*refs):
        total = refs[0][...].astype(F32)
        for ref in refs[1:-1]:
            total += ref[...].astype(F32)
        refs[-1][...] = total.astype(BF)

    deep = 2 if shape[1] % 2 == 0 else 1
    block = (1, deep, *shape[2:])
    return pl.pallas_call(
        kernel,
        grid=(half, shape[1] // deep),
        out_shape=jax.ShapeDtypeStruct(shape, BF),
        in_specs=[pl.BlockSpec(block, lambda i, j: (half + i, j, 0, 0))] * len(terms),
        out_specs=pl.BlockSpec(block, lambda i, j: (i, j, 0, 0)),
        compiler_params=pltpu.CompilerParams(vmem_limit_bytes=60 * 2**20),
        cost_estimate=SHORT,
        name="add_stacks",
    )(*terms)


def add_slabs(places, terms, z_terms, first, count, divisor=None):
    rows, columns = terms[0].shape[2:]
    late = [(at, term) for at, term in z_terms if at <= first < at + term.shape[0]]

    def kernel(at_ref, *refs):
        out, refs = refs[-1], refs[:-1]
        total = None
        for i, ref in enumerate(refs[: len(terms) + len(late)]):
            value = (ref[0, 0] if i < len(terms) else ref[0]).astype(F32)
            total = value if total is None else total + value
        if divisor is not None:
            total = total / refs[-1][0]
        out[0] = total.astype(out.dtype)

    in_specs = [
        pl.BlockSpec((1, 1, rows, columns), lambda i, at: (0, at[0] ^ (first + i), 0, 0))
        for _ in terms
    ]
    in_specs += [
        pl.BlockSpec((1, rows, columns), lambda i, at, f=first - at_first: (f + i, 0, 0))
        for at_first, _ in late
    ]
    args = [*terms, *[term for _, term in late]]
    if divisor is not None:
        in_specs.append(pl.BlockSpec(memory_space=pltpu.SMEM))
        args.append(divisor.reshape(1))
    kind = BF if divisor is None else F32
    return pl.pallas_call(
        kernel,
        grid_spec=pltpu.PrefetchScalarGridSpec(
            num_scalar_prefetch=1,
            grid=(count,),
            in_specs=in_specs,
            out_specs=pl.BlockSpec((1, rows, columns), lambda i, at: (i, 0, 0)),
        ),
        out_shape=jax.ShapeDtypeStruct((count, rows, columns), kind),
        compiler_params=pltpu.CompilerParams(vmem_limit_bytes=60 * 2**20),
        cost_estimate=SHORT,
        name="add_slabs",
    )(places.at_z.astype(jnp.int32).reshape(1), *args)


class Slots:
    def __init__(self, places):
        self.places = places
        self.before, self.now, self.ready = (), [], []

    def tie(self, value):
        return after(value, *self.before, *self.ready)

    def note(self, *values):
        self.now += values

    def next(self, *values):
        self.note(*values)
        self.before, self.now, self.ready = tuple(self.now), [], []

    def send(self, value, flip):
        value = after(value, *self.before)
        self.ready.append(value)
        return self.follow(value, flip)

    def follow(self, value, flip):
        other = self.places.swap(value, flip)
        self.note(other)
        return other


class Gather:
    def __init__(self, slots, shard):
        self.slots, self.places = slots, slots.places
        self.rows = self.places.wide * shard.shape[0]
        self.parts = [shard[None]]

    def all_z(self):
        for d in range(1, self.places.z):
            self.parts.append(self.slots.send(self.parts[0], lambda core: (d, 0, 0, 0)))

    def step(self, i, exchange):
        joined = join([p.reshape(-1, *p.shape[-2:]) for p in self.parts])
        self.parts = [joined]
        self.parts.append(exchange(joined, self.places.step_flip(i)))

    def first(self):
        for i in range(len(self.places.orders[0]) - 1):
            self.step(i, self.slots.follow if i else self.slots.send)

    def last(self):
        self.step(len(self.places.orders[0]) - 1, self.slots.send)

    def cores(self):
        parts = [p.reshape(-1, self.places.z, *p.shape[-2:]) for p in self.parts]
        self.parts = parts + [self.slots.send(p, lambda core: (0, 0, 1, 0)) for p in parts]

    def whole(self):
        whole = assemble(self.places, self.slots.tie(tuple(self.parts)))
        return whole.reshape(-1, self.rows, whole.shape[-1])


class Scatter:
    def __init__(self, slots, a, parts):
        self.slots, self.places = slots, slots.places
        stack, self.to_core = grad_stacks(self.places, a, parts)
        self.terms, self.z_terms, self.half = [stack], [], stack.shape[0]

    def cores(self, exchange):
        self.terms.append(exchange(self.to_core, lambda core: (0, 0, 1, 0)))

    def hold(self):
        self.terms[0] = self.slots.tie(self.terms[0])

    def step(self, i, exchange):
        self.half //= 2
        send = add_stacks(self.terms, self.half)
        self.terms.append(exchange(send, self.places.step_flip(i)))

    def first(self):
        self.step(len(self.places.orders[0]) - 1, self.slots.send)

    def last(self):
        for i in reversed(range(len(self.places.orders[0]) - 1)):
            chained = i < len(self.places.orders[0]) - 2
            self.step(i, self.slots.follow if chained else self.slots.send)

    def step_z(self, *bits):
        for i, bit in enumerate(bits):
            exchange = self.slots.follow if i else self.slots.send
            send = add_slabs(self.places, self.terms, self.z_terms, bit, bit)
            self.z_terms.append((0, exchange(send, lambda core: (bit, 0, 0, 0))))

    def direct_z(self):
        for d in reversed(range(1, self.places.z)):
            send = add_slabs(self.places, self.terms, self.z_terms, d, 1)
            self.z_terms.append((0, self.slots.send(send, lambda core: (d, 0, 0, 0))))

    def result(self, divisor):
        divisor = self.slots.tie(divisor)
        return add_slabs(self.places, self.terms, self.z_terms, 0, 1, divisor)[0]


class ChipScatter(Scatter):
    def __init__(self, slots, turned, parts):
        self.slots, self.places = slots, slots.places
        keep, self.ready = chip_stacks(self.places, turned, parts)
        self.terms, self.z_terms, self.half = [keep], [], keep.shape[0]

    def first(self):
        flip = self.places.step_flip(len(self.places.orders[0]) - 1)
        self.terms.append(self.slots.send(self.ready, flip))


def to_core(core):
    return (0, 0, 1, 0)


def dot(a, b, dims, out=F32):
    return lax.dot_general(a, b, (dims, ((), ())), preferred_element_type=F32).astype(out)


def split(a, count):
    width = a.shape[1] // count
    return [a[:, n * width : (n + 1) * width] for n in range(count)]


def on_device(
    inputs,
    cotangent,
    class_ids,
    step_ids,
    image_counts,
    w_qkv,
    w_out,
    w_gate,
    w_up,
    w_down,
    ada_weight,
    ada_bias,
    class_table,
    norm_gains,
):
    places = Places()
    wide, narrow, at_w, at_n = places.wide, places.narrow, places.w, places.x
    images, length, width = inputs.shape
    tables, sums = head_tables(length), head_sums()
    gains = jnp.tile(norm_gains, (1, H))
    local_count = image_counts[0]

    tokens = images * length

    def flat(v):
        return v.reshape(tokens, -1)

    def deep(v):
        return v.reshape(images, length, -1)

    t = Slots(places)
    z_low, z_high = places.z_bits[:1], places.z_bits[1:]
    z_down = z_high[::-1]
    qkv, out, gate, up, down = [
        Gather(t, shard) for shard in (w_qkv, w_out, w_gate, w_up, w_down)
    ]

    qkv.all_z()
    small = [class_ids, step_ids, image_counts, ada_bias]
    small = jnp.concatenate([v.astype(F32) for v in small])[None]
    bits = places.all_bits()
    small = places.gather_bits(places.open_small(small), bits)
    small = small.reshape(wide * narrow, -1)
    t.next(small)

    qkv.first()
    out.all_z()
    small = t.tie(small)
    ids = small[:, : 2 * images].reshape(-1, 2, images).transpose(0, 2, 1).reshape(-1, 2)
    ids = ids.astype(jnp.int32)
    real_count = jnp.sum(small[:, 2 * images])
    bias = small[:, 2 * images + 1 :].reshape(-1)
    rows_here, cols_here = class_table.shape
    class_hot = ids[:, :1] - at_n * rows_here == jnp.arange(rows_here, dtype=jnp.int32)[None, :]
    picked = dot(class_hot.astype(BF), class_table, ((1,), (0,)))
    column = at_w * cols_here + jnp.arange(cols_here, dtype=jnp.int32)
    half_width = width // 2
    frequency = jnp.exp(-math.log(10000.0) * (column % half_width).astype(F32) / half_width)
    angles = ids[:, 1:].astype(F32) * frequency[None, :]
    wave = jnp.where(column[None, :] < half_width, jnp.cos(angles), jnp.sin(angles))
    condition = places.add_narrow(picked) + wave
    cond_act = jax.nn.silu(condition).astype(BF)
    t.next(cond_act)

    qkv.last()
    gate.all_z()
    mod_part = dot(t.tie(cond_act), ada_weight, ((1,), (0,)))
    mod_part = places.scatter_chip_row(mod_part.reshape(wide, narrow, images, -1))
    t.next(mod_part, *tables, sums)

    qkv.cores()
    out.first()
    gate.first()
    mod_part = places.trade_narrow(places.scatter_z(t.tie(mod_part)))
    t.next(mod_part)

    out.last()
    gate.last()
    up.all_z()
    qkv_b = qkv.whole()
    modulation = t.tie(mod_part).transpose(1, 0, 2).reshape(images, -1) + bias
    pieces = modulation.reshape(images, 6, width)
    normed, _ = layer_norm(inputs.astype(F32))
    attn_in = flat((normed * (1.0 + pieces[:, 1:2]) + pieces[:, 0:1]).astype(BF))
    t.next(attn_in, qkv_b)

    out.cores()
    gate.cores()
    up.first()
    packed = project(t.tie(attn_in), qkv_b)
    attn_turned, attn_other = turn(places, t.tie(attn_in))
    t.next(*packed, attn_other)

    attn_turned = [attn_turned, t.send(attn_other, to_core)]
    up.last()
    down.all_z()
    packed = t.tie(packed)
    queries, key_rows, value_rows, mixed = attention_forward(packed, gains, tables, sums, images)
    slot_real = (jnp.arange(images, dtype=jnp.int32) < local_count).astype(F32)
    grad_y = cotangent.astype(F32) * slot_real[:, None, None]
    d_mlp = split(flat((pieces[:, 5:6] * grad_y).astype(BF)), narrow)
    t.next(mixed, *d_mlp)

    up.cores()
    down.first()
    out_b = out.whole()
    attn_out, hidden_one, mlp_in = attention_tail(mixed, out_b, flat(inputs), pieces, images)
    gate_b = gate.whole()[0]
    mlp_turned, mlp_other = turn(places, mlp_in)
    t.next(mlp_in, gate_b, mlp_other)

    mlp_turned = [mlp_turned, t.send(mlp_other, to_core)]
    down.last()
    up_b = up.whole()[0]
    gate_val, up_val, hidden_mid = gated(mlp_in, gate_b, up_b)
    t.next(hidden_mid)

    down.cores()
    g_down = Scatter(t, t.tie(hidden_mid), d_mlp)
    t.next(g_down.to_core)

    g_down.cores(t.send)
    down_b = down.whole()
    t.next(down_b)

    g_down.first()
    d_gate, d_up, d_mlp_in = gated_back(t.tie(d_mlp), down_b, gate_val, up_val, gate_b, up_b)
    t.next(d_mlp_in)

    g_down.last()
    d_gate_got = t.send(d_gate, to_core)
    d_up_got = t.send(d_up, to_core)
    d_hidden, d_mixed, sums_b, *d_attn = middle_back(
        t.tie(d_mlp_in), hidden_one, attn_out, flat(cotangent), pieces, out_b, image_counts, images
    )
    g_gate = ChipScatter(t, mlp_turned, [[after(d_gate, d_mixed)], [d_gate_got]])
    t.next(g_gate.ready)

    g_gate.first()
    g_down.hold()
    g_down.step_z(*z_down)
    g_up = ChipScatter(t, mlp_turned, [[t.tie(d_up)], [d_up_got]])
    g_out = Scatter(t, mixed, t.tie(d_attn))
    block_output, sums_gate = block_tail(
        t.tie(hidden_mid), down_b, hidden_one, flat(cotangent), pieces, image_counts, images
    )
    t.next(g_up.ready, g_out.to_core, sums_gate)

    g_up.first()
    g_gate.last()
    g_out.cores(t.send)
    g_down.step_z(*z_low)
    d_packed, gain_terms = attention_backward(
        packed, queries, key_rows, value_rows, t.tie(d_mixed), gains, tables, sums, images
    )
    t.next(*d_packed)

    d_packed_got = [
        t.send(d.reshape(-1, 8, d.shape[1]), to_core).reshape(d.shape) for d in d_packed
    ]
    for grad in (g_up, g_out, g_gate):
        grad.hold()
    g_up.last()
    g_out.first()
    g_gate.step_z(*z_down)
    g_qkv = ChipScatter(t, attn_turned, [t.tie(d_packed), d_packed_got])
    t.next(g_qkv.ready)

    g_qkv.first()
    for grad in (g_out, g_up, g_gate):
        grad.hold()
    g_out.last()
    g_up.step_z(*z_down)
    g_gate.step_z(*z_low)
    d_tokens, sums_a = block_head_back(
        t.tie(d_packed), d_hidden, flat(inputs), pieces, qkv_b, images
    )
    grad_gains = gain_terms.sum(0).reshape(2, H, HD).sum(1).reshape(1, -1)
    gains_high = grad_gains.astype(BF)
    gains_low = (grad_gains - gains_high.astype(F32)).astype(BF)
    rest = jnp.zeros((images - 2, 2 * HD), BF)
    grad_gains = jnp.concatenate([gains_high, gains_low, rest], axis=0)
    d_modulation = jnp.concatenate([sums_a, sums_b[:, 2:], sums_b[:, :2], sums_gate], axis=1)
    d_modulation = d_modulation.astype(BF).reshape(images, -1)
    d_modulation = jnp.concatenate([d_modulation, grad_gains], axis=1)
    t.next(d_modulation)

    g_qkv.last()
    for grad in (g_up, g_out):
        grad.hold()
    g_up.step_z(*z_low)
    g_out.step_z(*z_down)
    d_all = places.open_small(t.tie(d_modulation))
    d_all = places.gather_bits(d_all, bits[: len(places.z_bits)])
    t.next(d_all)

    g_qkv.direct_z()
    g_out.step_z(*z_low)
    d_all = places.gather_bits(after(d_all, *t.before), bits[len(places.z_bits) :])
    d_all = d_all.reshape(wide * narrow * images, -1)
    gain_sum = d_all[:, 6 * width : 6 * width + 2 * HD].astype(F32)
    gain_sum = jnp.sum(gain_sum, axis=0).reshape(2, HD) / real_count
    d_mod = d_all[:, : 6 * width]
    ada_cols = ada_weight.shape[1]
    d_mod_here = lax.dynamic_slice_in_dim(d_mod, at_n * ada_cols, ada_cols, 1)
    g_ada = dot(cond_act, d_mod_here, ((0,), (0,))) / real_count
    bias_cols = ada_bias.shape[0]
    bias_at = (at_w * narrow + at_n) * bias_cols
    g_bias = jnp.sum(lax.dynamic_slice_in_dim(d_mod, bias_at, bias_cols, 1).astype(F32), axis=0)
    g_bias = g_bias / real_count
    d_cond_act = places.add_narrow(dot(d_mod_here, ada_weight, ((1,), (1,))))
    cond_sigmoid = jax.nn.sigmoid(condition)
    d_condition = d_cond_act * cond_sigmoid * (1.0 + condition * (1.0 - cond_sigmoid))
    g_table = jnp.dot(class_hot.astype(F32).T, d_condition, precision=HIGHEST) / real_count
    r_out, r_gate, r_up, r_down = [g.result(real_count) for g in (g_out, g_gate, g_up, g_down)]
    at, late = g_qkv.z_terms[-1]
    g_qkv.z_terms[-1] = (at, after(late, g_ada, g_table, r_out, r_gate, r_up, r_down))
    r_qkv = g_qkv.result(real_count)

    return (
        deep(block_output),
        deep(d_tokens),
        r_qkv,
        r_out,
        r_gate,
        r_up,
        r_down,
        g_ada,
        g_bias,
        g_table,
        gain_sum,
    )


def solution(mesh):
    split = P("wide", "narrow")
    images = P(ALL, None, None)
    return jax.shard_map(
        on_device,
        mesh=mesh,
        in_specs=(
            images,
            images,
            P(ALL),
            P(ALL),
            P(ALL),
            split,
            split,
            split,
            split,
            split,
            split,
            P(ALL),
            P("narrow", "wide"),
            P(),
        ),
        out_specs=(
            images,
            images,
            split,
            split,
            split,
            split,
            split,
            split,
            P(ALL),
            P("narrow", "wide"),
            P(),
        ),
        check_vma=False,
    )
```
